32 devices in a mesh: dp: 8 (over z, x), seq: 4 (over y, core).
Axes of the slice: x: 2, y: 2, z: 4, core: 2. Of those that a mesh axis runs over, the one named last changes fastest.
Arguments:
- byte_ids: int32 [16, 2048], P('dp', 'seq'), may hold values from 0 to 258
- lengths: int32 [16], replicated, may hold values from 1 to 2048, 20480 in all
- deal_order: int32 [16], P('dp'), may hold values from 0 to 15, each once
- buckets: int32 [2047], replicated, may hold values from 0 to 31, as said below
- embedding: bfloat16 [259, 768], P(None, 'dp'), may hold values from -6 to 6
- conv_w: bfloat16 [4, 768], P(None, 'dp'), may hold values from -3 to 3
- score_w: bfloat16 [768], P('dp'), may hold values from -0.625 to 0.625
- gain_one: bfloat16 [768], P('dp'), may hold values from 0.5 to 1.5
- w_query: bfloat16 [768, 768], P('dp'), may hold values from -0.109375 to 0.109375
- w_key: bfloat16 [768, 768], P('dp'), may hold values from -0.109375 to 0.109375
- w_value: bfloat16 [768, 768], P('dp'), may hold values from -0.21875 to 0.21875
- w_out: bfloat16 [768, 768], P('dp'), may hold values from -1.25 to 1.25
- rel_bias: bfloat16 [32, 12], replicated, may hold values from -6 to 6
- gain_two: bfloat16 [768], P('dp'), may hold values from 0.5 to 1.5
- w_gate: bfloat16 [768, 2048], P('dp'), may hold values from -0.21875 to 0.21875
- w_up: bfloat16 [768, 2048], P('dp'), may hold values from -0.21875 to 0.21875
- w_down: bfloat16 [2048, 768], P('dp'), may hold values from -0.125 to 0.125
- cotangent: bfloat16 [16, 1024, 768], P('dp', 'seq'), may hold values from -6 to 6
Outputs:
- output: bfloat16 [16, 1024, 768], P('dp', 'seq')
- d_input: bfloat16 [16, 2048, 768], P('dp', 'seq')
- grad_embedding: float32 [259, 768], P(None, 'dp')
- grad_conv: float32 [4, 768], P(None, 'dp')
- grad_score: float32 [768], P('dp')
- grad_gain_one: float32 [768], P('dp')
- grad_query: float32 [768, 768], P('dp')
- grad_key: float32 [768, 768], P('dp')
- grad_value: float32 [768, 768], P('dp')
- grad_out: float32 [768, 768], P('dp')
- grad_rel_bias: float32 [32, 12], replicated
- grad_gain_two: float32 [768], P('dp')
- grad_gate: float32 [768, 2048], P('dp')
- grad_up: float32 [768, 2048], P('dp')
- grad_down: float32 [2048, 768], P('dp')
The draws below stay inside these ranges and needn't reach their ends.
Inputs may be any that keep to these rules, and one draw needn't show every extreme that they name: Row r holds sequence deal_order[r]; its positions from lengths[deal_order[r]] on are padding; some sequence fills all 2048 positions. `deal_order`: each sequence number appears once. Bidirectional buckets of the offset j - i in the manner of T5: offsets j - i > 0 take the upper 32 / 2 buckets; magnitudes under 32 / 4 each have their own bucket, larger ones fall into ranges spaced by the logarithm up to 128, the edges of each half drawn apart, each edge at T5's or up to a quarter above it, and all magnitudes of 128 or more share the last bucket of their half.
All inputs are finite; a program needn't handle non-finite values.
Results may differ from the reference program's by a relative error of at most 0.019.
Values may be sent and summed in bfloat16 or wider, within the bound.
No kernel may reach another device: no remote copies, remote signals or barrier semaphores. Data moves between devices by JAX's collectives and lax.ppermute only.
A program may use at most 320 MiB of HBM per device.

```python
import math
import jax
import jax.numpy as jnp
import numpy as np
from jax import lax

D = 768
H = 12
DH = 64
FF = 2048
VOCAB = 259
NB = 32
S = 2048
T_SIZE = 1024
NSEQ = 16
REL = 2047


def draw_buckets(key, part):
    half = NB // 2
    exact = half // 2
    inner = half - exact - 1
    base_edges = np.array([int(exact * (128.0 / exact) ** (step / (half - exact))) for step in range(1, half - exact)], dtype=np.int32)
    base_vec = jnp.asarray(base_edges, dtype=jnp.int32)
    reach = base_vec // 4 + 1
    lower_key = jax.random.fold_in(key, 11)
    upper_key = jax.random.fold_in(key, 23)
    edges_lower = base_vec + jax.random.randint(lower_key, (inner,), 0, reach, dtype=jnp.int32)
    edges_upper = base_vec + jax.random.randint(upper_key, (inner,), 0, reach, dtype=jnp.int32)
    centre = (REL - 1) // 2
    forward = jnp.arange(REL, dtype=jnp.int32) - centre
    upper = (forward > 0).astype(jnp.int32)
    magnitude = jnp.abs(forward)
    edges = jnp.where(upper[:, None] > 0, edges_upper[None, :], edges_lower[None, :])
    spaced = exact + jnp.sum((magnitude[:, None] >= edges).astype(jnp.int32), axis=1)
    bucket = jnp.where(magnitude < exact, magnitude, spaced)
    return (bucket + upper * half).astype(jnp.int32)


def with_ends(entries, stream_key, low, high):
    longest = entries.shape.index(max(entries.shape))
    spots = []
    for shift in (0, 1):
        where = [jax.random.randint(jax.random.fold_in(stream_key, axis), (), 0, length) for axis, length in enumerate(entries.shape)]
        where[longest] = (where[longest] + shift) % entries.shape[longest]
        spots.append(tuple(where))
    return entries.at[spots[0]].set(low).at[spots[1]].set(high)


def steps_of(key, shape, shards, least, top_value):
    factor_of, own = 1.0, jax.random.fold_in(key, 6)
    for axis_at, shards_of in shards:
        draws = jnp.exp(jax.random.uniform(jax.random.fold_in(own, axis_at), (shards_of,), jnp.float32, least / len(shards), top_value / len(shards)))
        factor_of = factor_of * jnp.repeat(draws, shape[axis_at] // shards_of).reshape([-1 if axis == axis_at else 1 for axis in range(len(shape))])
    return factor_of


def length_profile(count, total, most, lean):
    weights = [(1 << 20) // math.isqrt(grade ** lean) + 1 for grade in range(2, count + 1)]
    spare, counts = total - most - (count - 1), [1] * (count - 1)
    while spare > 0:
        movable = [i for i in range(count - 1) if counts[i] < most]
        whole, left = sum([weights[i] for i in movable]), spare
        for i in movable:
            more = min(most - counts[i], max(1, left * weights[i] // whole), spare)
            counts[i] = counts[i] + more
            spare = spare - more
    return np.array([most] + counts)


def uneven_parts(stream_key, amount, total, most, slope):
    if amount == 2:
        one = jax.random.randint(stream_key, (), max(1, total - most), min(most, total - 1) + 1)
        return jnp.stack([one, total - one])
    sizes = jnp.asarray(length_profile(amount, total, most, slope), jnp.int32)
    pairs = (amount - 1) // 2
    source_of, taker = sizes[1:1 + 2 * pairs:2], sizes[2:2 + 2 * pairs:2]
    slack = jnp.minimum(source_of - 1, most - taker)
    shifted = jax.random.randint(jax.random.fold_in(stream_key, 1), (pairs,), 0, 1 << 20) % (slack + 1)
    sizes = sizes.at[1:1 + 2 * pairs:2].set(source_of - shifted).at[2:2 + 2 * pairs:2].set(taker + shifted)
    return sizes[jax.random.permutation(jax.random.fold_in(stream_key, 2), amount)]


def bell_draw(key, shape, scale, limit, split=(), kind=jnp.bfloat16):
    loudness = steps_of(key, shape, split, -0.22, 0.18) if split else 1.0
    result = jax.random.normal(key, shape, jnp.float32) * scale * loudness
    return jnp.minimum(jnp.maximum(result, -limit), limit).astype(kind)


def setup_inputs(seed: int = 0) -> dict:
    seeds = jax.random.split(jax.random.key(seed), 19)
    return {
        "byte_ids": with_ends(jax.random.randint(seeds[0], (NSEQ, S), 0, VOCAB), jax.random.fold_in(seeds[0], 1), 0, VOCAB - 1).astype(jnp.int32),
        "lengths": uneven_parts(seeds[1], NSEQ, NSEQ * S * 5 // 8, S, 2).astype(jnp.int32),
        "deal_order": jax.random.permutation(seeds[2], NSEQ).astype(jnp.int32),
        "buckets": draw_buckets(jax.random.fold_in(seeds[18], 71), 0),
        "embedding": bell_draw(seeds[4], (VOCAB, D), 1.0, 6.0, ((1, 8),)),
        "conv_w": bell_draw(seeds[5], (4, D), 0.5, 3.0, ((1, 8),)),
        "score_w": bell_draw(seeds[6], (D,), 0.1, 0.625, ((0, 8),)),
        "gain_one": jnp.clip(1.0 + 0.1 * jax.random.normal(seeds[7], (D,), jnp.float32), 0.5, 1.5).astype(jnp.bfloat16),
        "w_query": bell_draw(seeds[8], (D, D), 0.018, 0.109375, ((0, 8),)),
        "w_key": bell_draw(seeds[9], (D, D), 0.018, 0.109375, ((0, 8),)),
        "w_value": bell_draw(seeds[10], (D, D), D ** -0.5, 0.21875, ((0, 8),)),
        "w_out": bell_draw(seeds[11], (D, D), (D // 32) ** -0.5, 1.25, ((0, 8),)),
        "rel_bias": bell_draw(seeds[12], (NB, H), 1.0, 6.0),
        "gain_two": jnp.clip(1.0 + 0.1 * jax.random.normal(seeds[13], (D,), jnp.float32), 0.5, 1.5).astype(jnp.bfloat16),
        "w_gate": bell_draw(seeds[14], (D, FF), D ** -0.5, 0.21875, ((0, 8),)),
        "w_up": bell_draw(seeds[15], (D, FF), D ** -0.5, 0.21875, ((0, 8),)),
        "w_down": bell_draw(seeds[16], (FF, D), FF ** -0.5, 0.125, ((0, 8),)),
        "cotangent": bell_draw(seeds[17], (NSEQ, T_SIZE, D), 1.0, 6.0, ((0, 8), (1, 4))),
    }


EPS = 1e-06
NEG = -1000000000.0
HIGH = lax.Precision.HIGHEST

@jax.custom_vjp
def low(v):
    return lax.optimization_barrier(v.astype(jnp.bfloat16)).astype(jnp.float32)

@jax.custom_vjp
def low_back(v):
    return v

def low_keep(v):
    return (low(v), None)

def low_pass(kept, grad):
    return (grad,)

def back_keep(v):
    return (v, None)

def back_low(kept, grad):
    return (low(grad),)
low.defvjp(low_keep, low_pass)
low_back.defvjp(back_keep, back_low)

def rms_norm(hidden, gain_vec):
    factor = lax.rsqrt(lax.optimization_barrier(jnp.mean(hidden * hidden, axis=-1, keepdims=True)) + EPS)
    return hidden * factor * gain_vec

def block_means(padded, offset, extent):
    places = offset + jnp.arange(extent, dtype=jnp.int32)
    results = []
    for block_len in range(1, 5):
        remain = places % block_len
        summed = 0.0
        for shift_at in range(1 - block_len, block_len):
            select = ((shift_at >= -remain) & (shift_at <= block_len - 1 - remain)).astype(jnp.float32)
            summed = summed + select[:, None] * padded[..., 3 + shift_at:3 + shift_at + extent, :]
        results.append(summed / block_len)
    return results

def mix_blocks(padded, offset, extent, score_vec):
    averages = block_means(padded, offset, extent)
    scores = jnp.stack([lax.optimization_barrier(jnp.sum(mean_b * score_vec, axis=-1)) for mean_b in averages], axis=0)
    shares = jax.nn.softmax(scores, axis=0)
    pooled = sum((shares[which_b][..., None] * averages[which_b] for which_b in range(4)))
    dims_all = pooled.shape
    return lax.optimization_barrier(jnp.mean(pooled.reshape(dims_all[:-2] + (dims_all[-2] // 2, 2, dims_all[-1])), axis=-2))

def row_forward(emb_in, params, length, buckets):
    conv_vec, score_vec, gain_first, query_w, key_w, value_w, out_w, rel_f, gain_second, gate_w, up_w, down_w = params
    emb_in = low_back(emb_in)
    extent = emb_in.shape[0]
    places = jnp.arange(extent, dtype=jnp.int32)
    live = (places < length).astype(jnp.float32)[:, None]
    masked = emb_in * live
    padded_in = jnp.pad(masked, ((2, 1), (0, 0)))
    conv_out = sum((conv_vec[tap_at] * padded_in[tap_at:tap_at + extent] for tap_at in range(4))) * live
    padded = jnp.pad(conv_out, ((3, 3), (0, 0)))
    h_zero = mix_blocks(padded, 0, extent, score_vec)
    tokens = h_zero.shape[0]
    normed = low(rms_norm(h_zero, gain_first))
    query = low_back(low(jnp.dot(normed, query_w, precision=HIGH)))
    key_all = low_back(low(jnp.dot(normed, key_w, precision=HIGH)))
    value_all = low_back(low(jnp.dot(normed, value_w, precision=HIGH)))
    heads = query_w.shape[1] // DH
    query_4 = query.reshape(tokens, heads, DH)
    key_4 = key_all.reshape(tokens, heads, DH)
    value_4 = value_all.reshape(tokens, heads, DH)
    bias_rel = rel_f[buckets].T
    key_ok = 2 * jnp.arange(tokens, dtype=jnp.int32) < length
    blk_rows = min(512, tokens)

    def one_block(first_row):
        query_blk = lax.dynamic_slice_in_dim(query_4, first_row, blk_rows, 0)
        raw = jnp.einsum('qhd,khd->hqk', query_blk, key_4, precision=HIGH)
        rows_at = first_row + jnp.arange(blk_rows, dtype=jnp.int32)
        rel_index = jnp.arange(tokens, dtype=jnp.int32)[None, :] - rows_at[:, None] + tokens - 1
        raw = low_back(raw + jnp.take(bias_rel, rel_index, axis=1))
        raw = jnp.where(key_ok[None, None, :], raw, NEG)
        prob_low = low(jax.nn.softmax(raw, axis=-1))
        return jnp.einsum('hqk,khd->qhd', prob_low, value_4, precision=HIGH)
    starts = jnp.arange(tokens // blk_rows, dtype=jnp.int32) * blk_rows
    attended = lax.map(jax.checkpoint(one_block), starts).reshape(tokens, heads * DH)
    attended = low_back(low(attended))
    branch = low_back(jnp.dot(attended, out_w, precision=HIGH))
    h_one = h_zero + branch
    normed_two = low(rms_norm(h_one, gain_second))
    gate_val = low_back(jnp.dot(normed_two, gate_w, precision=HIGH))
    up_val = low_back(jnp.dot(normed_two, up_w, precision=HIGH))
    hidden = low(jax.nn.gelu(gate_val, approximate=True) * up_val)
    ff_out = low_back(jnp.dot(hidden, down_w, precision=HIGH))
    return h_one + ff_out

def reference(byte_ids, lengths, deal_order, buckets, embedding, conv_w, score_w, gain_one, w_query, w_key, w_value, w_out, rel_bias, gain_two, w_gate, w_up, w_down, cotangent):
    params = tuple((weight_in.astype(jnp.float32) for weight_in in (conv_w, score_w, gain_one, w_query, w_key, w_value, w_out, rel_bias, gain_two, w_gate, w_up, w_down)))
    embed_f = embedding.astype(jnp.float32)
    row_lengths = lengths[deal_order]

    def one_row(running, scan_item):
        ids_row, length, cot_row = scan_item
        embedded, take_back = jax.vjp(lambda emb_table: emb_table[ids_row], embed_f)
        out_row, pull = jax.vjp(lambda emb_in, param_in: row_forward(emb_in, param_in, length, buckets), embedded, params)
        d_emb, d_params = pull(cot_row.astype(jnp.float32))
        d_table, = take_back(d_emb)
        sums_new = (running[0] + d_table, tuple((first + second for first, second in zip(running[1], d_params))))
        return (sums_new, (out_row.astype(jnp.bfloat16), d_emb.astype(jnp.bfloat16)))
    start_sums = (jnp.zeros(embed_f.shape, jnp.float32), tuple((jnp.zeros(weight_in.shape, jnp.float32) for weight_in in params)))
    (grad_emb, grads), (outputs, d_inputs) = lax.scan(one_row, start_sums, (byte_ids, row_lengths, cotangent))
    g_conv, g_score, g_one, g_query, g_key, g_value, g_out, g_rel, g_two, g_gate, g_up, g_down = grads
    return (outputs, d_inputs, grad_emb, g_conv, g_score, g_one, g_query, g_key, g_value, g_out, g_rel, g_two, g_gate, g_up, g_down)
```

```python
import functools
import jax, jax.numpy as jnp
from jax import lax
from jax.experimental import pallas as pl
from jax.experimental.pallas import tpu as pltpu
DH=64
NEG=-1e9
F32, BF16 = jnp.float32, jnp.bfloat16


def dot_nt(a, b):
    return lax.dot_general(a, b, (((1,), (1,)), ((), ())), preferred_element_type=F32)


def dot_nn(a, b):
    return lax.dot_general(a, b, (((1,), (0,)), ((), ())), preferred_element_type=F32)


def fill_strips(rev_ref, strip_ref, heads, blk, nblk):
    for head in range(heads):
        for part in range(2 * nblk - 1):
            low = (2 * nblk - 2 - part) * blk
            segment = jnp.broadcast_to(rev_ref[head : head + 1, low : low + 2 * blk], (blk, 2 * blk))
            turned = pltpu.roll(segment, 0, 1, stride=1, stride_axis=0)
            strip_ref[head, part * blk : (part + 1) * blk, :] = turned[:, blk:]


def key_side(key, ok_col):
    rows = key.shape[0]
    lane = lax.broadcasted_iota(jnp.int32, (rows, DH), 1)
    extra = jnp.where(lane == 0, ok_col, 0.0).astype(BF16)
    return jnp.concatenate([key, extra], axis=1)


def query_side(query):
    rows = query.shape[0]
    lane = lax.broadcasted_iota(jnp.int32, (rows, DH), 1)
    return jnp.concatenate([query, jnp.where(lane == 0, 1.0, 0.0).astype(BF16)], axis=1)


def mask_column(place_ref, limit, blk, nblk):
    cols = []
    for b in range(nblk):
        at = place_ref[b] * blk + lax.broadcasted_iota(jnp.int32, (blk, DH), 0)
        cols.append(jnp.where(2 * at < limit, 0.0, NEG))
    return jnp.concatenate(cols, axis=0)


def attend_kernel(heads, blk, nblk, place_ref, len_ref, qkv_ref, rev_ref, out_ref, log_ref, strip_ref, kaug_ref, qaug_ref, vt_ref):
    row = pl.program_id(0)

    @pl.when(row == 0)
    def _():
        fill_strips(rev_ref, strip_ref, heads, blk, nblk)

    ok_col = mask_column(place_ref, len_ref[row], blk, nblk)
    width = heads * DH
    for head in range(heads):
        at = head * DH
        qaug_ref[...] = query_side(qkv_ref[0, :, at : at + DH])
        kaug_ref[...] = key_side(qkv_ref[0, :, width + at : width + at + DH], ok_col)
        vt_ref[...] = qkv_ref[0, :, 2 * width + at : 2 * width + at + DH].T

        def one_block(qb, carry):
            q_at = pl.multiple_of(qb * blk, blk)
            q_place = place_ref[qb]
            query = qaug_ref[pl.ds(q_at, blk), :]
            parts = []
            for kb in range(nblk):
                m_at = pl.multiple_of((place_ref[kb] - q_place + nblk - 1) * blk, blk)
                parts.append(dot_nt(kaug_ref[kb * blk : (kb + 1) * blk, :], query) + strip_ref[head, pl.ds(m_at, blk), :])
            top = functools.reduce(jnp.maximum, [jnp.max(p, axis=0, keepdims=True) for p in parts])
            total = jnp.zeros((1, blk), F32)
            acc = jnp.zeros((DH, blk), F32)
            for kb in range(nblk):
                weight = jnp.exp(parts[kb] - top)
                total += jnp.sum(weight, axis=0, keepdims=True)
                acc += dot_nn(vt_ref[:, kb * blk : (kb + 1) * blk], weight.astype(BF16))
            o_at = pl.multiple_of(q_place * blk, blk)
            out_ref[0, pl.ds(o_at, blk), at : at + DH] = (acc / total).T.astype(BF16)
            log_ref[0, head, pl.ds(qb, 1), :] = top + jnp.log(total)
            return carry

        lax.fori_loop(0, nblk, one_block, 0)


def attend(place, row_len, qkv, rev, heads, nblk):
    rows, tokens = qkv.shape[:2]
    blk = tokens // nblk
    return pl.pallas_call(
        functools.partial(attend_kernel, heads, blk, nblk),
        grid_spec=pltpu.PrefetchScalarGridSpec(
            num_scalar_prefetch=2,
            grid=(rows,),
            in_specs=[
                pl.BlockSpec((1, tokens, 3 * heads * DH), lambda r, *_: (r, 0, 0)),
                pl.BlockSpec(rev.shape, lambda r, *_: (0, 0)),
            ],
            out_specs=[
                pl.BlockSpec((1, tokens, heads * DH), lambda r, *_: (r, 0, 0)),
                pl.BlockSpec((1, heads, nblk, blk), lambda r, *_: (r, 0, 0, 0)),
            ],
            scratch_shapes=[
                pltpu.VMEM((heads, (2 * nblk - 1) * blk, blk), F32),
                pltpu.VMEM((tokens, 2 * DH), BF16),
                pltpu.VMEM((tokens, 2 * DH), BF16),
                pltpu.VMEM((DH, tokens), BF16),
            ],
        ),
        out_shape=[
            jax.ShapeDtypeStruct((rows, tokens, heads * DH), BF16),
            jax.ShapeDtypeStruct((rows, heads, nblk, blk), F32),
        ],
        compiler_params=pltpu.CompilerParams(vmem_limit_bytes=48 << 20),
        cost_estimate=pl.CostEstimate(flops=16 * rows * heads * tokens * tokens * DH, bytes_accessed=rows * tokens * heads * DH * 8, transcendentals=rows * heads * tokens * tokens),
        name="attend",
    )(place, row_len, qkv, rev)


def attend_back_kernel(heads, blk, nblk, place_ref, len_ref, qkv_ref, out_ref, dout_ref, log_ref, rev_ref, dqkv_ref, drev_ref,
                       strip_ref, grads_ref, kaug_ref, qaug_ref, kt_ref, dk_ref, dv_ref):
    row = pl.program_id(0)

    @pl.when(row == 0)
    def _():
        fill_strips(rev_ref, strip_ref, heads, blk, nblk)
        grads_ref[...] = jnp.zeros_like(grads_ref)

    ok_col = mask_column(place_ref, len_ref[row], blk, nblk)
    width = heads * DH
    for head in range(heads):
        at = head * DH
        qaug_ref[...] = query_side(qkv_ref[0, :, at : at + DH])
        key = qkv_ref[0, :, width + at : width + at + DH]
        kaug_ref[...] = key_side(key, ok_col)
        kt_ref[...] = key.T
        dk_ref[...] = jnp.zeros_like(dk_ref)
        dv_ref[...] = jnp.zeros_like(dv_ref)

        def one_block(qb, carry):
            q_at = pl.multiple_of(qb * blk, blk)
            q_place = place_ref[qb]
            o_at = pl.multiple_of(q_place * blk, blk)
            query = qaug_ref[pl.ds(q_at, blk), :]
            dout = dout_ref[0, pl.ds(o_at, blk), at : at + DH]
            prod = dout.astype(F32) * out_ref[0, pl.ds(o_at, blk), at : at + DH].astype(F32)
            inner = jnp.sum(prod.T, axis=0, keepdims=True)
            log_row = log_ref[0, head, pl.ds(qb, 1), :]
            dqt = jnp.zeros((DH, blk), F32)
            for kb in range(nblk):
                here = slice(kb * blk, (kb + 1) * blk)
                m_at = pl.multiple_of((place_ref[kb] - q_place + nblk - 1) * blk, blk)
                score = dot_nt(kaug_ref[here, :], query) + strip_ref[head, pl.ds(m_at, blk), :]
                prob = jnp.exp(score - log_row)
                d_prob = dot_nt(qkv_ref[0, here, 2 * width + at : 2 * width + at + DH], dout)
                d_score = prob * (d_prob - inner)
                low = d_score.astype(BF16)
                grads_ref[head, pl.ds(m_at, blk), :] += d_score
                dv_ref[here, :] += dot_nn(prob.astype(BF16), dout)
                dk_ref[here, :] += dot_nn(low, query[:, :DH])
                dqt += dot_nn(kt_ref[:, here], low)
            dqkv_ref[0, pl.ds(q_at, blk), at : at + DH] = dqt.T.astype(BF16)
            return carry

        lax.fori_loop(0, nblk, one_block, 0)
        dqkv_ref[0, :, width + at : width + at + DH] = dk_ref[...].astype(BF16)
        dqkv_ref[0, :, 2 * width + at : 2 * width + at + DH] = dv_ref[...].astype(BF16)

    @pl.when(row == pl.num_programs(0) - 1)
    def _():
        flip = (
            lax.broadcasted_iota(jnp.int32, (blk, blk), 0) + lax.broadcasted_iota(jnp.int32, (blk, blk), 1) == blk - 1
        ).astype(F32).astype(BF16)
        drev_ref[...] = jnp.zeros_like(drev_ref)
        for head in range(heads):
            for part in range(2 * nblk - 1):
                grad = grads_ref[head, part * blk : (part + 1) * blk, :]
                high = grad.astype(BF16)
                rest = (grad - high.astype(F32)).astype(BF16)
                turned = dot_nn(flip, high) + dot_nn(flip, rest)
                wide = jnp.concatenate([jnp.zeros((blk, blk), F32), turned], axis=1)
                moved = pltpu.roll(wide, blk + 1, 1, stride=1, stride_axis=0)
                low = (2 * nblk - 2 - part) * blk
                drev_ref[head : head + 1, low : low + 2 * blk] += jnp.sum(moved, axis=0, keepdims=True)


def attend_back(place, row_len, qkv, out, dout, logs, rev, heads, nblk):
    rows, tokens = qkv.shape[:2]
    blk = tokens // nblk
    return pl.pallas_call(
        functools.partial(attend_back_kernel, heads, blk, nblk),
        grid_spec=pltpu.PrefetchScalarGridSpec(
            num_scalar_prefetch=2,
            grid=(rows,),
            in_specs=[
                pl.BlockSpec((1, tokens, 3 * heads * DH), lambda r, *_: (r, 0, 0)),
                pl.BlockSpec((1, tokens, heads * DH), lambda r, *_: (r, 0, 0)),
                pl.BlockSpec((1, tokens, heads * DH), lambda r, *_: (r, 0, 0)),
                pl.BlockSpec((1, heads, nblk, blk), lambda r, *_: (r, 0, 0, 0)),
                pl.BlockSpec(rev.shape, lambda r, *_: (0, 0)),
            ],
            out_specs=[
                pl.BlockSpec((1, tokens, 3 * heads * DH), lambda r, *_: (r, 0, 0)),
                pl.BlockSpec(rev.shape, lambda r, *_: (0, 0)),
            ],
            scratch_shapes=[
                pltpu.VMEM((heads, (2 * nblk - 1) * blk, blk), F32),
                pltpu.VMEM((heads, (2 * nblk - 1) * blk, blk), F32),
                pltpu.VMEM((tokens, 2 * DH), BF16),
                pltpu.VMEM((tokens, 2 * DH), BF16),
                pltpu.VMEM((DH, tokens), BF16),
                pltpu.VMEM((tokens, DH), F32),
                pltpu.VMEM((tokens, DH), F32),
            ],
        ),
        out_shape=[
            jax.ShapeDtypeStruct((rows, tokens, 3 * heads * DH), BF16),
            jax.ShapeDtypeStruct(rev.shape, F32),
        ],
        compiler_params=pltpu.CompilerParams(vmem_limit_bytes=56 << 20),
        cost_estimate=pl.CostEstimate(flops=40 * rows * heads * tokens * tokens * DH, bytes_accessed=rows * tokens * heads * DH * 16, transcendentals=rows * heads * tokens * tokens),
        name="attend_back",
    )(place, row_len, qkv, out, dout, logs, rev)


EPS = 1e-06
VOCAB = 259
P = jax.sharding.PartitionSpec


def extended_2(x, width):
    size, length = lax.axis_size("seq"), x.shape[1]
    up = [(i, i + 1) for i in range(size - 1)]
    down = [(j, i) for i, j in up]
    before = lax.ppermute(x[:, length - width :], "seq", up)
    after = lax.ppermute(x[:, :width], "seq", down)
    return jnp.concatenate([before, x, after], axis=1)


def rms_norm(hidden, gain_vec):
    factor = lax.rsqrt(jnp.mean(hidden * hidden, axis=-1, keepdims=True) + EPS)
    return hidden * factor * gain_vec


def geglu(gate_in, upward):
    return jax.nn.gelu(gate_in, approximate=True) * upward


def block_means(padded, offset, extent):
    places = offset + jnp.arange(extent, dtype=jnp.int32)
    results = []
    for block_len in range(1, 5):
        remain = places % block_len
        summed = 0.0
        for shift_at in range(1 - block_len, block_len):
            select = ((shift_at >= -remain) & (shift_at <= block_len - 1 - remain)).astype(F32)
            summed = summed + select[:, None] * padded[..., 3 + shift_at : 3 + shift_at + extent, :]
        results.append(summed / block_len)
    return results


def mix_blocks(padded, offset, extent, score_vec):
    averages = block_means(padded, offset, extent)
    scores = jnp.stack([jnp.sum(mean_b * score_vec, axis=-1) for mean_b in averages], axis=0)
    shares = jax.nn.softmax(scores, axis=0)
    pooled = sum((shares[which_b][..., None] * averages[which_b] for which_b in range(4)))
    dims_all = pooled.shape
    return jnp.mean(pooled.reshape(dims_all[:-2] + (dims_all[-2] // 2, 2, dims_all[-1])), axis=-2)


def front_part(extended, conv_vec, score_vec, offset, row_len):
    extent = extended.shape[1] - 8
    conv_out = sum(
        (conv_vec[tap_at] * extended[:, tap_at : tap_at + extent + 4] for tap_at in range(4))
    )
    places = offset - 2 + jnp.arange(extent + 4, dtype=jnp.int32)
    inside = (places[None, :] >= 0) & (places[None, :] < row_len[:, None])
    conv_out = conv_out * inside[:, :, None].astype(F32)
    padded = jnp.pad(conv_out, ((0, 0), (1, 1), (0, 0)))
    return mix_blocks(padded, offset, extent, score_vec)


def flip_with(x, axis, bit):
    return lax.ppermute(x, axis, [(i, i ^ bit) for i in range(lax.axis_size(axis))])


def bits_of(axis):
    bits, bit = [], 1
    while bit < lax.axis_size(axis):
        bits.append(bit)
        bit *= 2
    return bits[::-1]


def gather_blocks(x):
    blocks = [x]
    for bit in bits_of("seq"):
        blocks = blocks + [flip_with(block, "seq", bit) for block in blocks]
    return jnp.stack(blocks, axis=1)


def places_of(n):
    places = [0]
    bit = n // 2
    while bit:
        places = places + [p ^ bit for p in places]
        bit //= 2
    return places


def scatter_blocks(parts):
    for bit in bits_of("seq")[::-1]:
        half = len(parts) // 2
        got = [flip_with(part.astype(BF16), "seq", bit) for part in parts[half:]]
        parts = [mine.astype(F32) + other.astype(F32) for mine, other in zip(parts[:half], got)]
    return parts[0]


def gather_dp(x):
    me = lax.axis_index("dp")
    bits = bits_of("dp")
    for _ in bits:
        x = x[None]
    for at, bit in enumerate(bits):
        other = flip_with(x, "dp", bit)
        upper = (me & bit) != 0
        x = jnp.concatenate([jnp.where(upper, other, x), jnp.where(upper, x, other)], axis=at)
    return x.reshape((lax.axis_size("dp"),) + x.shape[len(bits) :])


def scatter_dp(x):
    me = lax.axis_index("dp")
    bits = bits_of("dp")[::-1]
    x = x.reshape((2,) * len(bits) + x.shape[1:])
    for bit in bits:
        axis = [b for b in bits[::-1]].index(bit)
        low, high = lax.index_in_dim(x, 0, axis), lax.index_in_dim(x, 1, axis)
        upper = (me & bit) != 0
        keep, send = jnp.where(upper, high, low), jnp.where(upper, low, high)
        x = keep.astype(F32) + flip_with(send.astype(BF16), "dp", bit).astype(F32)
    return x.reshape(x.shape[len(bits) :])


def sum_seq(x):
    for bit in bits_of("seq")[::-1]:
        x = x + flip_with(x, "seq", bit)
    return x


def on_device(
    byte_ids,
    lengths,
    deal_order,
    buckets,
    embedding,
    conv_w,
    score_w,
    gain_one,
    w_query,
    w_key,
    w_value,
    w_out,
    rel_bias,
    gain_two,
    w_gate,
    w_up,
    w_down,
    cotangent,
):
    n = lax.axis_size("seq")
    dp = lax.axis_size("dp")
    me = lax.axis_index("seq")
    rows_dev, extent = byte_ids.shape
    share, width = w_query.shape
    d_model = share * dp
    head_cols = width // n
    heads_dev = head_cols // DH
    ff_cols = w_gate.shape[1] // n
    down_rows = w_down.shape[0] // n
    tok = cotangent.shape[1]
    seq_len = tok * n
    place = jnp.array(places_of(n), jnp.int32) ^ me

    vocab = embedding.shape[0]
    front_pack = jnp.concatenate(
        [embedding, conv_w, score_w[None], gain_one[None], gain_two[None]], axis=0
    )
    front_all = gather_dp(front_pack).transpose(1, 0, 2).reshape(vocab + 7, d_model)
    emb_all = front_all[:vocab]
    conv_all = front_all[vocab : vocab + 4]
    score_all, gain_first, gain_second = (front_all[vocab + 4 + i] for i in range(3))

    def own_cols(weight):
        return lax.dynamic_slice_in_dim(weight, me * head_cols, head_cols, 1)

    qkv_pack = jnp.concatenate([own_cols(w_query), own_cols(w_key), own_cols(w_value)], axis=1)
    qkv_w = gather_dp(qkv_pack).reshape(d_model, 3 * head_cols)

    def own_ff(weight):
        return lax.dynamic_index_in_dim(weight.reshape(share, dp, n, down_rows), me, 2, keepdims=False).reshape(
            share, ff_cols
        )

    down_own = lax.dynamic_slice_in_dim(w_down, me * down_rows, down_rows, 0)
    pad_rows = max(share, down_rows)
    rest_pack = jnp.concatenate([own_ff(w_gate), own_ff(w_up), w_out], axis=1)
    rest_pack = jnp.pad(rest_pack, ((0, pad_rows - share), (0, 0)))
    rest_pack = jnp.concatenate([rest_pack, jnp.pad(down_own, ((0, pad_rows - down_rows), (0, 0)))], axis=1)
    rest_all = lax.all_gather(rest_pack, "dp", axis=0, tiled=False)
    gate_up_w = rest_all[:, :share, : 2 * ff_cols].reshape(d_model, 2 * ff_cols)
    out_w = rest_all[:, :share, 2 * ff_cols : 2 * ff_cols + width].reshape(d_model, width)
    down_w = rest_all[:, :down_rows, 2 * ff_cols + width :].reshape(ff_cols, width)

    offset = me * extent
    matches = deal_order[:, None] == jnp.arange(lengths.shape[0], dtype=jnp.int32)[None, :]
    row_len = jnp.sum(jnp.where(matches, lengths[None, :], 0), axis=1)
    places = offset + jnp.arange(extent, dtype=jnp.int32)
    live = (places[None, :] < row_len[:, None]).astype(BF16)[:, :, None]
    onehot_ids = (byte_ids[:, :, None] == jnp.arange(vocab, dtype=jnp.int32)).astype(BF16)
    masked = jnp.einsum("rtv,vd->rtd", onehot_ids, emb_all, preferred_element_type=F32).astype(BF16) * live
    extended = extended_2(masked, 4)

    def front_call(ext_in, conv_in, score_in):
        return front_part(ext_in, conv_in, score_in, offset, row_len)

    h_zero, front_back = jax.vjp(
        front_call, extended.astype(F32), conv_all.astype(F32), score_all.astype(F32)
    )
    normed_one, norm_one_back = jax.vjp(rms_norm, h_zero, gain_first.astype(F32))
    low_one = gather_blocks(normed_one.astype(BF16)).reshape(rows_dev, seq_len, d_model)
    qkv = jnp.einsum("rtd,de->rte", low_one, qkv_w, preferred_element_type=F32).astype(BF16)

    first_head = me * heads_dev
    bias_loc = lax.dynamic_slice_in_dim(rel_bias, first_head, heads_dev, 1)
    offsets = jnp.concatenate([jnp.full((1,), -1, jnp.int32), buckets[::-1]])
    onehot = (offsets[None, :] == jnp.arange(rel_bias.shape[0], dtype=jnp.int32)[:, None]).astype(BF16)
    rev = jnp.einsum("nh,nx->hx", bias_loc, onehot, preferred_element_type=F32)

    attended_heads, logs = attend(place, row_len, qkv, rev, heads_dev, n)
    attended = lax.all_to_all(attended_heads, "seq", split_axis=1, concat_axis=2, tiled=True)
    h_one = h_zero + jnp.dot(attended, out_w, preferred_element_type=F32)
    normed_two, norm_two_back = jax.vjp(rms_norm, h_one, gain_second.astype(F32))
    low_two = gather_blocks(normed_two.astype(BF16)).reshape(rows_dev, seq_len, d_model)
    cot_all = gather_blocks(cotangent).reshape(rows_dev, seq_len, d_model)
    gate_up = jnp.dot(low_two, gate_up_w, preferred_element_type=F32)
    mixed_ff, ff_back = jax.vjp(geglu, gate_up[..., :ff_cols], gate_up[..., ff_cols:])
    hidden = mixed_ff.astype(BF16)

    def blocks_of(x):
        x = x.reshape(rows_dev, n, tok, x.shape[-1])
        return [x[:, b] for b in range(n)]

    ff_out = scatter_blocks(blocks_of(jnp.dot(hidden, down_w, preferred_element_type=F32)))
    output = (h_one + ff_out).astype(BF16)
    grad_down = jnp.einsum("gtf,gtd->fd", hidden, cot_all, preferred_element_type=F32)
    d_hidden = jnp.einsum("gtd,fd->gtf", cot_all, down_w, preferred_element_type=F32)
    d_gate_f, d_up_f = ff_back(d_hidden)
    d_gate_up = jnp.concatenate([d_gate_f.astype(BF16), d_up_f.astype(BF16)], axis=-1)
    grad_gate_up = jnp.einsum("gtd,gtf->df", low_two, d_gate_up, preferred_element_type=F32)
    d_norm_two = scatter_blocks(
        blocks_of(jnp.einsum("gtf,df->gtd", d_gate_up, gate_up_w, preferred_element_type=F32))
    )
    d_h_norm, grad_gain_two = norm_two_back(d_norm_two)
    d_h_one = cotangent.astype(F32) + d_h_norm
    d_branch = d_h_one.astype(BF16)
    grad_out = jnp.einsum("gtd,gte->de", attended, d_branch, preferred_element_type=F32)
    d_attended = jnp.einsum("gte,de->gtd", d_branch, out_w, preferred_element_type=F32).astype(BF16)
    d_heads = lax.all_to_all(d_attended, "seq", split_axis=2, concat_axis=1, tiled=True)

    d_qkv, d_rev = attend_back(place, row_len, qkv, attended_heads, d_heads, logs, rev, heads_dev, n)
    grad_qkv = jnp.einsum("gtd,gte->de", low_one, d_qkv, preferred_element_type=F32)
    d_norm_one = scatter_blocks(
        blocks_of(jnp.einsum("gte,de->gtd", d_qkv, qkv_w, preferred_element_type=F32))
    )
    d_h_first, grad_gain_one = norm_one_back(d_norm_one)
    d_h_zero = d_h_one + d_h_first
    d_ext, grad_conv, grad_score = front_back(d_h_zero)
    rim_out = jnp.concatenate([d_ext[:, :4], d_ext[:, -4:]], axis=1)
    rim_in = extended_2(rim_out.astype(BF16), 4).astype(rim_out.dtype)
    d_masked = d_ext[:, 4:-4] + jnp.pad(rim_in[:, :4], ((0, 0), (0, extent - 4), (0, 0)))
    d_masked = d_masked + jnp.pad(rim_in[:, 12:], ((0, 0), (extent - 4, 0), (0, 0)))
    d_input = (d_masked * live.astype(F32)).astype(BF16)
    grad_emb = jnp.einsum("rtv,rtd->vd", onehot_ids, d_input, preferred_element_type=F32)

    d_rel_loc = jnp.einsum("nx,hx->nh", onehot.astype(F32), d_rev, precision=lax.Precision.HIGHEST)
    d_rel_full = lax.dynamic_update_slice_in_dim(
        jnp.zeros(rel_bias.shape, F32), d_rel_loc, first_head, 1
    )
    grad_rel_bias = lax.psum(d_rel_full, ("dp", "seq"))

    pad_ff = jnp.pad(grad_gate_up.astype(BF16).reshape(dp, share, 2 * ff_cols), ((0, 0), (0, pad_rows - share), (0, 0)))
    pad_down = jnp.pad(
        grad_down.astype(BF16).reshape(dp, down_rows, width), ((0, 0), (0, pad_rows - down_rows), (0, 0))
    )
    ff_sum = lax.psum_scatter(jnp.concatenate([pad_ff, pad_down], axis=2), "dp", scatter_dimension=0, tiled=False)

    late = jnp.concatenate(
        [grad_qkv.reshape(dp, share, 3 * head_cols), grad_out.reshape(dp, share, width)], axis=2
    )
    late_sum = scatter_dp(late)
    front_grads = jnp.concatenate(
        [grad_emb, grad_conv, grad_score[None], grad_gain_one[None], grad_gain_two[None]], axis=0
    )
    front_sum = sum_seq(scatter_dp(front_grads.reshape(vocab + 7, dp, share).transpose(1, 0, 2)))
    g_out = sum_seq(late_sum[:, 3 * head_cols :])

    own = jnp.concatenate(
        [
            late_sum[:, : 3 * head_cols].astype(BF16).reshape(-1),
            ff_sum[:share, : 2 * ff_cols].reshape(-1),
            ff_sum[:down_rows, 2 * ff_cols :].reshape(-1),
        ]
    )
    every = lax.all_gather(own, "seq", axis=0, tiled=False).astype(F32)
    cut = share * 3 * head_cols
    cut_two = cut + share * 2 * ff_cols
    g_qkv = every[:, :cut].reshape(n, share, 3, head_cols).transpose(2, 1, 0, 3).reshape(3, share, width)
    g_gu = (
        every[:, cut:cut_two].reshape(n, share, 2, dp, down_rows).transpose(2, 1, 3, 0, 4).reshape(2, share, n * ff_cols)
    )
    g_down = every[:, cut_two:].reshape(n * down_rows, width)
    return (
        output,
        d_input,
        front_sum[:vocab],
        front_sum[vocab : vocab + 4],
        front_sum[vocab + 4],
        front_sum[vocab + 5],
        g_qkv[0],
        g_qkv[1],
        g_qkv[2],
        g_out,
        grad_rel_bias,
        front_sum[vocab + 6],
        g_gu[0],
        g_gu[1],
        g_down,
    )


def solution(mesh):
    return jax.shard_map(
        on_device,
        mesh=mesh,
        in_specs=(
            P("dp", "seq"),
            P(),
            P("dp"),
            P(),
            P(None, "dp"),
            P(None, "dp"),
            P("dp"),
            P("dp"),
            P("dp", None),
            P("dp", None),
            P("dp", None),
            P("dp", None),
            P(),
            P("dp"),
            P("dp", None),
            P("dp", None),
            P("dp", None),
            P("dp", "seq", None),
        ),
        out_specs=(
            P("dp", "seq", None),
            P("dp", "seq", None),
            P(None, "dp"),
            P(None, "dp"),
            P("dp"),
            P("dp"),
            P("dp", None),
            P("dp", None),
            P("dp", None),
            P("dp", None),
            P(),
            P("dp"),
            P("dp", None),
            P("dp", None),
            P("dp", None),
        ),
        check_vma=False,
    )
```

```python
import functools
import jax, jax.numpy as jnp
from jax import lax
from jax.experimental import pallas as pl
from jax.experimental.pallas import tpu as pltpu
DH=64
NEG=-1e9
F32, BF16 = jnp.float32, jnp.bfloat16


def dot_nt(a, b):
    return lax.dot_general(a, b, (((1,), (1,)), ((), ())), preferred_element_type=F32)


def dot_nn(a, b):
    return lax.dot_general(a, b, (((1,), (0,)), ((), ())), preferred_element_type=F32)


def tile_at(place_ref, kb, qb, nblk):
    return jnp.clip(place_ref[kb] - place_ref[qb], -2, 2) + 2


def strip_kernel(nblk, rev_ref, strip_ref):
    heads, _, blk = strip_ref.shape
    for head in range(heads):
        for part in range(5):
            low = (nblk + 1 - part) * blk
            here = slice(part * blk, (part + 1) * blk)
            if part in (0, 4):
                strip_ref[head, here, :] = jnp.broadcast_to(rev_ref[head : head + 1, low + blk : low + blk + 1], (blk, blk))
                continue
            segment = jnp.broadcast_to(rev_ref[head : head + 1, low : low + 2 * blk], (blk, 2 * blk))
            strip_ref[head, here, :] = pltpu.roll(segment, 0, 1, stride=1, stride_axis=0)[:, blk:]


def bias_strips(rev, nblk):
    heads, width = rev.shape
    blk = width // (2 * nblk)
    return pl.pallas_call(
        functools.partial(strip_kernel, nblk),
        out_shape=jax.ShapeDtypeStruct((heads, 5 * blk, blk), F32),
        compiler_params=pltpu.CompilerParams(vmem_limit_bytes=32 << 20),
        name="strips",
    )(rev)


def key_side(key, ok_col):
    rows = key.shape[0]
    lane = lax.broadcasted_iota(jnp.int32, (rows, DH), 1)
    extra = jnp.where(lane == 0, ok_col, 0.0).astype(BF16)
    return jnp.concatenate([key, extra], axis=1)


def query_side(query):
    rows = query.shape[0]
    lane = lax.broadcasted_iota(jnp.int32, (rows, DH), 1)
    return jnp.concatenate([query, jnp.where(lane == 0, 1.0, 0.0).astype(BF16)], axis=1)


def mask_column(place_ref, limit, blk, nblk):
    cols = []
    for b in range(nblk):
        at = place_ref[b] * blk + lax.broadcasted_iota(jnp.int32, (blk, DH), 0)
        cols.append(jnp.where(2 * at < limit, 0.0, NEG))
    return jnp.concatenate(cols, axis=0)


def dot_tn(a, b):
    return lax.dot_general(a, b, (((0,), (0,)), ((), ())), preferred_element_type=F32)


def in_vmem(args):
    return [pl.BlockSpec(memory_space=pltpu.VMEM) for _ in args]


def scalars():
    return pl.BlockSpec(memory_space=pltpu.SMEM)


def attend_kernel(heads, nblk, place_ref, len_ref, *refs):
    xs, (w_ref, strip_ref), refs = refs[:nblk], refs[nblk : nblk + 2], refs[nblk + 2 :]
    outs, (qkv_ref, log_ref, att_ref, kaug_ref, qaug_ref, vt_ref) = refs[:nblk], refs[nblk:]
    blk = xs[0].shape[0]
    for b in range(nblk):
        qkv_ref[b * blk : (b + 1) * blk, :] = dot_nn(xs[b][...], w_ref[...]).astype(BF16)
    ok_col = mask_column(place_ref, len_ref[0], blk, nblk)
    width = heads * DH
    for head in range(heads):
        at = head * DH
        qaug_ref[...] = query_side(qkv_ref[:, at : at + DH])
        kaug_ref[...] = key_side(qkv_ref[:, width + at : width + at + DH], ok_col)
        vt_ref[...] = qkv_ref[:, 2 * width + at : 2 * width + at + DH].T

        def one_block(qb, carry):
            q_at = pl.multiple_of(qb * blk, blk)
            query = qaug_ref[pl.ds(q_at, blk), :]
            parts = []
            for kb in range(nblk):
                m_at = pl.multiple_of(tile_at(place_ref, kb, qb, nblk) * blk, blk)
                parts.append(dot_nt(kaug_ref[kb * blk : (kb + 1) * blk, :], query) + strip_ref[head, pl.ds(m_at, blk), :])
            top = functools.reduce(jnp.maximum, [jnp.max(p, axis=0, keepdims=True) for p in parts])
            total = jnp.zeros((1, blk), F32)
            acc = jnp.zeros((DH, blk), F32)
            for kb in range(nblk):
                weight = jnp.exp(parts[kb] - top)
                total += jnp.sum(weight, axis=0, keepdims=True)
                acc += dot_nn(vt_ref[:, kb * blk : (kb + 1) * blk], weight.astype(BF16))
            att_ref[pl.ds(q_at, blk), at : at + DH] = (acc / total).T.astype(BF16)
            log_ref[head, pl.ds(qb, 1), :] = top + jnp.log(total)
            return carry

        lax.fori_loop(0, nblk, one_block, 0)
    for b in range(nblk):
        outs[b][...] = att_ref[b * blk : (b + 1) * blk, :]


def attend(place, row_len, xs, w_qkv, strips):
    nblk = len(xs)
    blk = xs[0].shape[0]
    heads = strips.shape[0]
    tokens = nblk * blk
    outs = [jax.ShapeDtypeStruct((blk, heads * DH), BF16)] * nblk + [
        jax.ShapeDtypeStruct((tokens, 3 * heads * DH), BF16),
        jax.ShapeDtypeStruct((heads, nblk, blk), F32),
    ]
    args = [*xs, w_qkv, strips]
    got = pl.pallas_call(
        functools.partial(attend_kernel, heads, nblk),
        in_specs=[scalars(), scalars(), *in_vmem(args)],
        out_specs=in_vmem(outs),
        out_shape=outs,
        scratch_shapes=[
            pltpu.VMEM((tokens, heads * DH), BF16),
            pltpu.VMEM((tokens, 2 * DH), BF16),
            pltpu.VMEM((tokens, 2 * DH), BF16),
            pltpu.VMEM((DH, tokens), BF16),
        ],
        compiler_params=pltpu.CompilerParams(vmem_limit_bytes=48 << 20),
        cost_estimate=pl.CostEstimate(flops=48 * heads * tokens * tokens * DH, bytes_accessed=8 << 20, transcendentals=heads * tokens * tokens),
        name="attend",
    )(place, row_len, *args)
    return got[:nblk], got[nblk], got[nblk + 1]


def attend_back_kernel(heads, nblk, first, final, place_ref, len_ref, *refs):
    xs, (w_ref, qkv_ref), refs = refs[:nblk], refs[nblk : nblk + 2], refs[nblk + 2 :]
    os, dos, (log_ref, strip_ref), refs = refs[:nblk], refs[nblk : 2 * nblk], refs[2 * nblk : 2 * nblk + 2], refs[2 * nblk + 2 :]
    sum_in = None
    if not first:
        sum_in, refs = refs[0], refs[1:]
    dns, (sum_ref, drev_ref), refs = refs[:nblk], refs[nblk : nblk + 2], refs[nblk + 2 :]
    grads_ref, kaug_ref, qaug_ref, kt_ref, dk_ref, dv_ref, o_ref, do_ref, dqkv_ref = refs
    blk = xs[0].shape[0]
    for b in range(nblk):
        o_ref[b * blk : (b + 1) * blk, :] = os[b][...]
        do_ref[b * blk : (b + 1) * blk, :] = dos[b][...]
    ok_col = mask_column(place_ref, len_ref[0], blk, nblk)
    width = heads * DH
    for head in range(heads):
        grads_ref[head] = jnp.zeros(grads_ref.shape[1:], F32)
        at = head * DH
        qaug_ref[...] = query_side(qkv_ref[:, at : at + DH])
        key = qkv_ref[:, width + at : width + at + DH]
        kaug_ref[...] = key_side(key, ok_col)
        kt_ref[...] = key.T
        dk_ref[...] = jnp.zeros_like(dk_ref)
        dv_ref[...] = jnp.zeros_like(dv_ref)

        def one_block(qb, carry):
            q_at = pl.multiple_of(qb * blk, blk)
            query = qaug_ref[pl.ds(q_at, blk), :]
            dout = do_ref[pl.ds(q_at, blk), at : at + DH]
            prod = dout.astype(F32) * o_ref[pl.ds(q_at, blk), at : at + DH].astype(F32)
            inner = jnp.sum(prod.T, axis=0, keepdims=True)
            log_row = log_ref[head, pl.ds(qb, 1), :]
            dqt = jnp.zeros((DH, blk), F32)
            for kb in range(nblk):
                here = slice(kb * blk, (kb + 1) * blk)
                m_at = pl.multiple_of(tile_at(place_ref, kb, qb, nblk) * blk, blk)
                score = dot_nt(kaug_ref[here, :], query) + strip_ref[head, pl.ds(m_at, blk), :]
                prob = jnp.exp(score - log_row)
                d_prob = dot_nt(qkv_ref[here, 2 * width + at : 2 * width + at + DH], dout)
                d_score = prob * (d_prob - inner)
                low = d_score.astype(BF16)
                grads_ref[head, pl.ds(m_at, blk), :] += d_score
                dv_ref[here, :] += dot_nn(prob.astype(BF16), dout)
                dk_ref[here, :] += dot_nn(low, query[:, :DH])
                dqt += dot_nn(kt_ref[:, here], low)
            dqkv_ref[pl.ds(q_at, blk), at : at + DH] = dqt.T.astype(BF16)
            return carry

        lax.fori_loop(0, nblk, one_block, 0)
        dqkv_ref[:, width + at : width + at + DH] = dk_ref[...].astype(BF16)
        dqkv_ref[:, 2 * width + at : 2 * width + at + DH] = dv_ref[...].astype(BF16)

    total = None
    for b in range(nblk):
        here = dqkv_ref[b * blk : (b + 1) * blk, :]
        dns[b][...] = dot_nt(here, w_ref[...]).astype(BF16)
        grad = dot_tn(xs[b][...], here)
        total = grad if total is None else total + grad
    if not first:
        total += sum_in[...]
    sum_ref[...] = total.astype(BF16).reshape(sum_ref.shape) if final else total

    flip = (
        lax.broadcasted_iota(jnp.int32, (blk, blk), 0) + lax.broadcasted_iota(jnp.int32, (blk, blk), 1) == blk - 1
    ).astype(F32).astype(BF16)
    drev_ref[...] = jnp.zeros_like(drev_ref)
    for head in range(heads):
        for part in range(5):
            low = (nblk + 1 - part) * blk
            grad = grads_ref[head, part * blk : (part + 1) * blk, :]
            if part in (0, 4):
                whole = jnp.sum(jnp.sum(grad, axis=0, keepdims=True), axis=1, keepdims=True)
                drev_ref[head : head + 1, low + blk : low + blk + 1] += whole
                continue
            high = grad.astype(BF16)
            rest = (grad - high.astype(F32)).astype(BF16)
            turned = dot_nn(flip, high) + dot_nn(flip, rest)
            wide = jnp.concatenate([jnp.zeros((blk, blk), F32), turned], axis=1)
            moved = pltpu.roll(wide, blk + 1, 1, stride=1, stride_axis=0)
            drev_ref[head : head + 1, low : low + 2 * blk] += jnp.sum(moved, axis=0, keepdims=True)


def attend_back(place, row_len, xs, w_qkv, qkv, outs, douts, logs, strips, sum_in, parts):
    nblk = len(xs)
    blk, d_model = xs[0].shape
    heads = strips.shape[0]
    tokens = nblk * blk
    cols = 3 * heads * DH
    args = [*xs, w_qkv, qkv, *outs, *douts, logs, strips] + ([] if sum_in is None else [sum_in])
    sum_shape = jax.ShapeDtypeStruct((parts, d_model // parts, cols), BF16) if parts else jax.ShapeDtypeStruct((d_model, cols), F32)
    shapes = [jax.ShapeDtypeStruct((blk, d_model), BF16)] * nblk + [sum_shape, jax.ShapeDtypeStruct((heads, 2 * tokens), F32)]
    got = pl.pallas_call(
        functools.partial(attend_back_kernel, heads, nblk, sum_in is None, bool(parts)),
        in_specs=[scalars(), scalars(), *in_vmem(args)],
        out_specs=in_vmem(shapes),
        out_shape=shapes,
        scratch_shapes=[
            pltpu.VMEM((heads, 5 * blk, blk), F32),
            pltpu.VMEM((tokens, 2 * DH), BF16),
            pltpu.VMEM((tokens, 2 * DH), BF16),
            pltpu.VMEM((DH, tokens), BF16),
            pltpu.VMEM((tokens, DH), F32),
            pltpu.VMEM((tokens, DH), F32),
            pltpu.VMEM((tokens, heads * DH), BF16),
            pltpu.VMEM((tokens, heads * DH), BF16),
            pltpu.VMEM((tokens, cols), BF16),
        ],
        compiler_params=pltpu.CompilerParams(vmem_limit_bytes=56 << 20),
        cost_estimate=pl.CostEstimate(flops=120 * heads * tokens * tokens * DH, bytes_accessed=16 << 20, transcendentals=heads * tokens * tokens),
        name="attend_back",
    )(place, row_len, *args)
    return got[:nblk], got[nblk], got[nblk + 1]


EPS = 1e-06


def project_kernel(nblk, rows, place_ref, *refs):
    cols_refs, refs = refs[:nblk], refs[nblk:]
    atts, refs = refs[: rows * nblk], refs[rows * nblk :]
    hids, gain_ref, w_ref, outs = refs[:rows], refs[rows], refs[rows + 1], refs[rows + 2 :]
    cols = cols_refs[0].shape[1]
    for b in range(nblk):
        for g in range(nblk):

            @pl.when(place_ref[b] == g)
            def _():
                w_ref[:, g * cols : (g + 1) * cols] = cols_refs[b][...]

    for r in range(rows):
        hid = hids[r][...]
        for b in range(nblk):
            here = pl.ds(pl.multiple_of(place_ref[b] * cols, 16), cols)
            hid += dot_nn(atts[r * nblk + b][...], w_ref[here, :])
        outs[2 * r][...] = hid
        factor = lax.rsqrt(jnp.mean(hid * hid, axis=-1, keepdims=True) + EPS)
        outs[2 * r + 1][...] = (hid * factor * gain_ref[...]).astype(BF16)


def project(place, w_blocks, atts, hids, gain):
    rows, nblk = len(atts), len(w_blocks)
    width = w_blocks[0].shape[0]
    args = [*w_blocks, *[block for row in atts for block in row], *hids, gain]
    outs = [jax.ShapeDtypeStruct((width, hids[0].shape[1]), BF16)]
    for hid in hids:
        outs += [jax.ShapeDtypeStruct(hid.shape, F32), jax.ShapeDtypeStruct(hid.shape, BF16)]
    got = pl.pallas_call(
        functools.partial(project_kernel, nblk, rows),
        in_specs=[scalars(), *in_vmem(args)],
        out_specs=in_vmem(outs),
        out_shape=outs,
        compiler_params=pltpu.CompilerParams(vmem_limit_bytes=32 << 20),
        cost_estimate=pl.CostEstimate(flops=4 * rows * hids[0].shape[0] * width * width, bytes_accessed=3 << 20, transcendentals=0),
        name="project",
    )(place, *args)
    return got[0], got[1::2], got[2::2]


def norm_back(hid, gain, d_norm):
    factor = lax.rsqrt(jnp.mean(hid * hid, axis=-1, keepdims=True) + EPS)
    scaled = hid * factor
    weighted = d_norm * gain
    inner = jnp.mean(scaled * weighted, axis=-1, keepdims=True)
    return factor * (weighted - scaled * inner), jnp.sum(d_norm * scaled, axis=0, keepdims=True)


def project_back_kernel(nblk, pieces, row, first, final, place_ref, *refs):
    adds, atts, refs = refs[:pieces], refs[pieces : pieces + nblk], refs[pieces + nblk :]
    (w_ref, hid_ref, cot_ref, gain_ref), refs = refs[:4], refs[4:]
    sum_in = None
    if not first:
        sum_in, refs = refs[0], refs[1:]
    dhid_ref, gain_out, datts, sum_ref, acc_ref = refs[0], refs[1], refs[2 : 2 + nblk], refs[2 + nblk], refs[3 + nblk]
    d_norm = adds[0][...].astype(F32)
    for add in adds[1:]:
        d_norm += add[...].astype(F32)
    back, gain_grad = norm_back(hid_ref[...], gain_ref[...], d_norm)
    gain_out[...] = gain_grad
    d_hid = cot_ref[row].astype(F32) + back
    dhid_ref[...] = d_hid
    branch = d_hid.astype(BF16)
    cols = atts[0].shape[1]
    for b in range(nblk):
        here = pl.ds(pl.multiple_of(place_ref[b] * cols, 16), cols)
        datts[b][...] = dot_nt(branch, w_ref[here, :]).astype(BF16)
        grad = dot_tn(atts[b][...], branch)
        acc_ref[here, :] = grad if first else sum_in[here, :] + grad
    if final:
        sum_ref[...] = acc_ref[...].astype(BF16).reshape(sum_ref.shape)
    else:
        sum_ref[...] = acc_ref[...]


def project_back(place, adds, atts, w_out, hid, cot, row, gain, sum_in, parts):
    nblk = len(atts)
    blk, cols = atts[0].shape
    width, d_model = w_out.shape
    args = [*adds, *atts, w_out, hid, cot, gain] + ([] if sum_in is None else [sum_in])
    sum_shape = jax.ShapeDtypeStruct((parts, width // parts, d_model), BF16) if parts else jax.ShapeDtypeStruct((width, d_model), F32)
    outs = [jax.ShapeDtypeStruct(hid.shape, F32), jax.ShapeDtypeStruct((1, d_model), F32)]
    outs += [jax.ShapeDtypeStruct((blk, cols), BF16)] * nblk + [sum_shape]
    got = pl.pallas_call(
        functools.partial(project_back_kernel, nblk, len(adds), row, sum_in is None, bool(parts)),
        in_specs=[scalars(), *in_vmem(args)],
        out_specs=in_vmem(outs),
        out_shape=outs,
        scratch_shapes=[pltpu.VMEM((width, d_model), F32)],
        compiler_params=pltpu.CompilerParams(vmem_limit_bytes=32 << 20),
        cost_estimate=pl.CostEstimate(flops=8 * blk * width * d_model, bytes_accessed=6 << 20, transcendentals=0),
        name="project_back",
    )(place, *args)
    return got[0], got[1], got[2 : 2 + nblk], got[2 + nblk]


def first_back_kernel(pieces, *refs):
    adds, (hid_ref, dhid_ref, gain_ref, out_ref, low_ref, high_ref, gain_out) = refs[:pieces], refs[pieces:]
    d_norm = adds[0][...].astype(F32)
    for add in adds[1:]:
        d_norm += add[...].astype(F32)
    back, gain_grad = norm_back(hid_ref[...], gain_ref[...], d_norm)
    gain_out[...] = gain_grad
    d_hid = dhid_ref[...] + back
    out_ref[...] = d_hid
    low_ref[...] = d_hid[:8]
    high_ref[...] = d_hid[-8:]


def first_back(adds, hid, d_hid, gain):
    args = [*adds, hid, d_hid, gain]
    d_model = hid.shape[1]
    outs = [jax.ShapeDtypeStruct(s, F32) for s in (hid.shape, (8, d_model), (8, d_model), (1, d_model))]
    return pl.pallas_call(
        functools.partial(first_back_kernel, len(adds)),
        in_specs=in_vmem(args),
        out_specs=in_vmem(outs),
        out_shape=outs,
        compiler_params=pltpu.CompilerParams(vmem_limit_bytes=32 << 20),
        cost_estimate=pl.CostEstimate(flops=20 * hid.shape[0] * d_model, bytes_accessed=4 << 20, transcendentals=0),
        name="first_back",
    )(*args)


EDGE = 8


def split_two(x):
    high = x.astype(BF16)
    return high, (x - high.astype(F32)).astype(BF16)


def dot_fine(dot, a, b):
    a_high, a_rest = split_two(a)
    b_high, b_rest = split_two(b)
    return dot(a_high, b_high) + (dot(a_high, b_rest) + dot(a_rest, b_high))


def dot_half(dot, a, b_low):
    a_high, a_rest = split_two(a)
    return dot(a_high, b_low) + dot(a_rest, b_low)


def same_block(first, frame, size):
    def group(axis, shape):
        place = lax.broadcasted_iota(jnp.int32, shape, axis) + first
        return jnp.floor((place.astype(F32) + 0.5) * (1.0 / size))

    return (group(0, (frame, 1)) == group(1, (1, frame))).astype(F32)


def unpack_front(pack_ref, wall_ref):
    parts, _, share = pack_ref.shape
    for d in range(parts):
        wall_ref[:, d * share : (d + 1) * share] = pack_ref[d]


def front_kernel(vocab, at_ref, len_ref, ids_ref, pack_ref, hid_ref, norm_ref, conv_ref, mask_ref, share_ref, wall_ref, tri_ref, quad_ref, pair_ref, x_ref):
    row = pl.program_id(0)
    frame = ids_ref.shape[2]
    tok = hid_ref.shape[1]
    first = at_ref[0] - EDGE

    @pl.when(row == 0)
    def _():
        unpack_front(pack_ref, wall_ref)
        for ref, size in ((pair_ref, 2), (tri_ref, 3), (quad_ref, 4)):
            ref[...] = same_block(first + 12 * EDGE, frame, size).astype(BF16)

    limit = len_ref[row]
    pad = wall_ref.shape[0]
    place_row = lax.broadcasted_iota(jnp.int32, (1, frame), 1) + first
    live_row = (place_row >= 0) & (place_row < limit)
    ids = jnp.where(live_row, ids_ref[0], -1)
    onehot = (lax.broadcasted_iota(jnp.int32, (pad, frame), 0) == ids).astype(F32).astype(BF16)
    masked = lax.dot_general(onehot, wall_ref[...], (((0,), (0,)), ((), ())), preferred_element_type=F32)
    mask_ref[0] = masked[EDGE : frame - EDGE].astype(BF16)
    x_ref[0:EDGE, :] = jnp.zeros((EDGE, masked.shape[1]), F32)
    x_ref[EDGE : EDGE + frame, :] = masked
    x_ref[EDGE + frame :, :] = jnp.zeros((EDGE, masked.shape[1]), F32)
    vectors = wall_ref[pad - 16 :, :].astype(F32)
    base = vocab - (pad - 16)
    place_col = lax.broadcasted_iota(jnp.int32, (frame, 1), 0) + first
    live_col = ((place_col >= 0) & (place_col < limit)).astype(F32)
    conv = vectors[base : base + 1] * x_ref[EDGE - 2 : EDGE - 2 + frame, :]
    for j in range(1, 4):
        conv += vectors[base + j : base + j + 1] * x_ref[EDGE - 2 + j : EDGE - 2 + j + frame, :]
    conv = conv * live_col
    conv_ref[0] = conv
    c_high, c_rest = split_two(conv)
    score_w = jnp.broadcast_to(vectors[base + 4 : base + 5], (8, conv.shape[1])).astype(BF16)
    single = (dot_nt(score_w, c_high) + dot_nt(score_w, c_rest))[0:1]
    s_high = single.astype(BF16).astype(F32)
    s_mid = (single - s_high).astype(BF16).astype(F32)
    stack = jnp.concatenate([s_high, s_mid, single - s_high - s_mid, jnp.zeros((5, frame), F32)], axis=0).astype(BF16)
    scores = [single]
    for ref, size in ((pair_ref, 2), (tri_ref, 3), (quad_ref, 4)):
        scores.append(jnp.sum(dot_nn(stack, ref[...]), axis=0, keepdims=True) * (1.0 / size))
    top = functools.reduce(jnp.maximum, scores)
    raw = [jnp.exp(s - top) for s in scores]
    total = raw[0] + raw[1] + raw[2] + raw[3]
    shares = jnp.concatenate([r / total for r in raw] + [jnp.zeros((4, frame), F32)], axis=0)
    share_ref[0] = shares
    cols = shares.T
    one = (lax.broadcasted_iota(jnp.int32, (frame, frame), 0) == lax.broadcasted_iota(jnp.int32, (frame, frame), 1))
    mix = jnp.where(one, cols[:, 0:1], 0.0)
    for at, (ref, size) in enumerate(((pair_ref, 2), (tri_ref, 3), (quad_ref, 4))):
        mix += ref[...].astype(F32) * (cols[:, at + 1 : at + 2] * (1.0 / size))
    start = 2 * lax.broadcasted_iota(jnp.int32, (tok, frame), 0) + EDGE
    here = lax.broadcasted_iota(jnp.int32, (tok, frame), 1)
    pool = jnp.where((here == start) | (here == start + 1), 0.5, 0.0).astype(BF16)
    m_high, m_rest = split_two(mix)
    weights = dot_nn(pool, m_high) + dot_nn(pool, m_rest)
    w_high, w_rest = split_two(weights)
    hid = dot_nn(w_high, c_high) + (dot_nn(w_high, c_rest) + dot_nn(w_rest, c_high))
    hid_ref[0] = hid
    factor = lax.rsqrt(jnp.mean(hid * hid, axis=-1, keepdims=True) + EPS)
    norm_ref[0] = (hid * factor * vectors[base + 5 : base + 6]).astype(BF16)


def front_forward(at, row_len, ids, pack, vocab, d_model):
    rows, _, frame = ids.shape
    extent = frame - 2 * EDGE
    tok = extent // 2
    pad = pack.shape[1]
    by_row = lambda r, *_: (r, 0, 0)
    return pl.pallas_call(
        functools.partial(front_kernel, vocab),
        grid_spec=pltpu.PrefetchScalarGridSpec(
            num_scalar_prefetch=2,
            grid=(rows,),
            in_specs=[
                pl.BlockSpec((1, 1, frame), by_row),
                pl.BlockSpec(pack.shape, lambda r, *_: (0, 0, 0)),
            ],
            out_specs=[
                pl.BlockSpec((1, tok, d_model), by_row),
                pl.BlockSpec((1, tok, d_model), by_row),
                pl.BlockSpec((1, frame, d_model), by_row),
                pl.BlockSpec((1, extent, d_model), by_row),
                pl.BlockSpec((1, 8, frame), by_row),
            ],
            scratch_shapes=[
                pltpu.VMEM((pad, d_model), BF16),
                pltpu.VMEM((frame, frame), BF16),
                pltpu.VMEM((frame, frame), BF16),
                pltpu.VMEM((frame, frame), BF16),
                pltpu.VMEM((frame + 2 * EDGE, d_model), F32),
            ],
        ),
        out_shape=[
            jax.ShapeDtypeStruct((rows, tok, d_model), F32),
            jax.ShapeDtypeStruct((rows, tok, d_model), BF16),
            jax.ShapeDtypeStruct((rows, frame, d_model), F32),
            jax.ShapeDtypeStruct((rows, extent, d_model), BF16),
            jax.ShapeDtypeStruct((rows, 8, frame), F32),
        ],
        compiler_params=pltpu.CompilerParams(vmem_limit_bytes=48 << 20),
        cost_estimate=pl.CostEstimate(flops=rows * 8 * frame * frame * d_model, bytes_accessed=rows * frame * d_model * 9, transcendentals=0),
        name="front",
    )(at, row_len, ids, pack)


def front_back_kernel(vocab, at_ref, len_ref, ids_ref, pack_ref, dhid_ref, rim_ref, conv_ref, mask_ref, share_ref, gain_ref, din_ref, grad_ref,
                      wall_ref, tri_ref, quad_ref, pair_ref, dconv_ref, sum_ref):
    row = pl.program_id(0)
    frame = ids_ref.shape[2]
    tok = dhid_ref.shape[1]
    extent = frame - 2 * EDGE
    first = at_ref[0] - EDGE
    pad = wall_ref.shape[0]

    @pl.when(row == 0)
    def _():
        unpack_front(pack_ref, wall_ref)
        for ref, size in ((pair_ref, 2), (tri_ref, 3), (quad_ref, 4)):
            ref[...] = same_block(first + 12 * EDGE, frame, size).astype(BF16)
        sum_ref[...] = jnp.zeros_like(sum_ref)

    limit = len_ref[row]
    vectors = wall_ref[pad - 16 :, :].astype(F32)
    base = vocab - (pad - 16)
    shares = [share_ref[0, b : b + 1, :] for b in range(4)]
    one = (lax.broadcasted_iota(jnp.int32, (frame, frame), 0) == lax.broadcasted_iota(jnp.int32, (frame, frame), 1)).astype(F32)
    masks = [one] + [ref[...].astype(F32) * (1.0 / size) for ref, size in ((pair_ref, 2), (tri_ref, 3), (quad_ref, 4))]
    mix = functools.reduce(jnp.add, [m * s for m, s in zip(masks, shares)])
    start = 2 * lax.broadcasted_iota(jnp.int32, (frame, tok), 1) + EDGE
    here = lax.broadcasted_iota(jnp.int32, (frame, tok), 0)
    pool = jnp.where((here == start) | (here == start + 1), 0.5, 0.0).astype(BF16)
    rim_at = lax.broadcasted_iota(jnp.int32, (frame, EDGE), 1)
    rim_start = 2 * rim_at + jnp.where(rim_at < EDGE // 2, 0, extent)
    rim_here = lax.broadcasted_iota(jnp.int32, (frame, EDGE), 0)
    rim_pool = jnp.where((rim_here == rim_start) | (rim_here == rim_start + 1), 0.5, 0.0).astype(BF16)
    m_high, m_rest = split_two(mix)
    conv = conv_ref[0]
    c_high, c_rest = split_two(conv)
    d_conv = jnp.zeros(conv.shape, F32)
    cross = jnp.zeros((frame, frame), F32)
    for ref, spread in ((dhid_ref, pool), (rim_ref, rim_pool)):
        d_high, d_rest = split_two(ref[0])
        weights = dot_nn(m_high, spread) + dot_nn(m_rest, spread)
        w_high, w_rest = split_two(weights)
        d_conv += dot_nn(w_high, d_high) + (dot_nn(w_high, d_rest) + dot_nn(w_rest, d_high))
        pairs = dot_nt(c_high, d_high) + (dot_nt(c_high, d_rest) + dot_nt(c_rest, d_high))
        cross += dot_half(dot_nt, pairs, spread)
    d_shares = [jnp.sum(m * cross, axis=0, keepdims=True) for m in masks]
    inner = functools.reduce(jnp.add, [s * d for s, d in zip(shares, d_shares)])
    d_single = jnp.sum(
        functools.reduce(jnp.add, [m * (s * (d - inner)) for m, s, d in zip(masks, shares, d_shares)]), axis=1, keepdims=True
    )
    own_col = lax.broadcasted_iota(jnp.int32, (frame, 1), 0)
    place_col = own_col + first
    live_col = ((place_col >= 0) & (place_col < limit)).astype(F32)
    own = ((own_col >= EDGE) & (own_col < frame - EDGE)).astype(F32)
    dconv_ref[...] = (d_conv + d_single * vectors[base + 4 : base + 5]) * live_col
    grad_score = jnp.sum(conv * (d_single * own), axis=0, keepdims=True)
    masked = mask_ref[0].astype(F32)
    d_masked = jnp.zeros(masked.shape, F32)
    for j in range(4):
        moved = dconv_ref[EDGE + 2 - j : EDGE + 2 - j + extent, :]
        d_masked += vectors[base + j : base + j + 1] * moved
        sum_ref[vocab + j : vocab + j + 1, :] += jnp.sum(masked * moved, axis=0, keepdims=True)
    sum_ref[vocab + 4 : vocab + 5, :] += grad_score
    d_in = (d_masked * live_col[EDGE : frame - EDGE]).astype(BF16)
    din_ref[0] = d_in
    ids = ids_ref[0][:, EDGE : frame - EDGE]
    emb_rows = -(-vocab // 8) * 8
    onehot = (lax.broadcasted_iota(jnp.int32, (emb_rows, extent), 0) == ids).astype(F32).astype(BF16)
    sum_ref[0:emb_rows, :] += dot_nn(onehot, d_in)

    @pl.when(row == pl.num_programs(0) - 1)
    def _():
        sum_ref[vocab + 5 : vocab + 7, :] = gain_ref[0:2, :]
        parts, _, share = grad_ref.shape
        for d in range(parts):
            grad_ref[d] = sum_ref[:, d * share : (d + 1) * share].astype(BF16)


def front_backward(at, row_len, ids, pack, d_hid, rims, conv, masked, shares, gains, vocab):
    rows, _, frame = ids.shape
    extent = frame - 2 * EDGE
    tok, d_model = d_hid.shape[1:]
    pad = pack.shape[1]
    by_row = lambda r, *_: (r, 0, 0)
    return pl.pallas_call(
        functools.partial(front_back_kernel, vocab),
        grid_spec=pltpu.PrefetchScalarGridSpec(
            num_scalar_prefetch=2,
            grid=(rows,),
            in_specs=[
                pl.BlockSpec((1, 1, frame), by_row),
                pl.BlockSpec(pack.shape, lambda r, *_: (0, 0, 0)),
                pl.BlockSpec((1, tok, d_model), by_row),
                pl.BlockSpec((1, EDGE, d_model), by_row),
                pl.BlockSpec((1, frame, d_model), by_row),
                pl.BlockSpec((1, extent, d_model), by_row),
                pl.BlockSpec((1, 8, frame), by_row),
                pl.BlockSpec(gains.shape, lambda r, *_: (0, 0)),
            ],
            out_specs=[
                pl.BlockSpec((1, extent, d_model), by_row),
                pl.BlockSpec(pack.shape, lambda r, *_: (0, 0, 0)),
            ],
            scratch_shapes=[
                pltpu.VMEM((pad, d_model), BF16),
                pltpu.VMEM((frame, frame), BF16),
                pltpu.VMEM((frame, frame), BF16),
                pltpu.VMEM((frame, frame), BF16),
                pltpu.VMEM((frame, d_model), F32),
                pltpu.VMEM((pad, d_model), F32),
            ],
        ),
        out_shape=[
            jax.ShapeDtypeStruct((rows, extent, d_model), BF16),
            jax.ShapeDtypeStruct(pack.shape, BF16),
        ],
        compiler_params=pltpu.CompilerParams(vmem_limit_bytes=56 << 20),
        cost_estimate=pl.CostEstimate(flops=rows * 16 * frame * frame * d_model, bytes_accessed=rows * frame * d_model * 12, transcendentals=0),
        name="front_back",
    )(at, row_len, ids, pack, d_hid, rims, conv, masked, shares, gains)


GELU_C = 0.7978845608
GELU_A = 0.044715


def pack_down(x):
    rows, third = x.shape[1], x.shape[2] // 3
    left, mid, right = x[..., :third], x[..., third : 2 * third], x[..., 2 * third :]
    return jnp.concatenate(
        [jnp.concatenate([left, right[:, : rows // 2]], axis=1), jnp.concatenate([mid, right[:, rows // 2 :]], axis=1)], axis=2
    )


def unpack_down(x):
    rows, third = x.shape[1] * 2 // 3, x.shape[2] // 2
    right = jnp.concatenate([x[:, rows:, :third], x[:, rows:, third:]], axis=1)
    return jnp.concatenate([x[:, :rows, :third], x[:, :rows, third:], right], axis=2)


def feed_kernel(nblk, rows, row, sizes, *refs):
    share, ff_cols, width, down_rows = sizes
    x_refs, cot_refs, rest_ref = refs[:nblk], refs[nblk : 2 * nblk], refs[2 * nblk]
    refs = refs[2 * nblk + 1 :]
    sums_in, outs_in = None, ()
    if row > 0:
        outs_in, sums_in, refs = refs[:nblk], refs[nblk : nblk + 2], refs[nblk + 2 :]
    outs, dnorms, grads = refs[:nblk], refs[nblk : 2 * nblk], refs[2 * nblk :]
    if row == rows - 1:
        pack_ref, sum_a, sum_b = grads
    else:
        sum_a, sum_b = grads
    parts = rest_ref.shape[0]
    w_in = rest_ref[:, :share, : 2 * ff_cols].reshape(parts * share, 2 * ff_cols)
    w_down = unpack_down(rest_ref[:, :, 2 * ff_cols :]).reshape(parts * down_rows, width)
    for b in range(nblk):
        x, cot = x_refs[b][...], cot_refs[b][row]
        both = dot_nn(x, w_in)
        gate, up = both[:, :ff_cols], both[:, ff_cols:]
        square = gate * gate
        turned = jnp.tanh(GELU_C * gate * (1.0 + GELU_A * square))
        half = 0.5 * (1.0 + turned)
        gelu = gate * half
        slope = half + (0.5 * GELU_C) * gate * (1.0 - turned * turned) * (1.0 + (3.0 * GELU_A) * square)
        hidden = (gelu * up).astype(BF16)
        if row > 0:
            outs[b][:row] = outs_in[b][...]
        outs[b][row] = dot_nn(hidden, w_down).astype(BF16)
        d_hidden = dot_nt(cot, w_down)
        d_both = jnp.concatenate([(d_hidden * up * slope).astype(BF16), (d_hidden * gelu).astype(BF16)], axis=1)
        dnorms[b][...] = dot_nt(d_both, w_in).astype(BF16)
        grad_a, grad_b = dot_tn(x, d_both), dot_tn(hidden, cot)
        if b == 0 and sums_in is None:
            sum_a[...] = grad_a
            sum_b[...] = grad_b
        elif b == 0:
            sum_a[...] = sums_in[0][...] + grad_a
            sum_b[...] = sums_in[1][...] + grad_b
        else:
            sum_a[...] += grad_a
            sum_b[...] += grad_b
    if row == rows - 1:
        pack_ref[:, :, : 2 * ff_cols] = sum_a[...].astype(BF16).reshape(parts, share, 2 * ff_cols)
        pack_ref[:, :, 2 * ff_cols :] = pack_down(sum_b[...].astype(BF16).reshape(parts, down_rows, width))


def feed(xs, cots, rest, before, row, sizes):
    nblk = len(xs)
    tok, d_model = xs[0].shape
    share, ff_cols, width, down_rows = sizes
    parts, rows = rest.shape[0], cots[0].shape[0]
    sum_shapes = [(d_model, 2 * ff_cols), (parts * down_rows, width)]
    outs = [jax.ShapeDtypeStruct((row + 1, tok, width), BF16)] * nblk + [jax.ShapeDtypeStruct((tok, d_model), BF16)] * nblk
    scratch = []
    if row == rows - 1:
        outs.append(jax.ShapeDtypeStruct(rest.shape, BF16))
        scratch = [pltpu.VMEM(s, F32) for s in sum_shapes]
    else:
        outs += [jax.ShapeDtypeStruct(s, F32) for s in sum_shapes]
    args = [*xs, *cots, rest, *before]
    flops = 2 * nblk * tok * d_model * ff_cols * 9
    got = pl.pallas_call(
        functools.partial(feed_kernel, nblk, rows, row, sizes),
        in_specs=in_vmem(args),
        out_specs=in_vmem(outs),
        out_shape=outs,
        scratch_shapes=scratch,
        compiler_params=pltpu.CompilerParams(vmem_limit_bytes=56 << 20),
        cost_estimate=pl.CostEstimate(flops=flops, bytes_accessed=12 << 20, transcendentals=nblk * tok * ff_cols),
        name="feed",
    )(*args)
    return got[:nblk], got[nblk : 2 * nblk], got[2 * nblk :]


P = jax.sharding.PartitionSpec


def rims_of(x, width):
    size, length = lax.axis_size("seq"), x.shape[1]
    up = [(i, i + 1) for i in range(size - 1)]
    down = [(j, i) for i, j in up]
    before = lax.ppermute(x[:, length - width :], "seq", up)
    after = lax.ppermute(x[:, :width], "seq", down)
    return before, after


def flip_with(x, axis, bit):
    return lax.ppermute(x, axis, [(i, i ^ bit) for i in range(lax.axis_size(axis))])


def bits_of(axis):
    bits, bit = [], 1
    while bit < lax.axis_size(axis):
        bits.append(bit)
        bit *= 2
    return bits[::-1]


def after(x, *others):
    return lax.optimization_barrier((x,) + others)[0]


def places_of(n):
    places = [0]
    bit = n // 2
    while bit:
        places = places + [p ^ bit for p in places]
        bit //= 2
    return places


def swap_blocks(parts):
    return [part if bit == 0 else flip_with(part, "seq", bit) for part, bit in zip(parts, places_of(len(parts)))]


def gather_direct(x):
    return swap_blocks([x] * lax.axis_size("seq"))


def gather_first(x):
    blocks = [x]
    for bit in bits_of("seq")[:-1]:
        blocks = blocks + [flip_with(block, "seq", bit) for block in blocks]
    return blocks


def gather_last(blocks):
    return blocks + [flip_with(block, "seq", 1) for block in blocks]


def gather_two(x):
    return gather_last(gather_first(x))


def scatter_first(parts):
    half = len(parts) // 2
    got = [flip_with(part, "seq", 1) for part in parts[half:]]
    send = [(a.astype(F32) + b.astype(F32)).astype(BF16) for a, b in zip(parts[1:half], got[1:])]
    return [parts[0], got[0]], send


def scatter_last(own, send):
    return own + [flip_with(part, "seq", place) for part, place in zip(send, places_of(2 * len(send) + 2)[1:])]


def add_up(parts):
    return functools.reduce(jnp.add, [part.astype(F32) for part in parts])


def swap_dp(x):
    return lax.all_to_all(x, "dp", split_axis=0, concat_axis=0, tiled=True)


def sum_parts(x):
    return jnp.sum(x.astype(F32), axis=0)


def gather_step(x, bit):
    axis = bits_of("dp").index(bit)
    other = flip_with(x, "dp", bit)
    upper = (lax.axis_index("dp") & bit) != 0
    return jnp.concatenate([jnp.where(upper, other, x), jnp.where(upper, x, other)], axis=axis)


def gather_start(x):
    return x.reshape((1,) * len(bits_of("dp")) + x.shape)


def sum_seq(x):
    for bit in bits_of("seq")[::-1]:
        x = x + flip_with(x.astype(BF16), "seq", bit).astype(F32)
    return x


def in_order(blocks, me):
    n = len(blocks)
    bits = bits_of("seq")
    x = jnp.stack(blocks).reshape((2,) * len(bits) + blocks[0].shape)
    for at, bit in enumerate(bits[::-1]):
        upper = (me & bit) != 0
        x = jnp.where(upper, jnp.flip(x, at), x)
    x = x.transpose(tuple(range(len(bits)))[::-1] + tuple(range(len(bits), x.ndim)))
    return x.reshape((n,) + blocks[0].shape)


def on_device(
    byte_ids,
    lengths,
    deal_order,
    buckets,
    embedding,
    conv_w,
    score_w,
    gain_one,
    w_query,
    w_key,
    w_value,
    w_out,
    rel_bias,
    gain_two,
    w_gate,
    w_up,
    w_down,
    cotangent,
):
    n = lax.axis_size("seq")
    dp = lax.axis_size("dp")
    me = lax.axis_index("seq")
    rows_dev, extent = byte_ids.shape
    share, width = w_query.shape
    d_model = share * dp
    head_cols = width // n
    heads_dev = head_cols // DH
    ff_cols = w_gate.shape[1] // n
    down_rows = w_down.shape[0] // n
    tok = cotangent.shape[1]
    place = jnp.array(places_of(n), jnp.int32) ^ me

    vocab = embedding.shape[0]
    pad_vocab = -(-(vocab + 7) // 16) * 16
    front_pack = jnp.concatenate(
        [embedding, conv_w, score_w[None], gain_one[None], gain_two[None], jnp.zeros((pad_vocab - vocab - 7, share), BF16)], axis=0
    )

    def own_cols(weight):
        return lax.dynamic_slice_in_dim(weight, me * head_cols, head_cols, 1)

    qkv_pack = jnp.concatenate([own_cols(w_query), own_cols(w_key), own_cols(w_value), own_cols(w_out)], axis=1)
    front_all, qkv_w = gather_start(front_pack), gather_start(qkv_pack)
    up_bits = bits_of("dp")
    qkv_bits = up_bits[-1:] + up_bits[:-1]
    for at, bit in enumerate(up_bits):
        front_all = gather_step(front_all, bit)
        if at < len(up_bits) - 1:
            qkv_w = after(gather_step(qkv_w, qkv_bits[at]), front_all)
    front_all = front_all.reshape((dp,) + front_pack.shape)
    gain_first = front_all[:, vocab + 5].reshape(1, d_model).astype(F32)
    gain_second = front_all[:, vocab + 6].reshape(1, d_model).astype(F32)

    def own_ff(weight):
        return lax.dynamic_index_in_dim(weight.reshape(share, dp, n, down_rows), me, 2, keepdims=False).reshape(
            share, ff_cols
        )

    down_own = lax.dynamic_slice_in_dim(w_down, me * down_rows, down_rows, 0)
    rest_pack = jnp.concatenate([own_ff(w_gate), own_ff(w_up), pack_down(down_own[None])[0]], axis=1)
    rest_all = lax.all_gather(after(rest_pack, front_all), "dp", axis=0, tiled=False)

    offset = me * extent
    matches = deal_order[:, None] == jnp.arange(lengths.shape[0], dtype=jnp.int32)[None, :]
    row_len = jnp.sum(jnp.where(matches, lengths[None, :], 0), axis=1)
    rim_low, rim_high = rims_of(byte_ids, EDGE)
    ids = jnp.concatenate([rim_low, byte_ids, rim_high], axis=1)[:, None, :]
    at = jnp.full((1,), offset, jnp.int32)
    row_ids = range(rows_dev)
    lens = [row_len[r : r + 1] for r in row_ids]

    first_head = me * heads_dev
    bias_loc = lax.dynamic_slice_in_dim(rel_bias, first_head, heads_dev, 1)
    offsets = jnp.concatenate([jnp.full((1,), -1, jnp.int32), buckets[::-1]])
    onehot = (offsets[None, :] == jnp.arange(rel_bias.shape[0], dtype=jnp.int32)[:, None]).astype(BF16)
    strips = bias_strips(jnp.einsum("nh,nx->hx", bias_loc, onehot, preferred_element_type=F32), n)

    cots = gather_two(cotangent)
    normed, h_zero, kept = [], [], []
    gate = (strips,)
    for r in row_ids:
        h, low, *rest = front_forward(at, lens[r], after(ids[r : r + 1], *gate), front_all, vocab, d_model)
        if r == 0:
            qkv_w = gather_step(after(qkv_w, low), qkv_bits[-1])
        gate = (low,)
        h_zero.append(h[0])
        normed.append(low[0])
        kept.append(rest)
    low_one = [gather_two(low) if r == 0 else gather_direct(low) for r, low in enumerate(normed)]
    qkv_w = qkv_w.reshape(d_model, 4 * head_cols)
    out_blocks = gather_first(qkv_w[:, 3 * head_cols :])
    qkv_w = qkv_w[:, : 3 * head_cols]
    gate = gate + tuple(cots)
    atts, qkvs, logs, mixed = [], [], [], []
    for r in row_ids:
        xs = [after(low_one[r][0], *gate)] + list(low_one[r][1:])
        att, qkv, log = attend(place, lens[r], xs, qkv_w, strips)
        gate = (qkv,)
        atts.append(att)
        qkvs.append(qkv)
        logs.append(log)
        mixed.append(swap_blocks(att))
        if r == 0:
            out_blocks = gather_last([after(block, *gate) for block in out_blocks])
    w_out_all, h_one, lows = project(place, out_blocks, [[after(m[0], *gate)] + m[1:] for m in mixed], h_zero, gain_second)
    low_two = [gather_two(low) if r == 0 else gather_direct(low) for r, low in enumerate(lows)]
    sizes = (share, ff_cols, width, down_rows)
    d_norm_two, before = [], ()
    for r in row_ids:
        xs = [after(low_two[r][0], *gate)] + low_two[r][1:]
        ff_outs, d_norm, sums = feed(xs, cots, rest_all, before, r, sizes)
        before = (*ff_outs, *sums)
        gate = (d_norm[0],)
        d_norm_two.append(swap_blocks(d_norm) if r < rows_dev - 1 else scatter_last(*scatter_first(d_norm)))
    ff_sum = lax.psum_scatter(sums[0], "dp", scatter_dimension=0, tiled=False)
    d_h_one, gains_two, d_mixed, out_grad = [], [], [], None
    for r in row_ids:
        adds = [after(d_norm_two[r][0], *gate)] + d_norm_two[r][1:]
        d_h, gain_grad, d_att, out_grad = project_back(
            place, adds, mixed[r], w_out_all, h_one[r], cotangent, r, gain_second, out_grad, dp if r == rows_dev - 1 else 0
        )
        gate = (d_h,)
        d_h_one.append(d_h)
        gains_two.append(gain_grad)
        d_mixed.append(swap_blocks(d_att))
    ff_own, ff_send = scatter_first([after(ff_out, *gate) for ff_out in ff_outs])
    out_parts = swap_dp(out_grad)
    d_norms, qkv_grad, d_revs = [], None, []
    for r in row_ids:
        douts = [after(d_mixed[r][0], *gate)] + d_mixed[r][1:]
        d_norm, qkv_grad, d_rev = attend_back(
            place, lens[r], low_one[r], qkv_w, qkvs[r], atts[r], douts, logs[r], strips, qkv_grad, dp if r == rows_dev - 1 else 0
        )
        gate = (d_norm[0],)
        d_norms.append(d_norm)
        d_revs.append(d_rev)
        if r == 0:
            ff_send = [after(part, *gate) for part in ff_send]
            gate = gate + tuple(ff_send)
            ff_whole = scatter_last(ff_own, ff_send)
    output = (jnp.stack(h_one) + add_up([after(part, *gate) for part in ff_whole])).astype(BF16)
    qkv_parts = swap_dp(qkv_grad)
    d_rel_loc = jnp.einsum("nx,hx->nh", onehot.astype(F32), sum(d_revs), precision=lax.Precision.HIGHEST)
    d_rel = lax.dynamic_update_slice_in_dim(jnp.zeros(rel_bias.shape, F32), d_rel_loc, first_head, 1)
    rel_steps = [("seq", bit) for bit in bits_of("seq")[::-1]] + [("dp", bit) for bit in bits_of("dp")[::-1]]

    d_first = [swap_blocks(d_norm) for d_norm in d_norms[:-1]]
    last_own, last_send = scatter_first(d_norms[-1])
    d_first.append(scatter_last(last_own, last_send))
    g_out = sum_parts(out_parts)
    d_inputs, front_grads = [], []
    for r in row_ids:
        adds = [after(d_first[r][0], *gate)] + d_first[r][1:]
        d_h_zero, low_rim, high_rim, gain_grad = first_back(adds, h_zero[r], d_h_one[r], gain_first)
        size = lax.axis_size("seq")
        low_side = lax.ppermute(high_rim, "seq", [(i, i + 1) for i in range(size - 1)])[EDGE // 2 :]
        high_side = lax.ppermute(low_rim, "seq", [(i + 1, i) for i in range(size - 1)])[: EDGE // 2]
        rims = jnp.concatenate([low_side, high_side], axis=0)[None]
        d_rel = d_rel + flip_with(d_rel, *rel_steps.pop(0))
        if r == 0:
            rims = after(rims, d_rel, *last_send, g_out, ff_sum)
        conv_out, masked, shares = kept[r]
        d_in, front_grad = front_backward(
            at, lens[r], ids[r : r + 1], front_all, d_h_zero[None], rims, conv_out, masked, shares,
            jnp.concatenate([gain_grad, gains_two[r]], axis=0), vocab,
        )
        gate = (front_grad,)
        d_rel = after(d_rel, d_in)
        d_inputs.append(d_in[0])
        front_grads.append(front_grad)
    d_input = jnp.stack(d_inputs)
    front_parts = swap_dp(add_up(front_grads).astype(BF16))

    def every(x):
        return in_order(gather_two(x.astype(BF16)), me)

    ff_all = every(after(ff_sum, d_inputs[0]))
    g_gu = ff_all[:, :, : 2 * ff_cols].reshape(n, share, 2, dp, down_rows)
    g_gu = g_gu.transpose(2, 1, 3, 0, 4).reshape(2, share, n * ff_cols).astype(F32)
    g_down = unpack_down(ff_all[:, :, 2 * ff_cols :]).reshape(n * down_rows, width).astype(F32)
    while rel_steps:
        d_rel = d_rel + flip_with(d_rel, *rel_steps.pop(0))
    g_qkv = every(sum_parts(after(qkv_parts, *gate)).reshape(share, 3, head_cols))
    g_qkv = g_qkv.transpose(2, 1, 0, 3).reshape(3, share, width).astype(F32)
    g_out = sum_seq(after(g_out, *gate))
    front_sum = sum_seq(sum_parts(front_parts))
    return (
        output,
        d_input,
        front_sum[:vocab],
        front_sum[vocab : vocab + 4],
        front_sum[vocab + 4],
        front_sum[vocab + 5],
        g_qkv[0],
        g_qkv[1],
        g_qkv[2],
        g_out,
        d_rel,
        front_sum[vocab + 6],
        g_gu[0],
        g_gu[1],
        g_down,
    )


def solution(mesh):
    return jax.shard_map(
        on_device,
        mesh=mesh,
        in_specs=(
            P("dp", "seq"),
            P(),
            P("dp"),
            P(),
            P(None, "dp"),
            P(None, "dp"),
            P("dp"),
            P("dp"),
            P("dp", None),
            P("dp", None),
            P("dp", None),
            P("dp", None),
            P(),
            P("dp"),
            P("dp", None),
            P("dp", None),
            P("dp", None),
            P("dp", "seq", None),
        ),
        out_specs=(
            P("dp", "seq", None),
            P("dp", "seq", None),
            P(None, "dp"),
            P(None, "dp"),
            P("dp"),
            P("dp"),
            P("dp", None),
            P("dp", None),
            P("dp", None),
            P("dp", None),
            P(),
            P("dp"),
            P("dp", None),
            P("dp", None),
            P("dp", None),
        ),
        check_vma=False,
    )
```

```python
import functools
import jax, jax.numpy as jnp
from jax import lax
from jax.experimental import pallas as pl
from jax.experimental.pallas import tpu as pltpu
DH=64
NEG=-1e9
F32, BF16 = jnp.float32, jnp.bfloat16


def dot_nt(a, b):
    return lax.dot_general(a, b, (((1,), (1,)), ((), ())), preferred_element_type=F32)


def dot_nn(a, b):
    return lax.dot_general(a, b, (((1,), (0,)), ((), ())), preferred_element_type=F32)


def tile_at(place_ref, kb, qb, nblk):
    return jnp.clip(place_ref[kb] - place_ref[qb], -2, 2) + 2


def strip_kernel(nblk, rev_ref, strip_ref):
    heads, _, blk = strip_ref.shape
    for head in range(heads):
        for part in range(5):
            low = (nblk + 1 - part) * blk
            here = slice(part * blk, (part + 1) * blk)
            if part in (0, 4):
                strip_ref[head, here, :] = jnp.broadcast_to(rev_ref[head : head + 1, low + blk : low + blk + 1], (blk, blk))
                continue
            segment = jnp.broadcast_to(rev_ref[head : head + 1, low : low + 2 * blk], (blk, 2 * blk))
            strip_ref[head, here, :] = pltpu.roll(segment, 0, 1, stride=1, stride_axis=0)[:, blk:]


def bias_strips(rev, nblk):
    heads, width = rev.shape
    blk = width // (2 * nblk)
    return pl.pallas_call(
        functools.partial(strip_kernel, nblk),
        out_shape=jax.ShapeDtypeStruct((heads, 5 * blk, blk), F32),
        compiler_params=pltpu.CompilerParams(vmem_limit_bytes=32 << 20),
        name="strips",
    )(rev)


def key_side(key, ok_col):
    rows = key.shape[0]
    lane = lax.broadcasted_iota(jnp.int32, (rows, DH), 1)
    extra = jnp.where(lane == 0, ok_col, 0.0).astype(BF16)
    return jnp.concatenate([key, extra], axis=1)


def query_side(query):
    rows = query.shape[0]
    lane = lax.broadcasted_iota(jnp.int32, (rows, DH), 1)
    return jnp.concatenate([query, jnp.where(lane == 0, 1.0, 0.0).astype(BF16)], axis=1)


def mask_column(place_ref, limit, blk, nblk):
    cols = []
    for b in range(nblk):
        at = place_ref[b] * blk + lax.broadcasted_iota(jnp.int32, (blk, DH), 0)
        cols.append(jnp.where(2 * at < limit, 0.0, NEG))
    return jnp.concatenate(cols, axis=0)


def dot_tn(a, b):
    return lax.dot_general(a, b, (((0,), (0,)), ((), ())), preferred_element_type=F32)


def whole(arg):
    return pl.BlockSpec(arg.shape, lambda *_: (0,) * len(arg.shape), pipeline_mode=pl.Buffered(1))


def in_vmem(args):
    return [whole(arg) for arg in args]


def scalars():
    return pl.BlockSpec(memory_space=pltpu.SMEM)


def attend_kernel(heads, nblk, place_ref, len_ref, *refs):
    xs, (w_ref, strip_ref), refs = refs[:nblk], refs[nblk : nblk + 2], refs[nblk + 2 :]
    outs, (qkv_ref, log_ref, att_ref, kaug_ref, qaug_ref, vt_ref) = refs[:nblk], refs[nblk:]
    blk = xs[0].shape[0]
    for b in range(nblk):
        qkv_ref[b * blk : (b + 1) * blk, :] = dot_nn(xs[b][...], w_ref[...]).astype(BF16)
    ok_col = mask_column(place_ref, len_ref[0], blk, nblk)
    width = heads * DH
    for head in range(heads):
        at = head * DH
        qaug_ref[...] = query_side(qkv_ref[:, at : at + DH])
        kaug_ref[...] = key_side(qkv_ref[:, width + at : width + at + DH], ok_col)
        vt_ref[...] = qkv_ref[:, 2 * width + at : 2 * width + at + DH].T

        def one_block(qb, carry):
            q_at = pl.multiple_of(qb * blk, blk)
            query = qaug_ref[pl.ds(q_at, blk), :]
            parts = []
            for kb in range(nblk):
                m_at = pl.multiple_of(tile_at(place_ref, kb, qb, nblk) * blk, blk)
                parts.append(dot_nt(kaug_ref[kb * blk : (kb + 1) * blk, :], query) + strip_ref[head, pl.ds(m_at, blk), :])
            top = functools.reduce(jnp.maximum, [jnp.max(p, axis=0, keepdims=True) for p in parts])
            total = jnp.zeros((1, blk), F32)
            acc = jnp.zeros((DH, blk), F32)
            for kb in range(nblk):
                weight = jnp.exp(parts[kb] - top)
                total += jnp.sum(weight, axis=0, keepdims=True)
                acc += dot_nn(vt_ref[:, kb * blk : (kb + 1) * blk], weight.astype(BF16))
            att_ref[pl.ds(q_at, blk), at : at + DH] = (acc / total).T.astype(BF16)
            log_ref[head, pl.ds(qb, 1), :] = top + jnp.log(total)
            return carry

        lax.fori_loop(0, nblk, one_block, 0, unroll=2)
    for b in range(nblk):
        outs[b][...] = att_ref[b * blk : (b + 1) * blk, :]


def attend(place, row_len, xs, w_qkv, strips):
    nblk = len(xs)
    blk = xs[0].shape[0]
    heads = strips.shape[0]
    tokens = nblk * blk
    outs = [jax.ShapeDtypeStruct((blk, heads * DH), BF16)] * nblk + [
        jax.ShapeDtypeStruct((tokens, 3 * heads * DH), BF16),
        jax.ShapeDtypeStruct((heads, nblk, blk), F32),
    ]
    args = [*xs, w_qkv, strips]
    got = pl.pallas_call(
        functools.partial(attend_kernel, heads, nblk),
        grid=(1,),
        in_specs=[scalars(), scalars(), *in_vmem(args)],
        out_specs=in_vmem(outs),
        out_shape=outs,
        scratch_shapes=[
            pltpu.VMEM((tokens, heads * DH), BF16),
            pltpu.VMEM((tokens, 2 * DH), BF16),
            pltpu.VMEM((tokens, 2 * DH), BF16),
            pltpu.VMEM((DH, tokens), BF16),
        ],
        compiler_params=pltpu.CompilerParams(vmem_limit_bytes=48 << 20),
        cost_estimate=pl.CostEstimate(flops=48 * heads * tokens * tokens * DH, bytes_accessed=8 << 20, transcendentals=heads * tokens * tokens),
        name="attend",
    )(place, row_len, *args)
    return got[:nblk], got[nblk], got[nblk + 1]


def attend_back_kernel(heads, nblk, first, final, place_ref, len_ref, *refs):
    xs, (w_ref, qkv_ref), refs = refs[:nblk], refs[nblk : nblk + 2], refs[nblk + 2 :]
    os, dos, (log_ref, strip_ref), refs = refs[:nblk], refs[nblk : 2 * nblk], refs[2 * nblk : 2 * nblk + 2], refs[2 * nblk + 2 :]
    sum_in = None
    if not first:
        sum_in, refs = refs[0], refs[1:]
    dns, (sum_ref, drev_ref), refs = refs[:nblk], refs[nblk : nblk + 2], refs[nblk + 2 :]
    grads_ref, kaug_ref, qaug_ref, kt_ref, dk_ref, dv_ref, o_ref, do_ref, dqkv_ref = refs
    blk = xs[0].shape[0]
    for b in range(nblk):
        o_ref[b * blk : (b + 1) * blk, :] = os[b][...]
        do_ref[b * blk : (b + 1) * blk, :] = dos[b][...]
    ok_col = mask_column(place_ref, len_ref[0], blk, nblk)
    width = heads * DH
    for head in range(heads):
        grads_ref[head] = jnp.zeros(grads_ref.shape[1:], F32)
        at = head * DH
        qaug_ref[...] = query_side(qkv_ref[:, at : at + DH])
        key = qkv_ref[:, width + at : width + at + DH]
        kaug_ref[...] = key_side(key, ok_col)
        kt_ref[...] = key.T
        dk_ref[...] = jnp.zeros_like(dk_ref)
        dv_ref[...] = jnp.zeros_like(dv_ref)

        def one_block(qb, carry):
            q_at = pl.multiple_of(qb * blk, blk)
            query = qaug_ref[pl.ds(q_at, blk), :]
            dout = do_ref[pl.ds(q_at, blk), at : at + DH]
            prod = dout.astype(F32) * o_ref[pl.ds(q_at, blk), at : at + DH].astype(F32)
            inner = jnp.sum(prod.T, axis=0, keepdims=True)
            log_row = log_ref[head, pl.ds(qb, 1), :]
            dqt = jnp.zeros((DH, blk), F32)
            for kb in range(nblk):
                here = slice(kb * blk, (kb + 1) * blk)
                m_at = pl.multiple_of(tile_at(place_ref, kb, qb, nblk) * blk, blk)
                score = dot_nt(kaug_ref[here, :], query) + strip_ref[head, pl.ds(m_at, blk), :]
                prob = jnp.exp(score - log_row)
                d_prob = dot_nt(qkv_ref[here, 2 * width + at : 2 * width + at + DH], dout)
                d_score = prob * (d_prob - inner)
                low = d_score.astype(BF16)
                grads_ref[head, pl.ds(m_at, blk), :] += d_score
                dv_ref[here, :] += dot_nn(prob.astype(BF16), dout)
                dk_ref[here, :] += dot_nn(low, query[:, :DH])
                dqt += dot_nn(kt_ref[:, here], low)
            dqkv_ref[pl.ds(q_at, blk), at : at + DH] = dqt.T.astype(BF16)
            return carry

        [one_block(qb, 0) for qb in range(nblk)]
        dqkv_ref[:, width + at : width + at + DH] = dk_ref[...].astype(BF16)
        dqkv_ref[:, 2 * width + at : 2 * width + at + DH] = dv_ref[...].astype(BF16)

    total = None
    for b in range(nblk):
        here = dqkv_ref[b * blk : (b + 1) * blk, :]
        dns[b][...] = dot_nt(here, w_ref[...]).astype(BF16)
        grad = dot_tn(xs[b][...], here)
        total = grad if total is None else total + grad
    if not first:
        total += sum_in[...]
    sum_ref[...] = total.astype(BF16).reshape(sum_ref.shape) if final else total

    flip = (
        lax.broadcasted_iota(jnp.int32, (blk, blk), 0) + lax.broadcasted_iota(jnp.int32, (blk, blk), 1) == blk - 1
    ).astype(F32).astype(BF16)
    drev_ref[...] = jnp.zeros_like(drev_ref)
    for head in range(heads):
        for part in range(5):
            low = (nblk + 1 - part) * blk
            grad = grads_ref[head, part * blk : (part + 1) * blk, :]
            if part in (0, 4):
                whole = jnp.sum(jnp.sum(grad, axis=0, keepdims=True), axis=1, keepdims=True)
                drev_ref[head : head + 1, low + blk : low + blk + 1] += whole
                continue
            high = grad.astype(BF16)
            rest = (grad - high.astype(F32)).astype(BF16)
            turned = dot_nn(flip, high) + dot_nn(flip, rest)
            wide = jnp.concatenate([jnp.zeros((blk, blk), F32), turned], axis=1)
            moved = pltpu.roll(wide, blk + 1, 1, stride=1, stride_axis=0)
            drev_ref[head : head + 1, low : low + 2 * blk] += jnp.sum(moved, axis=0, keepdims=True)


def attend_back(place, row_len, xs, w_qkv, qkv, outs, douts, logs, strips, sum_in, parts):
    nblk = len(xs)
    blk, d_model = xs[0].shape
    heads = strips.shape[0]
    tokens = nblk * blk
    cols = 3 * heads * DH
    args = [*xs, w_qkv, qkv, *outs, *douts, logs, strips] + ([] if sum_in is None else [sum_in])
    sum_shape = jax.ShapeDtypeStruct((parts, d_model // parts, cols), BF16) if parts else jax.ShapeDtypeStruct((d_model, cols), F32)
    shapes = [jax.ShapeDtypeStruct((blk, d_model), BF16)] * nblk + [sum_shape, jax.ShapeDtypeStruct((heads, 2 * tokens), F32)]
    got = pl.pallas_call(
        functools.partial(attend_back_kernel, heads, nblk, sum_in is None, bool(parts)),
        grid=(1,),
        in_specs=[scalars(), scalars(), *in_vmem(args)],
        out_specs=in_vmem(shapes),
        out_shape=shapes,
        scratch_shapes=[
            pltpu.VMEM((heads, 5 * blk, blk), F32),
            pltpu.VMEM((tokens, 2 * DH), BF16),
            pltpu.VMEM((tokens, 2 * DH), BF16),
            pltpu.VMEM((DH, tokens), BF16),
            pltpu.VMEM((tokens, DH), F32),
            pltpu.VMEM((tokens, DH), F32),
            pltpu.VMEM((tokens, heads * DH), BF16),
            pltpu.VMEM((tokens, heads * DH), BF16),
            pltpu.VMEM((tokens, cols), BF16),
        ],
        compiler_params=pltpu.CompilerParams(vmem_limit_bytes=56 << 20),
        cost_estimate=pl.CostEstimate(flops=120 * heads * tokens * tokens * DH, bytes_accessed=16 << 20, transcendentals=heads * tokens * tokens),
        name="attend_back",
    )(place, row_len, *args)
    return got[:nblk], got[nblk], got[nblk + 1]


EPS = 1e-06


def project_kernel(nblk, rows, place_ref, *refs):
    cols_refs, refs = refs[:nblk], refs[nblk:]
    atts, refs = refs[: rows * nblk], refs[rows * nblk :]
    hids, gain_ref, w_ref, outs = refs[:rows], refs[rows], refs[rows + 1], refs[rows + 2 :]
    cols = cols_refs[0].shape[1]
    for b in range(nblk):
        for g in range(nblk):

            @pl.when(place_ref[b] == g)
            def _():
                w_ref[:, g * cols : (g + 1) * cols] = cols_refs[b][...]

    for r in range(rows):
        hid = hids[r][...]
        for b in range(nblk):
            here = pl.ds(pl.multiple_of(place_ref[b] * cols, 16), cols)
            hid += dot_nn(atts[r * nblk + b][...], w_ref[here, :])
        outs[2 * r][...] = hid
        factor = lax.rsqrt(jnp.mean(hid * hid, axis=-1, keepdims=True) + EPS)
        outs[2 * r + 1][...] = (hid * factor * gain_ref[...]).astype(BF16)


def project(place, w_blocks, atts, hids, gain):
    rows, nblk = len(atts), len(w_blocks)
    width = w_blocks[0].shape[0]
    args = [*w_blocks, *[block for row in atts for block in row], *hids, gain]
    outs = [jax.ShapeDtypeStruct((width, hids[0].shape[1]), BF16)]
    for hid in hids:
        outs += [jax.ShapeDtypeStruct(hid.shape, F32), jax.ShapeDtypeStruct(hid.shape, BF16)]
    got = pl.pallas_call(
        functools.partial(project_kernel, nblk, rows),
        grid=(1,),
        in_specs=[scalars(), *in_vmem(args)],
        out_specs=in_vmem(outs),
        out_shape=outs,
        compiler_params=pltpu.CompilerParams(vmem_limit_bytes=60 << 20),
        cost_estimate=pl.CostEstimate(flops=4 * rows * hids[0].shape[0] * width * width, bytes_accessed=3 << 20, transcendentals=0),
        name="project",
    )(place, *args)
    return got[0], got[1::2], got[2::2]


def norm_back(hid, gain, d_norm):
    factor = lax.rsqrt(jnp.mean(hid * hid, axis=-1, keepdims=True) + EPS)
    scaled = hid * factor
    weighted = d_norm * gain
    inner = jnp.mean(scaled * weighted, axis=-1, keepdims=True)
    return factor * (weighted - scaled * inner), jnp.sum(d_norm * scaled, axis=0, keepdims=True)


def project_back_kernel(nblk, pieces, row, first, final, place_ref, *refs):
    adds, atts, refs = refs[:pieces], refs[pieces : pieces + nblk], refs[pieces + nblk :]
    (w_ref, hid_ref, cot_ref, gain_ref), refs = refs[:4], refs[4:]
    sum_in = None
    if not first:
        sum_in, refs = refs[0], refs[1:]
    dhid_ref, gain_out, datts, sum_ref, acc_ref = refs[0], refs[1], refs[2 : 2 + nblk], refs[2 + nblk], refs[3 + nblk]
    d_norm = adds[0][...].astype(F32)
    for add in adds[1:]:
        d_norm += add[...].astype(F32)
    back, gain_grad = norm_back(hid_ref[...], gain_ref[...], d_norm)
    gain_out[...] = gain_grad
    d_hid = cot_ref[row].astype(F32) + back
    dhid_ref[...] = d_hid
    branch = d_hid.astype(BF16)
    cols = atts[0].shape[1]
    for b in range(nblk):
        here = pl.ds(pl.multiple_of(place_ref[b] * cols, 16), cols)
        datts[b][...] = dot_nt(branch, w_ref[here, :]).astype(BF16)
        grad = dot_tn(atts[b][...], branch)
        acc_ref[here, :] = grad if first else sum_in[here, :] + grad
    if final:
        sum_ref[...] = acc_ref[...].astype(BF16).reshape(sum_ref.shape)
    else:
        sum_ref[...] = acc_ref[...]


def project_back(place, adds, atts, w_out, hid, cot, row, gain, sum_in, parts):
    nblk = len(atts)
    blk, cols = atts[0].shape
    width, d_model = w_out.shape
    args = [*adds, *atts, w_out, hid, cot, gain] + ([] if sum_in is None else [sum_in])
    sum_shape = jax.ShapeDtypeStruct((parts, width // parts, d_model), BF16) if parts else jax.ShapeDtypeStruct((width, d_model), F32)
    outs = [jax.ShapeDtypeStruct(hid.shape, F32), jax.ShapeDtypeStruct((1, d_model), F32)]
    outs += [jax.ShapeDtypeStruct((blk, cols), BF16)] * nblk + [sum_shape]
    got = pl.pallas_call(
        functools.partial(project_back_kernel, nblk, len(adds), row, sum_in is None, bool(parts)),
        grid=(1,),
        in_specs=[scalars(), *in_vmem(args)],
        out_specs=in_vmem(outs),
        out_shape=outs,
        scratch_shapes=[pltpu.VMEM((width, d_model), F32)],
        compiler_params=pltpu.CompilerParams(vmem_limit_bytes=60 << 20),
        cost_estimate=pl.CostEstimate(flops=8 * blk * width * d_model, bytes_accessed=6 << 20, transcendentals=0),
        name="project_back",
    )(place, *args)
    return got[0], got[1], got[2 : 2 + nblk], got[2 + nblk]


def first_back_kernel(pieces, *refs):
    adds, (hid_ref, dhid_ref, gain_ref, out_ref, low_ref, high_ref, gain_out) = refs[:pieces], refs[pieces:]
    d_norm = adds[0][...].astype(F32)
    for add in adds[1:]:
        d_norm += add[...].astype(F32)
    back, gain_grad = norm_back(hid_ref[...], gain_ref[...], d_norm)
    gain_out[...] = gain_grad
    d_hid = dhid_ref[...] + back
    out_ref[...] = d_hid
    low_ref[...] = d_hid[:8]
    high_ref[...] = d_hid[-8:]


def first_back(adds, hid, d_hid, gain):
    args = [*adds, hid, d_hid, gain]
    d_model = hid.shape[1]
    outs = [jax.ShapeDtypeStruct(s, F32) for s in (hid.shape, (8, d_model), (8, d_model), (1, d_model))]
    return pl.pallas_call(
        functools.partial(first_back_kernel, len(adds)),
        grid=(1,),
        in_specs=in_vmem(args),
        out_specs=in_vmem(outs),
        out_shape=outs,
        compiler_params=pltpu.CompilerParams(vmem_limit_bytes=32 << 20),
        cost_estimate=pl.CostEstimate(flops=20 * hid.shape[0] * d_model, bytes_accessed=4 << 20, transcendentals=0),
        name="first_back",
    )(*args)


EDGE = 8


def split_two(x):
    high = x.astype(BF16)
    return high, (x - high.astype(F32)).astype(BF16)


def dot_fine(dot, a, b):
    a_high, a_rest = split_two(a)
    b_high, b_rest = split_two(b)
    return dot(a_high, b_high) + (dot(a_high, b_rest) + dot(a_rest, b_high))


def dot_half(dot, a, b_low):
    a_high, a_rest = split_two(a)
    return dot(a_high, b_low) + dot(a_rest, b_low)


def same_block(first, frame, size):
    def group(axis, shape):
        place = lax.broadcasted_iota(jnp.int32, shape, axis) + first
        return jnp.floor((place.astype(F32) + 0.5) * (1.0 / size))

    return (group(0, (frame, 1)) == group(1, (1, frame))).astype(F32)


def unpack_front(pack_ref, wall_ref):
    parts, _, share = pack_ref.shape
    for d in range(parts):
        wall_ref[:, d * share : (d + 1) * share] = pack_ref[d]


def front_kernel(vocab, at_ref, len_ref, ids_ref, pack_ref, hid_ref, norm_ref, conv_ref, mask_ref, share_ref, wall_ref, tri_ref, quad_ref, pair_ref, x_ref):
    row = pl.program_id(0)
    frame = ids_ref.shape[2]
    tok = hid_ref.shape[1]
    first = at_ref[0] - EDGE

    @pl.when(row == 0)
    def _():
        unpack_front(pack_ref, wall_ref)
        for ref, size in ((pair_ref, 2), (tri_ref, 3), (quad_ref, 4)):
            ref[...] = same_block(first + 12 * EDGE, frame, size).astype(BF16)

    limit = len_ref[row]
    pad = wall_ref.shape[0]
    place_row = lax.broadcasted_iota(jnp.int32, (1, frame), 1) + first
    live_row = (place_row >= 0) & (place_row < limit)
    ids = jnp.where(live_row, ids_ref[0], -1)
    onehot = (lax.broadcasted_iota(jnp.int32, (pad, frame), 0) == ids).astype(F32).astype(BF16)
    masked = lax.dot_general(onehot, wall_ref[...], (((0,), (0,)), ((), ())), preferred_element_type=F32)
    mask_ref[0] = masked[EDGE : frame - EDGE].astype(BF16)
    x_ref[0:EDGE, :] = jnp.zeros((EDGE, masked.shape[1]), F32)
    x_ref[EDGE : EDGE + frame, :] = masked
    x_ref[EDGE + frame :, :] = jnp.zeros((EDGE, masked.shape[1]), F32)
    low = vocab // 16 * 16
    vectors = wall_ref[low : -(-(vocab + 7) // 16) * 16, :].astype(F32)
    base = vocab - low
    place_col = lax.broadcasted_iota(jnp.int32, (frame, 1), 0) + first
    live_col = ((place_col >= 0) & (place_col < limit)).astype(F32)
    conv = vectors[base : base + 1] * x_ref[EDGE - 2 : EDGE - 2 + frame, :]
    for j in range(1, 4):
        conv += vectors[base + j : base + j + 1] * x_ref[EDGE - 2 + j : EDGE - 2 + j + frame, :]
    conv = conv * live_col
    conv_ref[0] = conv
    c_high, c_rest = split_two(conv)
    score_w = jnp.broadcast_to(vectors[base + 4 : base + 5], (8, conv.shape[1])).astype(BF16)
    single = (dot_nt(score_w, c_high) + dot_nt(score_w, c_rest))[0:1]
    s_high = single.astype(BF16).astype(F32)
    s_mid = (single - s_high).astype(BF16).astype(F32)
    stack = jnp.concatenate([s_high, s_mid, single - s_high - s_mid, jnp.zeros((5, frame), F32)], axis=0).astype(BF16)
    scores = [single]
    for ref, size in ((pair_ref, 2), (tri_ref, 3), (quad_ref, 4)):
        scores.append(jnp.sum(dot_nn(stack, ref[...]), axis=0, keepdims=True) * (1.0 / size))
    top = functools.reduce(jnp.maximum, scores)
    raw = [jnp.exp(s - top) for s in scores]
    total = raw[0] + raw[1] + raw[2] + raw[3]
    shares = jnp.concatenate([r / total for r in raw] + [jnp.zeros((4, frame), F32)], axis=0)
    share_ref[0] = shares
    cols = shares.T
    one = (lax.broadcasted_iota(jnp.int32, (frame, frame), 0) == lax.broadcasted_iota(jnp.int32, (frame, frame), 1))
    mix = jnp.where(one, cols[:, 0:1], 0.0)
    for at, (ref, size) in enumerate(((pair_ref, 2), (tri_ref, 3), (quad_ref, 4))):
        mix += ref[...].astype(F32) * (cols[:, at + 1 : at + 2] * (1.0 / size))
    start = 2 * lax.broadcasted_iota(jnp.int32, (tok, frame), 0) + EDGE
    here = lax.broadcasted_iota(jnp.int32, (tok, frame), 1)
    pool = jnp.where((here == start) | (here == start + 1), 0.5, 0.0).astype(BF16)
    m_high, m_rest = split_two(mix)
    weights = dot_nn(pool, m_high) + dot_nn(pool, m_rest)
    w_high, w_rest = split_two(weights)
    hid = dot_nn(w_high, c_high) + (dot_nn(w_high, c_rest) + dot_nn(w_rest, c_high))
    hid_ref[0] = hid
    factor = lax.rsqrt(jnp.mean(hid * hid, axis=-1, keepdims=True) + EPS)
    norm_ref[0] = (hid * factor * vectors[base + 5 : base + 6]).astype(BF16)


def front_forward(at, row_len, ids, pack, vocab, d_model):
    rows, _, frame = ids.shape
    extent = frame - 2 * EDGE
    tok = extent // 2
    pad = pack.shape[1]
    by_row = lambda r, *_: (r, 0, 0)
    return pl.pallas_call(
        functools.partial(front_kernel, vocab),
        grid_spec=pltpu.PrefetchScalarGridSpec(
            num_scalar_prefetch=2,
            grid=(rows,),
            in_specs=[
                pl.BlockSpec((1, 1, frame), by_row),
                pl.BlockSpec(pack.shape, lambda r, *_: (0, 0, 0)),
            ],
            out_specs=[
                pl.BlockSpec((1, tok, d_model), by_row),
                pl.BlockSpec((1, tok, d_model), by_row),
                pl.BlockSpec((1, frame, d_model), by_row),
                pl.BlockSpec((1, extent, d_model), by_row),
                pl.BlockSpec((1, 8, frame), by_row),
            ],
            scratch_shapes=[
                pltpu.VMEM((pad, d_model), BF16),
                pltpu.VMEM((frame, frame), BF16),
                pltpu.VMEM((frame, frame), BF16),
                pltpu.VMEM((frame, frame), BF16),
                pltpu.VMEM((frame + 2 * EDGE, d_model), F32),
            ],
        ),
        out_shape=[
            jax.ShapeDtypeStruct((rows, tok, d_model), F32),
            jax.ShapeDtypeStruct((rows, tok, d_model), BF16),
            jax.ShapeDtypeStruct((rows, frame, d_model), F32),
            jax.ShapeDtypeStruct((rows, extent, d_model), BF16),
            jax.ShapeDtypeStruct((rows, 8, frame), F32),
        ],
        compiler_params=pltpu.CompilerParams(vmem_limit_bytes=48 << 20),
        cost_estimate=pl.CostEstimate(flops=rows * 8 * frame * frame * d_model, bytes_accessed=rows * frame * d_model * 9, transcendentals=0),
        name="front",
    )(at, row_len, ids, pack)


def front_back_kernel(vocab, first_row, last_row, at_ref, len_ref, ids_ref, pack_ref, dhid_ref, low_ref, high_ref, conv_ref, mask_ref, share_ref, gain_one_ref, gain_two_ref, *refs):
    if last_row:
        rel_ref, refs = refs[0], refs[1:]
    if not first_row:
        before_ref, refs = refs[0], refs[2:]
    din_ref, grad_ref, wall_ref, tri_ref, quad_ref, pair_ref, dconv_ref, sum_ref = refs
    frame = ids_ref.shape[2]
    tok = dhid_ref.shape[0]
    extent = frame - 2 * EDGE
    first = at_ref[0] - EDGE
    pad = wall_ref.shape[0]

    unpack_front(pack_ref, wall_ref)
    for ref, size in ((pair_ref, 2), (tri_ref, 3), (quad_ref, 4)):
        ref[...] = same_block(first + 12 * EDGE, frame, size).astype(BF16)
    sum_ref[...] = jnp.zeros_like(sum_ref) if first_row else before_ref[...]
    limit = len_ref[0]
    low = vocab // 16 * 16
    vectors = wall_ref[low : -(-(vocab + 7) // 16) * 16, :].astype(F32)
    base = vocab - low
    shares = [share_ref[0, b : b + 1, :] for b in range(4)]
    one = (lax.broadcasted_iota(jnp.int32, (frame, frame), 0) == lax.broadcasted_iota(jnp.int32, (frame, frame), 1)).astype(F32)
    masks = [one] + [ref[...].astype(F32) * (1.0 / size) for ref, size in ((pair_ref, 2), (tri_ref, 3), (quad_ref, 4))]
    mix = functools.reduce(jnp.add, [m * s for m, s in zip(masks, shares)])
    start = 2 * lax.broadcasted_iota(jnp.int32, (frame, tok), 1) + EDGE
    here = lax.broadcasted_iota(jnp.int32, (frame, tok), 0)
    pool = jnp.where((here == start) | (here == start + 1), 0.5, 0.0).astype(BF16)
    rim_start = 2 * lax.broadcasted_iota(jnp.int32, (frame, 8), 1)
    rim_here = lax.broadcasted_iota(jnp.int32, (frame, 8), 0)

    def rim_pool(offset):
        begin = rim_start + offset
        return jnp.where((rim_here == begin) | (rim_here == begin + 1), 0.5, 0.0).astype(BF16)

    m_high, m_rest = split_two(mix)
    conv = conv_ref[0]
    c_high, c_rest = split_two(conv)
    d_conv = jnp.zeros(conv.shape, F32)
    cross = jnp.zeros((frame, frame), F32)
    for ref, spread in ((dhid_ref, pool), (low_ref, rim_pool(EDGE - 16)), (high_ref, rim_pool(EDGE + extent))):
        d_high, d_rest = split_two(ref[...])
        weights = dot_nn(m_high, spread) + dot_nn(m_rest, spread)
        w_high, w_rest = split_two(weights)
        d_conv += dot_nn(w_high, d_high) + (dot_nn(w_high, d_rest) + dot_nn(w_rest, d_high))
        pairs = dot_nt(c_high, d_high) + (dot_nt(c_high, d_rest) + dot_nt(c_rest, d_high))
        cross += dot_half(dot_nt, pairs, spread)
    d_shares = [jnp.sum(m * cross, axis=0, keepdims=True) for m in masks]
    inner = functools.reduce(jnp.add, [s * d for s, d in zip(shares, d_shares)])
    d_single = jnp.sum(
        functools.reduce(jnp.add, [m * (s * (d - inner)) for m, s, d in zip(masks, shares, d_shares)]), axis=1, keepdims=True
    )
    own_col = lax.broadcasted_iota(jnp.int32, (frame, 1), 0)
    place_col = own_col + first
    live_col = ((place_col >= 0) & (place_col < limit)).astype(F32)
    own = ((own_col >= EDGE) & (own_col < frame - EDGE)).astype(F32)
    dconv_ref[...] = (d_conv + d_single * vectors[base + 4 : base + 5]) * live_col
    grad_score = jnp.sum(conv * (d_single * own), axis=0, keepdims=True)
    masked = mask_ref[0].astype(F32)
    d_masked = jnp.zeros(masked.shape, F32)
    for j in range(4):
        moved = dconv_ref[EDGE + 2 - j : EDGE + 2 - j + extent, :]
        d_masked += vectors[base + j : base + j + 1] * moved
        sum_ref[vocab + j : vocab + j + 1, :] += jnp.sum(masked * moved, axis=0, keepdims=True)
    sum_ref[vocab + 4 : vocab + 5, :] += grad_score
    d_in = (d_masked * live_col[EDGE : frame - EDGE]).astype(BF16)
    din_ref[0] = d_in
    ids = ids_ref[0][:, EDGE : frame - EDGE]
    emb_rows = -(-vocab // 8) * 8
    onehot = (lax.broadcasted_iota(jnp.int32, (emb_rows, extent), 0) == ids).astype(F32).astype(BF16)
    sum_ref[0:emb_rows, :] += dot_nn(onehot, d_in)

    sum_ref[vocab + 5 : vocab + 6, :] += gain_one_ref[...]
    sum_ref[vocab + 6 : vocab + 7, :] += gain_two_ref[...]
    if last_row:
        parts, _, share = grad_ref.shape
        for d in range(parts):
            grad_ref[d] = sum_ref[:, d * share : (d + 1) * share].astype(BF16)
            grad_ref[d, vocab + 7 : vocab + 7 + rel_ref.shape[0], :] = rel_ref[...].astype(BF16)
    else:
        grad_ref[...] = sum_ref[...]


def front_backward(at, row_len, ids, pack, d_hid, rims, conv, masked, shares, gains, rel, vocab, row, rows, before):
    frame = ids.shape[2]
    extent = frame - 2 * EDGE
    d_model = d_hid.shape[1]
    pad = pack.shape[1]
    args = [ids, pack, d_hid, *rims, conv, masked, shares, *gains] + ([rel] if row == rows - 1 else [])
    specs = [scalars(), scalars(), *in_vmem(args)]
    aliases = {}
    if before:
        specs += [whole(before[0]), pl.BlockSpec(memory_space=pl.ANY)]
        aliases = {len(specs) - 1: 0}
    grads = jax.ShapeDtypeStruct(pack.shape, BF16) if row == rows - 1 else jax.ShapeDtypeStruct((pad, d_model), F32)
    return pl.pallas_call(
        functools.partial(front_back_kernel, vocab, row == 0, row == rows - 1),
        grid=(1,),
        in_specs=specs,
        out_specs=[pl.BlockSpec((1, extent, d_model), lambda *_: (row, 0, 0)), whole(grads)],
        out_shape=[jax.ShapeDtypeStruct((rows, extent, d_model), BF16), grads],
        scratch_shapes=[
            pltpu.VMEM((pad, d_model), BF16),
            pltpu.VMEM((frame, frame), BF16),
            pltpu.VMEM((frame, frame), BF16),
            pltpu.VMEM((frame, frame), BF16),
            pltpu.VMEM((frame, d_model), F32),
            pltpu.VMEM((pad, d_model), F32),
        ],
        input_output_aliases=aliases,
        compiler_params=pltpu.CompilerParams(vmem_limit_bytes=56 << 20),
        cost_estimate=pl.CostEstimate(flops=16 * frame * frame * d_model, bytes_accessed=frame * d_model * 12, transcendentals=0),
        name="front_back",
    )(at, row_len, *args, *before)


def settle_kernel(vocab, x_ref, got_ref, emb_ref, conv_ref, vec_ref, rel_ref):
    total = x_ref[...] + got_ref[...].astype(F32)
    emb_ref[...] = total[:vocab]
    conv_ref[...] = total[vocab : vocab + 4]
    vec_ref[...] = total[vocab + 4 : vocab + 7]
    rel_ref[...] = total[vocab + 7 : vocab + 7 + rel_ref.shape[0]]


def settle(x, got, vocab, rel_rows):
    share = x.shape[1]
    outs = [jax.ShapeDtypeStruct((rows, share), F32) for rows in (vocab, 4, 3, rel_rows)]
    return pl.pallas_call(
        functools.partial(settle_kernel, vocab),
        grid=(1,),
        in_specs=in_vmem([x, got]),
        out_specs=in_vmem(outs),
        out_shape=outs,
        name="settle",
    )(x, got)


GELU_C = 0.7978845608
GELU_A = 0.044715


def pack_down(x):
    rows, third = x.shape[1], x.shape[2] // 3
    left, mid, right = x[..., :third], x[..., third : 2 * third], x[..., 2 * third :]
    return jnp.concatenate(
        [jnp.concatenate([left, right[:, : rows // 2]], axis=1), jnp.concatenate([mid, right[:, rows // 2 :]], axis=1)], axis=2
    )


def unpack_down(x):
    rows, third = x.shape[1] * 2 // 3, x.shape[2] // 2
    right = jnp.concatenate([x[:, rows:, :third], x[:, rows:, third:]], axis=1)
    return jnp.concatenate([x[:, :rows, :third], x[:, :rows, third:], right], axis=2)


def feed_kernel(nblk, rows, row, sizes, *refs):
    share, ff_cols, width, down_rows = sizes
    x_refs, cot_refs, rest_ref = refs[:nblk], refs[nblk : 2 * nblk], refs[2 * nblk]
    refs = refs[2 * nblk + 1 :]
    sums_in, outs_in = None, ()
    if row > 0:
        outs_in, sums_in, refs = refs[:nblk], refs[nblk : nblk + 2], refs[nblk + 2 :]
    outs, dnorms, grads = refs[:nblk], refs[nblk : 2 * nblk], refs[2 * nblk :]
    if row == rows - 1:
        pack_ref, sum_a, sum_b = grads
    else:
        sum_a, sum_b = grads
    parts = rest_ref.shape[0]
    w_in = rest_ref[:, :share, : 2 * ff_cols].reshape(parts * share, 2 * ff_cols)
    w_down = unpack_down(rest_ref[:, :, 2 * ff_cols :]).reshape(parts * down_rows, width)
    for b in range(nblk):
        x, cot = x_refs[b][...], cot_refs[b][row]
        both = dot_nn(x, w_in)
        gate, up = both[:, :ff_cols], both[:, ff_cols:]
        square = gate * gate
        turned = jnp.tanh(GELU_C * gate * (1.0 + GELU_A * square))
        half = 0.5 * (1.0 + turned)
        gelu = gate * half
        slope = half + (0.5 * GELU_C) * gate * (1.0 - turned * turned) * (1.0 + (3.0 * GELU_A) * square)
        hidden = (gelu * up).astype(BF16)
        if row > 0:
            outs[b][:row] = outs_in[b][...]
        outs[b][row] = dot_nn(hidden, w_down).astype(BF16)
        d_hidden = dot_nt(cot, w_down)
        d_both = jnp.concatenate([(d_hidden * up * slope).astype(BF16), (d_hidden * gelu).astype(BF16)], axis=1)
        dnorms[b][...] = dot_nt(d_both, w_in).astype(BF16)
        grad_a, grad_b = dot_tn(x, d_both), dot_tn(hidden, cot)
        if b == 0 and sums_in is None:
            sum_a[...] = grad_a
            sum_b[...] = grad_b
        elif b == 0:
            sum_a[...] = sums_in[0][...] + grad_a
            sum_b[...] = sums_in[1][...] + grad_b
        else:
            sum_a[...] += grad_a
            sum_b[...] += grad_b
    if row == rows - 1:
        pack_ref[:, :, : 2 * ff_cols] = sum_a[...].astype(BF16).reshape(parts, share, 2 * ff_cols)
        pack_ref[:, :, 2 * ff_cols :] = pack_down(sum_b[...].astype(BF16).reshape(parts, down_rows, width))


def feed(xs, cots, rest, before, row, sizes):
    nblk = len(xs)
    tok, d_model = xs[0].shape
    share, ff_cols, width, down_rows = sizes
    parts, rows = rest.shape[0], cots[0].shape[0]
    sum_shapes = [(d_model, 2 * ff_cols), (parts * down_rows, width)]
    outs = [jax.ShapeDtypeStruct((row + 1, tok, width), BF16)] * nblk + [jax.ShapeDtypeStruct((tok, d_model), BF16)] * nblk
    scratch = []
    if row == rows - 1:
        outs.append(jax.ShapeDtypeStruct(rest.shape, BF16))
        scratch = [pltpu.VMEM(s, F32) for s in sum_shapes]
    else:
        outs += [jax.ShapeDtypeStruct(s, F32) for s in sum_shapes]
    args = [*xs, *cots, rest, *before]
    flops = 2 * nblk * tok * d_model * ff_cols * 9
    got = pl.pallas_call(
        functools.partial(feed_kernel, nblk, rows, row, sizes),
        grid=(1,),
        in_specs=in_vmem(args),
        out_specs=in_vmem(outs),
        out_shape=outs,
        scratch_shapes=scratch,
        compiler_params=pltpu.CompilerParams(vmem_limit_bytes=56 << 20),
        cost_estimate=pl.CostEstimate(flops=flops, bytes_accessed=12 << 20, transcendentals=nblk * tok * ff_cols),
        name="feed",
    )(*args)
    return got[:nblk], got[nblk : 2 * nblk], got[2 * nblk :]


P = jax.sharding.PartitionSpec


def rims_of(x, width):
    size, length = lax.axis_size("seq"), x.shape[1]
    up = [(i, i + 1) for i in range(size - 1)]
    down = [(j, i) for i, j in up]
    before = lax.ppermute(x[:, length - width :], "seq", up)
    after = lax.ppermute(x[:, :width], "seq", down)
    return before, after


def flip_with(x, axis, bit):
    return lax.ppermute(x, axis, [(i, i ^ bit) for i in range(lax.axis_size(axis))])


def bits_of(axis):
    bits, bit = [], 1
    while bit < lax.axis_size(axis):
        bits.append(bit)
        bit *= 2
    return bits[::-1]


def after(x, *others):
    return lax.optimization_barrier((x,) + others)[0]


def places_of(n):
    places = [0]
    bit = n // 2
    while bit:
        places = places + [p ^ bit for p in places]
        bit //= 2
    return places


def swap_blocks(parts):
    return [part if bit == 0 else flip_with(part, "seq", bit) for part, bit in zip(parts, places_of(len(parts)))]


def gather_direct(x):
    return swap_blocks([x] * lax.axis_size("seq"))


def gather_first(x):
    blocks = [x]
    for bit in bits_of("seq")[:-1]:
        blocks = blocks + [flip_with(block, "seq", bit) for block in blocks]
    return blocks


def gather_last(blocks):
    return blocks + [flip_with(block, "seq", 1) for block in blocks]


def gather_two(x):
    return gather_last(gather_first(x))


def scatter_first(parts):
    half = len(parts) // 2
    got = [flip_with(part, "seq", 1) for part in parts[half:]]
    send = [(a.astype(F32) + b.astype(F32)).astype(BF16) for a, b in zip(parts[1:half], got[1:])]
    return [parts[0], got[0]], send


def scatter_last(own, send):
    return own + [flip_with(part, "seq", place) for part, place in zip(send, places_of(2 * len(send) + 2)[1:])]


def add_up(parts):
    return functools.reduce(jnp.add, [part.astype(F32) for part in parts])


def scatter_step(x, bit):
    axis = bits_of("dp").index(bit)
    low, high = lax.index_in_dim(x, 0, axis), lax.index_in_dim(x, 1, axis)
    upper = (lax.axis_index("dp") & bit) != 0
    keep, send = jnp.where(upper, high, low), jnp.where(upper, low, high)
    return keep, flip_with(send.astype(BF16), "dp", bit)


def swap_dp(x):
    return lax.all_to_all(x, "dp", split_axis=0, concat_axis=0, tiled=True)


def sum_parts(x):
    return jnp.sum(x.astype(F32), axis=0)


def gather_step(x, bit, *gate):
    axis = bits_of("dp").index(bit)
    other = flip_with(x, "dp", bit)
    other = after(other, *gate) if gate else other
    upper = (lax.axis_index("dp") & bit) != 0
    return jnp.concatenate([jnp.where(upper, other, x), jnp.where(upper, x, other)], axis=axis)


def gather_start(x):
    return x.reshape((1,) * len(bits_of("dp")) + x.shape)


def sum_step(x, bit):
    low = x.astype(BF16)
    return low.astype(F32) + flip_with(low, "seq", bit).astype(F32)


def sum_seq(x):
    for bit in bits_of("seq")[::-1]:
        x = sum_step(x, bit)
    return x


def in_order(blocks, me):
    n = len(blocks)
    bits = bits_of("seq")
    x = jnp.stack(blocks).reshape((2,) * len(bits) + blocks[0].shape)
    for at, bit in enumerate(bits[::-1]):
        upper = (me & bit) != 0
        x = jnp.where(upper, jnp.flip(x, at), x)
    x = x.transpose(tuple(range(len(bits)))[::-1] + tuple(range(len(bits), x.ndim)))
    return x.reshape((n,) + blocks[0].shape)


def on_device(
    byte_ids,
    lengths,
    deal_order,
    buckets,
    embedding,
    conv_w,
    score_w,
    gain_one,
    w_query,
    w_key,
    w_value,
    w_out,
    rel_bias,
    gain_two,
    w_gate,
    w_up,
    w_down,
    cotangent,
):
    n = lax.axis_size("seq")
    dp = lax.axis_size("dp")
    me = lax.axis_index("seq")
    rows_dev, extent = byte_ids.shape
    share, width = w_query.shape
    d_model = share * dp
    head_cols = width // n
    heads_dev = head_cols // DH
    ff_cols = w_gate.shape[1] // n
    down_rows = w_down.shape[0] // n
    tok = cotangent.shape[1]
    place = jnp.array(places_of(n), jnp.int32) ^ me

    vocab = embedding.shape[0]
    rel_rows = -(-rel_bias.size // share)
    pad_vocab = -(-(vocab + 7 + rel_rows) // 16) * 16
    front_pack = jnp.concatenate(
        [embedding, conv_w, score_w[None], gain_one[None], gain_two[None], jnp.zeros((pad_vocab - vocab - 7, share), BF16)], axis=0
    )

    def own_cols(weight):
        return lax.dynamic_slice_in_dim(weight, me * head_cols, head_cols, 1)

    qkv_pack = jnp.concatenate([own_cols(w_query), own_cols(w_key), own_cols(w_value), own_cols(w_out)], axis=1)
    front_all, qkv_w = gather_start(front_pack), gather_start(qkv_pack)
    up_bits = bits_of("dp")
    qkv_bits = up_bits[-1:] + up_bits[:-1]
    for at, bit in enumerate(up_bits):
        front_all = gather_step(front_all, bit)
        if at == 0:
            byte_ids, cotangent, rel_in = (after(x, front_all) for x in (byte_ids, cotangent, rel_bias))
        if at < len(up_bits) - 1:
            qkv_w = after(gather_step(qkv_w, qkv_bits[at]), front_all)
    front_all = front_all.reshape((dp,) + front_pack.shape)
    gain_first = front_all[:, vocab + 5].reshape(1, d_model).astype(F32)
    gain_second = front_all[:, vocab + 6].reshape(1, d_model).astype(F32)

    def own_ff(weight):
        return lax.dynamic_index_in_dim(weight.reshape(share, dp, n, down_rows), me, 2, keepdims=False).reshape(
            share, ff_cols
        )

    down_own = lax.dynamic_slice_in_dim(w_down, me * down_rows, down_rows, 0)
    rest_pack = jnp.concatenate([own_ff(w_gate), own_ff(w_up), pack_down(down_own[None])[0]], axis=1)
    offset = me * extent
    matches = deal_order[:, None] == jnp.arange(lengths.shape[0], dtype=jnp.int32)[None, :]
    row_len = jnp.sum(jnp.where(matches, lengths[None, :], 0), axis=1)
    rim_low, rim_high = rims_of(byte_ids, EDGE)
    ids = jnp.concatenate([rim_low, byte_ids, rim_high], axis=1)[:, None, :]
    at = jnp.full((1,), offset, jnp.int32)
    row_ids = range(rows_dev)
    lens = [row_len[r : r + 1] for r in row_ids]

    first_head = me * heads_dev
    bias_loc = lax.dynamic_slice_in_dim(rel_in, first_head, heads_dev, 1)
    offsets = jnp.concatenate([jnp.full((1,), -1, jnp.int32), buckets[::-1]])
    onehot = (offsets[None, :] == jnp.arange(rel_bias.shape[0], dtype=jnp.int32)[:, None]).astype(BF16)
    strips = bias_strips(jnp.einsum("nh,nx->hx", bias_loc, onehot, preferred_element_type=F32), n)

    cots = gather_two(cotangent)
    normed, h_zero, kept = [], [], []
    gate = (strips,)
    for r in row_ids:
        h, low, *rest = front_forward(at, lens[r], after(ids[r : r + 1], *gate), front_all, vocab, d_model)
        if r == 0:
            qkv_w = after(qkv_w, low)
        gate = (low,)
        h_zero.append(h[0])
        normed.append(low[0])
        kept.append(rest)
    low_one = [gather_two(low) if r == 0 else gather_direct(low) for r, low in enumerate(normed)]
    qkv_w = gather_step(qkv_w, qkv_bits[-1], *gate)
    qkv_w = qkv_w.reshape(d_model, 4 * head_cols)
    rest_all = lax.all_gather(after(rest_pack, qkv_w), "dp", axis=0, tiled=False)
    out_blocks = gather_first(qkv_w[:, 3 * head_cols :])
    qkv_w = qkv_w[:, : 3 * head_cols]
    gate = gate + tuple(cots)
    atts, qkvs, logs, mixed = [], [], [], []
    for r in row_ids:
        xs = [after(low_one[r][0], *gate)] + list(low_one[r][1:])
        att, qkv, log = attend(place, lens[r], xs, qkv_w, strips)
        gate = (qkv,)
        atts.append(att)
        qkvs.append(qkv)
        logs.append(log)
        mixed.append(swap_blocks([after(a, *mixed[r - 1]) for a in att] if r else att))
        if r == 0:
            out_blocks = gather_last([after(block, *gate) for block in out_blocks])
    w_out_all, h_one, lows = project(place, out_blocks, [[after(m[0], *gate)] + m[1:] for m in mixed], h_zero, gain_second)
    low_two = [gather_two(low) if r == 0 else gather_direct(low) for r, low in enumerate(lows)]
    sizes = (share, ff_cols, width, down_rows)
    d_norm_two, before = [], ()
    for r in row_ids:
        xs = [after(low_two[r][0], *gate)] + low_two[r][1:]
        ff_outs, d_norm, sums = feed(xs, cots, rest_all, before, r, sizes)
        before = (*ff_outs, *sums)
        gate = (d_norm[0],)
        if r:
            d_norm = [after(part, *d_norm_two[r - 1]) for part in d_norm]
        if r < rows_dev - 1:
            d_norm_two.append(swap_blocks(d_norm))
        else:
            two_own, two_send = scatter_first(d_norm)
            d_norm_two.append(scatter_last(two_own, two_send))
    ff_sum = lax.psum_scatter(sums[0], "dp", scatter_dimension=0, tiled=False)
    d_h_one, gains_two, out_grad, d_norms, qkv_grad, d_revs = [], [], None, [], None, []
    for r in row_ids:
        last = r == rows_dev - 1
        adds = [after(d_norm_two[r][0], *gate)] + d_norm_two[r][1:]
        d_h, gain_grad, d_att, out_grad = project_back(
            place, adds, mixed[r], w_out_all, h_one[r], cotangent, r, gain_second, out_grad, dp if last else 0
        )
        gate = (d_h,)
        d_h_one.append(d_h)
        gains_two.append(gain_grad)
        douts = swap_blocks(d_att)
        if r == 0:
            ff_own, ff_send = scatter_first([after(ff_out, *gate) for ff_out in ff_outs])
            ff_whole = scatter_last(ff_own, ff_send)
            gate = gate + tuple(two_send) + tuple(ff_send)
        elif r == 1:
            gate = gate + tuple(ff_whole)
        d_norm, qkv_grad, d_rev = attend_back(
            place, lens[r], low_one[r], qkv_w, qkvs[r], atts[r], [after(douts[0], *gate)] + douts[1:], logs[r], strips,
            qkv_grad, dp if last else 0,
        )
        gate = (d_norm[0],)
        d_norms.append(d_norm)
        d_revs.append(d_rev)
    out_parts = swap_dp(out_grad)
    dp_bits = bits_of("dp")[::-1]
    qkv_sum = [qkv_grad.reshape((2,) * len(dp_bits) + qkv_grad.shape[1:])]
    d_rel_loc = jnp.einsum("nx,hx->nh", onehot.astype(F32), sum(d_revs), precision=lax.Precision.HIGHEST)
    d_rel = lax.dynamic_update_slice_in_dim(jnp.zeros(rel_bias.shape, F32), d_rel_loc, first_head, 1)
    d_rel = jnp.pad(d_rel.reshape(-1), (0, rel_rows * share - rel_bias.size)).reshape(rel_rows, share)

    d_first = [swap_blocks(d_norm) for d_norm in d_norms[:-1]]
    last_own, last_send = scatter_first([after(part, *d_first[-1]) for part in d_norms[-1]])
    d_first.append(scatter_last(last_own, last_send))
    seq_bits = bits_of("seq")[::-1]
    g_out = sum_parts(after(out_parts, *gate))
    front_grad = ()
    for r in row_ids:
        adds = [after(d_first[r][0], *gate)] + d_first[r][1:]
        d_h_zero, low_rim, high_rim, gain_grad = first_back(adds, h_zero[r], d_h_one[r], gain_first)
        size = lax.axis_size("seq")
        low_side = lax.ppermute(high_rim, "seq", [(i, i + 1) for i in range(size - 1)])
        high_side = lax.ppermute(low_rim, "seq", [(i + 1, i) for i in range(size - 1)])
        if dp_bits:
            qkv_sum = scatter_step(add_up([after(part, *gate) for part in qkv_sum]), dp_bits.pop(0))
        extra = (*last_send, g_out, ff_sum) if r == 0 else (g_out,)
        conv_out, masked, shares = kept[r]
        d_input, front_sum = front_backward(
            at, lens[r], ids[r : r + 1], front_all, after(d_h_zero, *extra), (low_side, high_side), conv_out, masked, shares,
            (gain_grad, gains_two[r]), d_rel, vocab, r, rows_dev, front_grad,
        )
        front_grad = (front_sum, d_input)
        gate = (front_sum,)
        if r == 0:
            ff_all = gather_first(ff_sum)
            ff_all = [ff_all[0]] + [after(block, *gate) for block in ff_all[1:]]
            gate = gate + tuple(ff_all[1:])
            ff_all = gather_last(ff_all)
            g_out = sum_step(after(g_out, *gate), seq_bits.pop(0))
    ff_all = [after(block, *gate) for block in ff_all]
    front_parts = swap_dp(after(front_sum, *ff_all))
    qkv_sum = add_up([after(part, *gate) for part in qkv_sum])
    while dp_bits:
        qkv_sum = scatter_step(qkv_sum, dp_bits.pop(0))
        tail = (qkv_sum[1],)
        qkv_sum = add_up(qkv_sum)
    g_out = after(g_out, *gate)
    while seq_bits:
        g_out = sum_step(g_out, seq_bits.pop(0))
    output = (jnp.stack([after(h, *tail) for h in h_one]) + add_up(ff_whole)).astype(BF16)
    ff_all = in_order([after(block, *tail) for block in ff_all], me)
    g_gu = ff_all[:, :, : 2 * ff_cols].reshape(n, share, 2, dp, down_rows)
    g_gu = g_gu.transpose(2, 1, 3, 0, 4).reshape(2, share, n * ff_cols).astype(F32)
    g_down = unpack_down(ff_all[:, :, 2 * ff_cols :]).reshape(n * down_rows, width).astype(F32)
    g_qkv = in_order(gather_two(qkv_sum.astype(BF16).reshape(share, 3, head_cols)), me)
    g_qkv = g_qkv.transpose(2, 1, 0, 3).reshape(3, share, width).astype(F32)
    front_sum = sum_parts(front_parts)
    front_bits = bits_of("seq")[::-1]
    for bit in front_bits[:-1]:
        front_sum = sum_step(front_sum, bit)
    front_low = front_sum.astype(BF16)
    g_emb, g_conv, g_vec, g_rel = settle(front_low.astype(F32), flip_with(front_low, "seq", front_bits[-1]), vocab, rel_rows)
    return (
        output,
        d_input,
        g_emb,
        g_conv,
        g_vec[0],
        g_vec[1],
        g_qkv[0],
        g_qkv[1],
        g_qkv[2],
        g_out,
        g_rel.reshape(-1)[: rel_bias.size].reshape(rel_bias.shape),
        g_vec[2],
        g_gu[0],
        g_gu[1],
        g_down,
    )


def solution(mesh):
    return jax.shard_map(
        on_device,
        mesh=mesh,
        in_specs=(
            P("dp", "seq"),
            P(),
            P("dp"),
            P(),
            P(None, "dp"),
            P(None, "dp"),
            P("dp"),
            P("dp"),
            P("dp", None),
            P("dp", None),
            P("dp", None),
            P("dp", None),
            P(),
            P("dp"),
            P("dp", None),
            P("dp", None),
            P("dp", None),
            P("dp", "seq", None),
        ),
        out_specs=(
            P("dp", "seq", None),
            P("dp", "seq", None),
            P(None, "dp"),
            P(None, "dp"),
            P("dp"),
            P("dp"),
            P("dp", None),
            P("dp", None),
            P("dp", None),
            P("dp", None),
            P(),
            P("dp"),
            P("dp", None),
            P("dp", None),
            P("dp", None),
        ),
        check_vma=False,
    )
```

```python
import functools
import jax, jax.numpy as jnp
from jax import lax
from jax.experimental import pallas as pl
from jax.experimental.pallas import tpu as pltpu
DH=64
NEG=-1e9
F32, BF16 = jnp.float32, jnp.bfloat16


def dot_nt(a, b):
    return lax.dot_general(a, b, (((1,), (1,)), ((), ())), preferred_element_type=F32)


def dot_nn(a, b):
    return lax.dot_general(a, b, (((1,), (0,)), ((), ())), preferred_element_type=F32)


def tile_at(place_ref, kb, qb, nblk):
    return jnp.clip(place_ref[kb] - place_ref[qb], -2, 2) + 2


def strip_kernel(nblk, rev_ref, strip_ref):
    heads, _, blk = strip_ref.shape
    for head in range(heads):
        for part in range(5):
            low = (nblk + 1 - part) * blk
            here = slice(part * blk, (part + 1) * blk)
            if part in (0, 4):
                strip_ref[head, here, :] = jnp.broadcast_to(rev_ref[head : head + 1, low + blk : low + blk + 1], (blk, blk))
                continue
            segment = jnp.broadcast_to(rev_ref[head : head + 1, low : low + 2 * blk], (blk, 2 * blk))
            strip_ref[head, here, :] = pltpu.roll(segment, 0, 1, stride=1, stride_axis=0)[:, blk:]


def bias_strips(rev, nblk):
    heads, width = rev.shape
    blk = width // (2 * nblk)
    return pl.pallas_call(
        functools.partial(strip_kernel, nblk),
        out_shape=jax.ShapeDtypeStruct((heads, 5 * blk, blk), F32),
        compiler_params=pltpu.CompilerParams(vmem_limit_bytes=32 << 20),
        name="strips",
    )(rev)


def key_side(key, ok_col):
    rows = key.shape[0]
    lane = lax.broadcasted_iota(jnp.int32, (rows, DH), 1)
    extra = jnp.where(lane == 0, ok_col, 0.0).astype(BF16)
    return jnp.concatenate([key, extra], axis=1)


def query_side(query):
    rows = query.shape[0]
    lane = lax.broadcasted_iota(jnp.int32, (rows, DH), 1)
    return jnp.concatenate([query, jnp.where(lane == 0, 1.0, 0.0).astype(BF16)], axis=1)


def mask_column(place_ref, limit, blk, nblk):
    cols = []
    for b in range(nblk):
        at = place_ref[b] * blk + lax.broadcasted_iota(jnp.int32, (blk, DH), 0)
        cols.append(jnp.where(2 * at < limit, 0.0, NEG))
    return jnp.concatenate(cols, axis=0)


def dot_tn(a, b):
    return lax.dot_general(a, b, (((0,), (0,)), ((), ())), preferred_element_type=F32)


def whole(arg):
    return pl.BlockSpec(arg.shape, lambda *_: (0,) * len(arg.shape), pipeline_mode=pl.Buffered(1))


def in_vmem(args):
    return [whole(arg) for arg in args]


def scalars():
    return pl.BlockSpec(memory_space=pltpu.SMEM)


def attend_kernel(heads, nblk, place_ref, len_ref, *refs):
    xs, (w_ref, strip_ref), refs = refs[:nblk], refs[nblk : nblk + 2], refs[nblk + 2 :]
    outs, (qkv_ref, log_ref, att_ref, kaug_ref, qaug_ref, vt_ref) = refs[:nblk], refs[nblk:]
    blk = xs[0].shape[0]
    for b in range(nblk):
        qkv_ref[b * blk : (b + 1) * blk, :] = dot_nn(xs[b][...], w_ref[...]).astype(BF16)
    ok_col = mask_column(place_ref, len_ref[0], blk, nblk)
    width = heads * DH
    for head in range(heads):
        at = head * DH
        qaug_ref[...] = query_side(qkv_ref[:, at : at + DH])
        kaug_ref[...] = key_side(qkv_ref[:, width + at : width + at + DH], ok_col)
        vt_ref[...] = qkv_ref[:, 2 * width + at : 2 * width + at + DH].T

        def one_block(qb, carry):
            q_at = pl.multiple_of(qb * blk, blk)
            query = qaug_ref[pl.ds(q_at, blk), :]
            parts = []
            for kb in range(nblk):
                m_at = pl.multiple_of(tile_at(place_ref, kb, qb, nblk) * blk, blk)
                parts.append(dot_nt(kaug_ref[kb * blk : (kb + 1) * blk, :], query) + strip_ref[head, pl.ds(m_at, blk), :])
            top = functools.reduce(jnp.maximum, [jnp.max(p, axis=0, keepdims=True) for p in parts])
            total = jnp.zeros((1, blk), F32)
            acc = jnp.zeros((DH, blk), F32)
            for kb in range(nblk):
                weight = jnp.exp(parts[kb] - top)
                total += jnp.sum(weight, axis=0, keepdims=True)
                acc += dot_nn(vt_ref[:, kb * blk : (kb + 1) * blk], weight.astype(BF16))
            att_ref[pl.ds(q_at, blk), at : at + DH] = (acc / total).T.astype(BF16)
            log_ref[head, pl.ds(qb, 1), :] = top + jnp.log(total)
            return carry

        lax.fori_loop(0, nblk, one_block, 0, unroll=2)
    for b in range(nblk):
        outs[b][...] = att_ref[b * blk : (b + 1) * blk, :]


def attend(place, row_len, xs, w_qkv, strips):
    nblk = len(xs)
    blk = xs[0].shape[0]
    heads = strips.shape[0]
    tokens = nblk * blk
    outs = [jax.ShapeDtypeStruct((blk, heads * DH), BF16)] * nblk + [
        jax.ShapeDtypeStruct((tokens, 3 * heads * DH), BF16),
        jax.ShapeDtypeStruct((heads, nblk, blk), F32),
    ]
    args = [*xs, w_qkv, strips]
    got = pl.pallas_call(
        functools.partial(attend_kernel, heads, nblk),
        grid=(1,),
        in_specs=[scalars(), scalars(), *in_vmem(args)],
        out_specs=in_vmem(outs),
        out_shape=outs,
        scratch_shapes=[
            pltpu.VMEM((tokens, heads * DH), BF16),
            pltpu.VMEM((tokens, 2 * DH), BF16),
            pltpu.VMEM((tokens, 2 * DH), BF16),
            pltpu.VMEM((DH, tokens), BF16),
        ],
        compiler_params=pltpu.CompilerParams(vmem_limit_bytes=48 << 20),
        cost_estimate=pl.CostEstimate(flops=48 * heads * tokens * tokens * DH, bytes_accessed=8 << 20, transcendentals=heads * tokens * tokens),
        name="attend",
    )(place, row_len, *args)
    return got[:nblk], got[nblk], got[nblk + 1]


def attend_back_kernel(heads, nblk, first, final, place_ref, len_ref, *refs):
    xs, (w_ref, qkv_ref), refs = refs[:nblk], refs[nblk : nblk + 2], refs[nblk + 2 :]
    os, dos, (log_ref, strip_ref), refs = refs[:nblk], refs[nblk : 2 * nblk], refs[2 * nblk : 2 * nblk + 2], refs[2 * nblk + 2 :]
    sum_in = None
    if not first:
        sum_in, refs = refs[0], refs[1:]
    dns, (sum_ref, drev_ref), refs = refs[:nblk], refs[nblk : nblk + 2], refs[nblk + 2 :]
    grads_ref, kaug_ref, qaug_ref, kt_ref, dk_ref, dv_ref, o_ref, do_ref, dqkv_ref = refs
    blk = xs[0].shape[0]
    for b in range(nblk):
        o_ref[b * blk : (b + 1) * blk, :] = os[b][...]
        do_ref[b * blk : (b + 1) * blk, :] = dos[b][...]
    ok_col = mask_column(place_ref, len_ref[0], blk, nblk)
    width = heads * DH
    for head in range(heads):
        grads_ref[head] = jnp.zeros(grads_ref.shape[1:], F32)
        at = head * DH
        qaug_ref[...] = query_side(qkv_ref[:, at : at + DH])
        key = qkv_ref[:, width + at : width + at + DH]
        kaug_ref[...] = key_side(key, ok_col)
        kt_ref[...] = key.T
        dk_ref[...] = jnp.zeros_like(dk_ref)
        dv_ref[...] = jnp.zeros_like(dv_ref)

        def one_block(qb, carry):
            q_at = pl.multiple_of(qb * blk, blk)
            query = qaug_ref[pl.ds(q_at, blk), :]
            dout = do_ref[pl.ds(q_at, blk), at : at + DH]
            prod = dout.astype(F32) * o_ref[pl.ds(q_at, blk), at : at + DH].astype(F32)
            inner = jnp.sum(prod.T, axis=0, keepdims=True)
            log_row = log_ref[head, pl.ds(qb, 1), :]
            dqt = jnp.zeros((DH, blk), F32)
            for kb in range(nblk):
                here = slice(kb * blk, (kb + 1) * blk)
                m_at = pl.multiple_of(tile_at(place_ref, kb, qb, nblk) * blk, blk)
                score = dot_nt(kaug_ref[here, :], query) + strip_ref[head, pl.ds(m_at, blk), :]
                prob = jnp.exp(score - log_row)
                d_prob = dot_nt(qkv_ref[here, 2 * width + at : 2 * width + at + DH], dout)
                d_score = prob * (d_prob - inner)
                low = d_score.astype(BF16)
                grads_ref[head, pl.ds(m_at, blk), :] += d_score
                dv_ref[here, :] += dot_nn(prob.astype(BF16), dout)
                dk_ref[here, :] += dot_nn(low, query[:, :DH])
                dqt += dot_nn(kt_ref[:, here], low)
            dqkv_ref[pl.ds(q_at, blk), at : at + DH] = dqt.T.astype(BF16)
            return carry

        [one_block(qb, 0) for qb in range(nblk)]
        dqkv_ref[:, width + at : width + at + DH] = dk_ref[...].astype(BF16)
        dqkv_ref[:, 2 * width + at : 2 * width + at + DH] = dv_ref[...].astype(BF16)

    total = None
    for b in range(nblk):
        here = dqkv_ref[b * blk : (b + 1) * blk, :]
        dns[b][...] = dot_nt(here, w_ref[...]).astype(BF16)
        grad = dot_tn(xs[b][...], here)
        total = grad if total is None else total + grad
    if not first:
        total += sum_in[...]
    sum_ref[...] = total.astype(BF16).reshape(sum_ref.shape) if final else total

    flip = (
        lax.broadcasted_iota(jnp.int32, (blk, blk), 0) + lax.broadcasted_iota(jnp.int32, (blk, blk), 1) == blk - 1
    ).astype(F32).astype(BF16)
    drev_ref[...] = jnp.zeros_like(drev_ref)
    for head in range(heads):
        for part in range(5):
            low = (nblk + 1 - part) * blk
            grad = grads_ref[head, part * blk : (part + 1) * blk, :]
            if part in (0, 4):
                whole = jnp.sum(jnp.sum(grad, axis=0, keepdims=True), axis=1, keepdims=True)
                drev_ref[head : head + 1, low + blk : low + blk + 1] += whole
                continue
            high = grad.astype(BF16)
            rest = (grad - high.astype(F32)).astype(BF16)
            turned = dot_nn(flip, high) + dot_nn(flip, rest)
            wide = jnp.concatenate([jnp.zeros((blk, blk), F32), turned], axis=1)
            moved = pltpu.roll(wide, blk + 1, 1, stride=1, stride_axis=0)
            drev_ref[head : head + 1, low : low + 2 * blk] += jnp.sum(moved, axis=0, keepdims=True)


def attend_back(place, row_len, xs, w_qkv, qkv, outs, douts, logs, strips, sum_in, parts):
    nblk = len(xs)
    blk, d_model = xs[0].shape
    heads = strips.shape[0]
    tokens = nblk * blk
    cols = 3 * heads * DH
    args = [*xs, w_qkv, qkv, *outs, *douts, logs, strips] + ([] if sum_in is None else [sum_in])
    sum_shape = jax.ShapeDtypeStruct((parts, d_model // parts, cols), BF16) if parts else jax.ShapeDtypeStruct((d_model, cols), F32)
    shapes = [jax.ShapeDtypeStruct((blk, d_model), BF16)] * nblk + [sum_shape, jax.ShapeDtypeStruct((heads, 2 * tokens), F32)]
    got = pl.pallas_call(
        functools.partial(attend_back_kernel, heads, nblk, sum_in is None, bool(parts)),
        grid=(1,),
        in_specs=[scalars(), scalars(), *in_vmem(args)],
        out_specs=in_vmem(shapes),
        out_shape=shapes,
        scratch_shapes=[
            pltpu.VMEM((heads, 5 * blk, blk), F32),
            pltpu.VMEM((tokens, 2 * DH), BF16),
            pltpu.VMEM((tokens, 2 * DH), BF16),
            pltpu.VMEM((DH, tokens), BF16),
            pltpu.VMEM((tokens, DH), F32),
            pltpu.VMEM((tokens, DH), F32),
            pltpu.VMEM((tokens, heads * DH), BF16),
            pltpu.VMEM((tokens, heads * DH), BF16),
            pltpu.VMEM((tokens, cols), BF16),
        ],
        compiler_params=pltpu.CompilerParams(vmem_limit_bytes=56 << 20),
        cost_estimate=pl.CostEstimate(flops=120 * heads * tokens * tokens * DH, bytes_accessed=16 << 20, transcendentals=heads * tokens * tokens),
        name="attend_back",
    )(place, row_len, *args)
    return got[:nblk], got[nblk], got[nblk + 1]


EPS = 1e-06


def project_kernel(nblk, rows, place_ref, *refs):
    cols_refs, refs = refs[:nblk], refs[nblk:]
    atts, refs = refs[: rows * nblk], refs[rows * nblk :]
    hids, gain_ref, w_ref, outs = refs[:rows], refs[rows], refs[rows + 1], refs[rows + 2 :]
    cols = cols_refs[0].shape[1]
    for b in range(nblk):
        for g in range(nblk):

            @pl.when(place_ref[b] == g)
            def _():
                w_ref[:, g * cols : (g + 1) * cols] = cols_refs[b][...]

    for r in range(rows):
        hid = hids[r][...]
        for b in range(nblk):
            here = pl.ds(pl.multiple_of(place_ref[b] * cols, 16), cols)
            hid += dot_nn(atts[r * nblk + b][...], w_ref[here, :])
        outs[2 * r][...] = hid
        factor = lax.rsqrt(jnp.mean(hid * hid, axis=-1, keepdims=True) + EPS)
        outs[2 * r + 1][...] = (hid * factor * gain_ref[...]).astype(BF16)


def project(place, w_blocks, atts, hids, gain):
    rows, nblk = len(atts), len(w_blocks)
    width = w_blocks[0].shape[0]
    args = [*w_blocks, *[block for row in atts for block in row], *hids, gain]
    outs = [jax.ShapeDtypeStruct((width, hids[0].shape[1]), BF16)]
    for hid in hids:
        outs += [jax.ShapeDtypeStruct(hid.shape, F32), jax.ShapeDtypeStruct(hid.shape, BF16)]
    got = pl.pallas_call(
        functools.partial(project_kernel, nblk, rows),
        grid=(1,),
        in_specs=[scalars(), *in_vmem(args)],
        out_specs=in_vmem(outs),
        out_shape=outs,
        compiler_params=pltpu.CompilerParams(vmem_limit_bytes=60 << 20),
        cost_estimate=pl.CostEstimate(flops=4 * rows * hids[0].shape[0] * width * width, bytes_accessed=3 << 20, transcendentals=0),
        name="project",
    )(place, *args)
    return got[0], got[1::2], got[2::2]


def norm_back(hid, gain, d_norm):
    factor = lax.rsqrt(jnp.mean(hid * hid, axis=-1, keepdims=True) + EPS)
    scaled = hid * factor
    weighted = d_norm * gain
    inner = jnp.mean(scaled * weighted, axis=-1, keepdims=True)
    return factor * (weighted - scaled * inner), jnp.sum(d_norm * scaled, axis=0, keepdims=True)


def project_back_kernel(nblk, pieces, row, final, place_ref, *refs):
    adds, atts, refs = refs[:pieces], refs[pieces : pieces + nblk], refs[pieces + nblk :]
    (w_ref, hid_ref, cot_ref, gain_ref), refs = refs[:4], refs[4:]
    earlier, refs = refs[: row * (nblk + 1)], refs[row * (nblk + 1) :]
    dhid_ref, gain_out, datts, sum_ref, acc_ref = refs[0], refs[1], refs[2 : 2 + nblk], refs[2 + nblk], refs[3 + nblk]
    d_norm = adds[0][...].astype(F32)
    for add in adds[1:]:
        d_norm += add[...].astype(F32)
    back, gain_grad = norm_back(hid_ref[...], gain_ref[...], d_norm)
    gain_out[...] = gain_grad
    d_hid = cot_ref[row].astype(F32) + back
    dhid_ref[...] = d_hid
    branch = d_hid.astype(BF16)
    cols = atts[0].shape[1]
    for b in range(nblk):
        here = pl.ds(pl.multiple_of(place_ref[b] * cols, 16), cols)
        datts[b][...] = dot_nt(branch, w_ref[here, :]).astype(BF16)
        if final:
            grad = dot_tn(atts[b][...], branch)
            for r in range(row):
                grad += dot_tn(earlier[r * (nblk + 1) + b][...], earlier[r * (nblk + 1) + nblk][...])
            acc_ref[here, :] = grad
    sum_ref[...] = acc_ref[...].astype(BF16).reshape(sum_ref.shape) if final else branch


def project_back(place, adds, atts, w_out, hid, cot, row, gain, earlier, parts):
    nblk = len(atts)
    blk, cols = atts[0].shape
    width, d_model = w_out.shape
    args = [*adds, *atts, w_out, hid, cot, gain, *earlier]
    sum_shape = jax.ShapeDtypeStruct((parts, width // parts, d_model) if parts else (blk, d_model), BF16)
    outs = [jax.ShapeDtypeStruct(hid.shape, F32), jax.ShapeDtypeStruct((1, d_model), F32)]
    outs += [jax.ShapeDtypeStruct((blk, cols), BF16)] * nblk + [sum_shape]
    got = pl.pallas_call(
        functools.partial(project_back_kernel, nblk, len(adds), row, bool(parts)),
        grid=(1,),
        in_specs=[scalars(), *in_vmem(args)],
        out_specs=in_vmem(outs),
        out_shape=outs,
        scratch_shapes=[pltpu.VMEM((width, d_model), F32)],
        compiler_params=pltpu.CompilerParams(vmem_limit_bytes=60 << 20),
        cost_estimate=pl.CostEstimate(flops=8 * blk * width * d_model, bytes_accessed=6 << 20, transcendentals=0),
        name="project_back",
    )(place, *args)
    return got[0], got[1], got[2 : 2 + nblk], got[2 + nblk]


def first_back_kernel(pieces, *refs):
    adds, (hid_ref, dhid_ref, gain_ref, out_ref, low_ref, high_ref, gain_out) = refs[:pieces], refs[pieces:]
    d_norm = adds[0][...].astype(F32)
    for add in adds[1:]:
        d_norm += add[...].astype(F32)
    back, gain_grad = norm_back(hid_ref[...], gain_ref[...], d_norm)
    gain_out[...] = gain_grad
    d_hid = dhid_ref[...] + back
    out_ref[...] = d_hid
    low_ref[...] = d_hid[:8]
    high_ref[...] = d_hid[-8:]


def first_back(adds, hid, d_hid, gain):
    args = [*adds, hid, d_hid, gain]
    d_model = hid.shape[1]
    outs = [jax.ShapeDtypeStruct(s, F32) for s in (hid.shape, (8, d_model), (8, d_model), (1, d_model))]
    return pl.pallas_call(
        functools.partial(first_back_kernel, len(adds)),
        grid=(1,),
        in_specs=in_vmem(args),
        out_specs=in_vmem(outs),
        out_shape=outs,
        compiler_params=pltpu.CompilerParams(vmem_limit_bytes=32 << 20),
        cost_estimate=pl.CostEstimate(flops=20 * hid.shape[0] * d_model, bytes_accessed=4 << 20, transcendentals=0),
        name="first_back",
    )(*args)


EDGE = 8


def split_two(x):
    high = x.astype(BF16)
    return high, (x - high.astype(F32)).astype(BF16)


def dot_fine(dot, a, b):
    a_high, a_rest = split_two(a)
    b_high, b_rest = split_two(b)
    return dot(a_high, b_high) + (dot(a_high, b_rest) + dot(a_rest, b_high))


def dot_half(dot, a, b_low):
    a_high, a_rest = split_two(a)
    return dot(a_high, b_low) + dot(a_rest, b_low)


def same_block(first, frame, size):
    def group(axis, shape):
        place = lax.broadcasted_iota(jnp.int32, shape, axis) + first
        return jnp.floor((place.astype(F32) + 0.5) * (1.0 / size))

    return (group(0, (frame, 1)) == group(1, (1, frame))).astype(F32)


def unpack_front(pack_ref, wall_ref):
    parts, _, share = pack_ref.shape
    for d in range(parts):
        wall_ref[:, d * share : (d + 1) * share] = pack_ref[d]


def front_kernel(vocab, at_ref, len_ref, ids_ref, pack_ref, hid_ref, norm_ref, conv_ref, mask_ref, share_ref, wall_ref, tri_ref, quad_ref, pair_ref, x_ref):
    row = pl.program_id(0)
    frame = ids_ref.shape[2]
    tok = hid_ref.shape[1]
    first = at_ref[0] - EDGE

    @pl.when(row == 0)
    def _():
        unpack_front(pack_ref, wall_ref)
        for ref, size in ((pair_ref, 2), (tri_ref, 3), (quad_ref, 4)):
            ref[...] = same_block(first + 12 * EDGE, frame, size).astype(BF16)

    limit = len_ref[row]
    pad = wall_ref.shape[0]
    place_row = lax.broadcasted_iota(jnp.int32, (1, frame), 1) + first
    live_row = (place_row >= 0) & (place_row < limit)
    ids = jnp.where(live_row, ids_ref[0], -1)
    onehot = (lax.broadcasted_iota(jnp.int32, (pad, frame), 0) == ids).astype(F32).astype(BF16)
    masked = lax.dot_general(onehot, wall_ref[...], (((0,), (0,)), ((), ())), preferred_element_type=F32)
    mask_ref[0] = masked[EDGE : frame - EDGE].astype(BF16)
    x_ref[0:EDGE, :] = jnp.zeros((EDGE, masked.shape[1]), F32)
    x_ref[EDGE : EDGE + frame, :] = masked
    x_ref[EDGE + frame :, :] = jnp.zeros((EDGE, masked.shape[1]), F32)
    low = vocab // 16 * 16
    vectors = wall_ref[low : -(-(vocab + 7) // 16) * 16, :].astype(F32)
    base = vocab - low
    place_col = lax.broadcasted_iota(jnp.int32, (frame, 1), 0) + first
    live_col = ((place_col >= 0) & (place_col < limit)).astype(F32)
    conv = vectors[base : base + 1] * x_ref[EDGE - 2 : EDGE - 2 + frame, :]
    for j in range(1, 4):
        conv += vectors[base + j : base + j + 1] * x_ref[EDGE - 2 + j : EDGE - 2 + j + frame, :]
    conv = conv * live_col
    conv_ref[0] = conv
    c_high, c_rest = split_two(conv)
    score_w = jnp.broadcast_to(vectors[base + 4 : base + 5], (8, conv.shape[1])).astype(BF16)
    single = (dot_nt(score_w, c_high) + dot_nt(score_w, c_rest))[0:1]
    s_high = single.astype(BF16).astype(F32)
    s_mid = (single - s_high).astype(BF16).astype(F32)
    stack = jnp.concatenate([s_high, s_mid, single - s_high - s_mid, jnp.zeros((5, frame), F32)], axis=0).astype(BF16)
    scores = [single]
    for ref, size in ((pair_ref, 2), (tri_ref, 3), (quad_ref, 4)):
        scores.append(jnp.sum(dot_nn(stack, ref[...]), axis=0, keepdims=True) * (1.0 / size))
    top = functools.reduce(jnp.maximum, scores)
    raw = [jnp.exp(s - top) for s in scores]
    total = raw[0] + raw[1] + raw[2] + raw[3]
    shares = jnp.concatenate([r / total for r in raw] + [jnp.zeros((4, frame), F32)], axis=0)
    share_ref[0] = shares
    cols = shares.T
    one = (lax.broadcasted_iota(jnp.int32, (frame, frame), 0) == lax.broadcasted_iota(jnp.int32, (frame, frame), 1))
    mix = jnp.where(one, cols[:, 0:1], 0.0)
    for at, (ref, size) in enumerate(((pair_ref, 2), (tri_ref, 3), (quad_ref, 4))):
        mix += ref[...].astype(F32) * (cols[:, at + 1 : at + 2] * (1.0 / size))
    start = 2 * lax.broadcasted_iota(jnp.int32, (tok, frame), 0) + EDGE
    here = lax.broadcasted_iota(jnp.int32, (tok, frame), 1)
    pool = jnp.where((here == start) | (here == start + 1), 0.5, 0.0).astype(BF16)
    m_high, m_rest = split_two(mix)
    weights = dot_nn(pool, m_high) + dot_nn(pool, m_rest)
    w_high, w_rest = split_two(weights)
    hid = dot_nn(w_high, c_high) + (dot_nn(w_high, c_rest) + dot_nn(w_rest, c_high))
    hid_ref[0] = hid
    factor = lax.rsqrt(jnp.mean(hid * hid, axis=-1, keepdims=True) + EPS)
    norm_ref[0] = (hid * factor * vectors[base + 5 : base + 6]).astype(BF16)


def front_forward(at, row_len, ids, pack, vocab, d_model):
    rows, _, frame = ids.shape
    extent = frame - 2 * EDGE
    tok = extent // 2
    pad = pack.shape[1]
    by_row = lambda r, *_: (r, 0, 0)
    return pl.pallas_call(
        functools.partial(front_kernel, vocab),
        grid_spec=pltpu.PrefetchScalarGridSpec(
            num_scalar_prefetch=2,
            grid=(rows,),
            in_specs=[
                pl.BlockSpec((1, 1, frame), by_row),
                pl.BlockSpec(pack.shape, lambda r, *_: (0, 0, 0)),
            ],
            out_specs=[
                pl.BlockSpec((1, tok, d_model), by_row),
                pl.BlockSpec((1, tok, d_model), by_row),
                pl.BlockSpec((1, frame, d_model), by_row),
                pl.BlockSpec((1, extent, d_model), by_row),
                pl.BlockSpec((1, 8, frame), by_row),
            ],
            scratch_shapes=[
                pltpu.VMEM((pad, d_model), BF16),
                pltpu.VMEM((frame, frame), BF16),
                pltpu.VMEM((frame, frame), BF16),
                pltpu.VMEM((frame, frame), BF16),
                pltpu.VMEM((frame + 2 * EDGE, d_model), F32),
            ],
        ),
        out_shape=[
            jax.ShapeDtypeStruct((rows, tok, d_model), F32),
            jax.ShapeDtypeStruct((rows, tok, d_model), BF16),
            jax.ShapeDtypeStruct((rows, frame, d_model), F32),
            jax.ShapeDtypeStruct((rows, extent, d_model), BF16),
            jax.ShapeDtypeStruct((rows, 8, frame), F32),
        ],
        compiler_params=pltpu.CompilerParams(vmem_limit_bytes=48 << 20),
        cost_estimate=pl.CostEstimate(flops=rows * 8 * frame * frame * d_model, bytes_accessed=rows * frame * d_model * 9, transcendentals=0),
        name="front",
    )(at, row_len, ids, pack)


def front_back_kernel(vocab, first_row, last_row, at_ref, len_ref, ids_ref, pack_ref, dhid_ref, low_ref, high_ref, conv_ref, mask_ref, share_ref, gain_one_ref, gain_two_ref, *refs):
    if last_row:
        rel_ref, refs = refs[0], refs[1:]
    if not first_row:
        before_ref, refs = refs[0], refs[2:]
    din_ref, grad_ref, wall_ref, tri_ref, quad_ref, pair_ref, dconv_ref, sum_ref = refs
    frame = ids_ref.shape[2]
    tok = dhid_ref.shape[0]
    extent = frame - 2 * EDGE
    first = at_ref[0] - EDGE
    pad = wall_ref.shape[0]

    unpack_front(pack_ref, wall_ref)
    for ref, size in ((pair_ref, 2), (tri_ref, 3), (quad_ref, 4)):
        ref[...] = same_block(first + 12 * EDGE, frame, size).astype(BF16)
    sum_ref[...] = jnp.zeros_like(sum_ref) if first_row else before_ref[...]
    limit = len_ref[0]
    low = vocab // 16 * 16
    vectors = wall_ref[low : -(-(vocab + 7) // 16) * 16, :].astype(F32)
    base = vocab - low
    shares = [share_ref[0, b : b + 1, :] for b in range(4)]
    one = (lax.broadcasted_iota(jnp.int32, (frame, frame), 0) == lax.broadcasted_iota(jnp.int32, (frame, frame), 1)).astype(F32)
    masks = [one] + [ref[...].astype(F32) * (1.0 / size) for ref, size in ((pair_ref, 2), (tri_ref, 3), (quad_ref, 4))]
    mix = functools.reduce(jnp.add, [m * s for m, s in zip(masks, shares)])
    start = 2 * lax.broadcasted_iota(jnp.int32, (frame, tok), 1) + EDGE
    here = lax.broadcasted_iota(jnp.int32, (frame, tok), 0)
    pool = jnp.where((here == start) | (here == start + 1), 0.5, 0.0).astype(BF16)
    rim_at = lax.broadcasted_iota(jnp.int32, (frame, 16), 1)
    rim_start = 2 * rim_at + jnp.where(rim_at < 8, EDGE - 16, EDGE + extent - 16)
    rim_here = lax.broadcasted_iota(jnp.int32, (frame, 16), 0)
    rim_pool = jnp.where((rim_here == rim_start) | (rim_here == rim_start + 1), 0.5, 0.0).astype(BF16)
    rims = jnp.concatenate([low_ref[...], high_ref[...]], axis=0)
    m_high, m_rest = split_two(mix)
    conv = conv_ref[0]
    c_high, c_rest = split_two(conv)
    d_conv = jnp.zeros(conv.shape, F32)
    cross = jnp.zeros((frame, frame), F32)
    for d_hid, spread in ((dhid_ref[...], pool), (rims, rim_pool)):
        d_high, d_rest = split_two(d_hid)
        weights = dot_nn(m_high, spread) + dot_nn(m_rest, spread)
        w_high, w_rest = split_two(weights)
        d_conv += dot_nn(w_high, d_high) + (dot_nn(w_high, d_rest) + dot_nn(w_rest, d_high))
        pairs = dot_nt(c_high, d_high) + (dot_nt(c_high, d_rest) + dot_nt(c_rest, d_high))
        cross += dot_half(dot_nt, pairs, spread)
    d_shares = [jnp.sum(m * cross, axis=0, keepdims=True) for m in masks]
    inner = functools.reduce(jnp.add, [s * d for s, d in zip(shares, d_shares)])
    d_single = jnp.sum(
        functools.reduce(jnp.add, [m * (s * (d - inner)) for m, s, d in zip(masks, shares, d_shares)]), axis=1, keepdims=True
    )
    own_col = lax.broadcasted_iota(jnp.int32, (frame, 1), 0)
    place_col = own_col + first
    live_col = ((place_col >= 0) & (place_col < limit)).astype(F32)
    own = ((own_col >= EDGE) & (own_col < frame - EDGE)).astype(F32)
    dconv_ref[...] = (d_conv + d_single * vectors[base + 4 : base + 5]) * live_col
    grad_score = jnp.sum(conv * (d_single * own), axis=0, keepdims=True)
    masked = mask_ref[0].astype(F32)
    d_masked = jnp.zeros(masked.shape, F32)
    for j in range(4):
        moved = dconv_ref[EDGE + 2 - j : EDGE + 2 - j + extent, :]
        d_masked += vectors[base + j : base + j + 1] * moved
        sum_ref[vocab + j : vocab + j + 1, :] += jnp.sum(masked * moved, axis=0, keepdims=True)
    sum_ref[vocab + 4 : vocab + 5, :] += grad_score
    d_in = (d_masked * live_col[EDGE : frame - EDGE]).astype(BF16)
    din_ref[0] = d_in
    ids = ids_ref[0][:, EDGE : frame - EDGE]
    emb_rows = -(-vocab // 8) * 8
    onehot = (lax.broadcasted_iota(jnp.int32, (emb_rows, extent), 0) == ids).astype(F32).astype(BF16)
    sum_ref[0:emb_rows, :] += dot_nn(onehot, d_in)

    sum_ref[vocab + 5 : vocab + 6, :] += gain_one_ref[...]
    sum_ref[vocab + 6 : vocab + 7, :] += gain_two_ref[...]
    if last_row:
        parts, _, share = grad_ref.shape
        for d in range(parts):
            grad_ref[d] = sum_ref[:, d * share : (d + 1) * share].astype(BF16)
            grad_ref[d, vocab + 7 : vocab + 7 + rel_ref.shape[0], :] = rel_ref[...].astype(BF16)
    else:
        grad_ref[...] = sum_ref[...]


def front_backward(at, row_len, ids, pack, d_hid, rims, conv, masked, shares, gains, rel, vocab, row, rows, before):
    frame = ids.shape[2]
    extent = frame - 2 * EDGE
    d_model = d_hid.shape[1]
    pad = pack.shape[1]
    args = [ids, pack, d_hid, *rims, conv, masked, shares, *gains] + ([rel] if row == rows - 1 else [])
    specs = [scalars(), scalars(), *in_vmem(args)]
    aliases = {}
    if before:
        specs += [whole(before[0]), pl.BlockSpec(memory_space=pl.ANY)]
        aliases = {len(specs) - 1: 0}
    grads = jax.ShapeDtypeStruct(pack.shape, BF16) if row == rows - 1 else jax.ShapeDtypeStruct((pad, d_model), F32)
    return pl.pallas_call(
        functools.partial(front_back_kernel, vocab, row == 0, row == rows - 1),
        grid=(1,),
        in_specs=specs,
        out_specs=[pl.BlockSpec((1, extent, d_model), lambda *_: (row, 0, 0)), whole(grads)],
        out_shape=[jax.ShapeDtypeStruct((rows, extent, d_model), BF16), grads],
        scratch_shapes=[
            pltpu.VMEM((pad, d_model), BF16),
            pltpu.VMEM((frame, frame), BF16),
            pltpu.VMEM((frame, frame), BF16),
            pltpu.VMEM((frame, frame), BF16),
            pltpu.VMEM((frame, d_model), F32),
            pltpu.VMEM((pad, d_model), F32),
        ],
        input_output_aliases=aliases,
        compiler_params=pltpu.CompilerParams(vmem_limit_bytes=56 << 20),
        cost_estimate=pl.CostEstimate(flops=16 * frame * frame * d_model, bytes_accessed=frame * d_model * 12, transcendentals=0),
        name="front_back",
    )(at, row_len, *args, *before)


def settle_kernel(vocab, x_ref, got_ref, emb_ref, conv_ref, vec_ref, rel_ref):
    total = x_ref[...] + got_ref[...].astype(F32)
    emb_ref[...] = total[:vocab]
    conv_ref[...] = total[vocab : vocab + 4]
    vec_ref[...] = total[vocab + 4 : vocab + 7]
    rel_ref[...] = total[vocab + 7 : vocab + 7 + rel_ref.shape[0]]


def settle(x, got, vocab, rel_rows):
    share = x.shape[1]
    outs = [jax.ShapeDtypeStruct((rows, share), F32) for rows in (vocab, 4, 3, rel_rows)]
    return pl.pallas_call(
        functools.partial(settle_kernel, vocab),
        grid=(1,),
        in_specs=in_vmem([x, got]),
        out_specs=in_vmem(outs),
        out_shape=outs,
        name="settle",
    )(x, got)


GELU_C = 0.7978845608
GELU_A = 0.044715


def pack_down(x):
    rows, third = x.shape[1], x.shape[2] // 3
    left, mid, right = x[..., :third], x[..., third : 2 * third], x[..., 2 * third :]
    return jnp.concatenate(
        [jnp.concatenate([left, right[:, : rows // 2]], axis=1), jnp.concatenate([mid, right[:, rows // 2 :]], axis=1)], axis=2
    )


def unpack_down(x):
    rows, third = x.shape[1] * 2 // 3, x.shape[2] // 2
    right = jnp.concatenate([x[:, rows:, :third], x[:, rows:, third:]], axis=1)
    return jnp.concatenate([x[:, :rows, :third], x[:, :rows, third:], right], axis=2)


def feed_kernel(nblk, rows, row, sizes, *refs):
    share, ff_cols, width, down_rows = sizes
    x_refs, cot_refs, rest_ref = refs[:nblk], refs[nblk : 2 * nblk], refs[2 * nblk]
    refs = refs[2 * nblk + 1 :]
    sums_in, outs_in = None, ()
    if row > 0:
        outs_in, sums_in, refs = refs[:nblk], refs[nblk : nblk + 2], refs[nblk + 2 :]
    outs, dnorms, grads = refs[:nblk], refs[nblk : 2 * nblk], refs[2 * nblk :]
    if row == rows - 1:
        pack_ref, sum_a, sum_b = grads
    else:
        sum_a, sum_b = grads
    parts = rest_ref.shape[0]
    w_in = rest_ref[:, :share, : 2 * ff_cols].reshape(parts * share, 2 * ff_cols)
    w_down = unpack_down(rest_ref[:, :, 2 * ff_cols :]).reshape(parts * down_rows, width)
    for b in range(nblk):
        x, cot = x_refs[b][...], cot_refs[b][row]
        both = dot_nn(x, w_in)
        gate, up = both[:, :ff_cols], both[:, ff_cols:]
        square = gate * gate
        turned = jnp.tanh(GELU_C * gate * (1.0 + GELU_A * square))
        half = 0.5 * (1.0 + turned)
        gelu = gate * half
        slope = half + (0.5 * GELU_C) * gate * (1.0 - turned * turned) * (1.0 + (3.0 * GELU_A) * square)
        hidden = (gelu * up).astype(BF16)
        if row > 0:
            outs[b][:row] = outs_in[b][...]
        outs[b][row] = dot_nn(hidden, w_down).astype(BF16)
        d_hidden = dot_nt(cot, w_down)
        d_both = jnp.concatenate([(d_hidden * up * slope).astype(BF16), (d_hidden * gelu).astype(BF16)], axis=1)
        dnorms[b][...] = dot_nt(d_both, w_in).astype(BF16)
        grad_a, grad_b = dot_tn(x, d_both), dot_tn(hidden, cot)
        if b == 0 and sums_in is None:
            sum_a[...] = grad_a
            sum_b[...] = grad_b
        elif b == 0:
            sum_a[...] = sums_in[0][...] + grad_a
            sum_b[...] = sums_in[1][...] + grad_b
        else:
            sum_a[...] += grad_a
            sum_b[...] += grad_b
    if row == rows - 1:
        pack_ref[:, :, : 2 * ff_cols] = sum_a[...].astype(BF16).reshape(parts, share, 2 * ff_cols)
        pack_ref[:, :, 2 * ff_cols :] = pack_down(sum_b[...].astype(BF16).reshape(parts, down_rows, width))


def feed(xs, cots, rest, before, row, sizes):
    nblk = len(xs)
    tok, d_model = xs[0].shape
    share, ff_cols, width, down_rows = sizes
    parts, rows = rest.shape[0], cots[0].shape[0]
    sum_shapes = [(d_model, 2 * ff_cols), (parts * down_rows, width)]
    outs = [jax.ShapeDtypeStruct((row + 1, tok, width), BF16)] * nblk + [jax.ShapeDtypeStruct((tok, d_model), BF16)] * nblk
    scratch = []
    if row == rows - 1:
        outs.append(jax.ShapeDtypeStruct(rest.shape, BF16))
        scratch = [pltpu.VMEM(s, F32) for s in sum_shapes]
    else:
        outs += [jax.ShapeDtypeStruct(s, F32) for s in sum_shapes]
    args = [*xs, *cots, rest, *before]
    flops = 2 * nblk * tok * d_model * ff_cols * 9
    got = pl.pallas_call(
        functools.partial(feed_kernel, nblk, rows, row, sizes),
        grid=(1,),
        in_specs=in_vmem(args),
        out_specs=in_vmem(outs),
        out_shape=outs,
        scratch_shapes=scratch,
        compiler_params=pltpu.CompilerParams(vmem_limit_bytes=56 << 20),
        cost_estimate=pl.CostEstimate(flops=flops, bytes_accessed=12 << 20, transcendentals=nblk * tok * ff_cols),
        name="feed",
    )(*args)
    return got[:nblk], got[nblk : 2 * nblk], got[2 * nblk :]


P = jax.sharding.PartitionSpec


def rims_of(x, width):
    size, length = lax.axis_size("seq"), x.shape[1]
    up = [(i, i + 1) for i in range(size - 1)]
    down = [(j, i) for i, j in up]
    before = lax.ppermute(x[:, length - width :], "seq", up)
    after = lax.ppermute(x[:, :width], "seq", down)
    return before, after


def flip_with(x, axis, bit):
    return lax.ppermute(x, axis, [(i, i ^ bit) for i in range(lax.axis_size(axis))])


def bits_of(axis):
    bits, bit = [], 1
    while bit < lax.axis_size(axis):
        bits.append(bit)
        bit *= 2
    return bits[::-1]


def after(x, *others):
    return lax.optimization_barrier((x,) + others)[0]


def places_of(n):
    places = [0]
    bit = n // 2
    while bit:
        places = places + [p ^ bit for p in places]
        bit //= 2
    return places


def swap_blocks(parts):
    return [part if bit == 0 else flip_with(part, "seq", bit) for part, bit in zip(parts, places_of(len(parts)))]


def gather_direct(x):
    return swap_blocks([x] * lax.axis_size("seq"))


def gather_first(x):
    blocks = [x]
    for bit in bits_of("seq")[:-1]:
        blocks = blocks + [flip_with(block, "seq", bit) for block in blocks]
    return blocks


def gather_last(blocks):
    return blocks + [flip_with(block, "seq", 1) for block in blocks]


def gather_two(x):
    return gather_last(gather_first(x))


def scatter_first(parts):
    half = len(parts) // 2
    got = [flip_with(part, "seq", 1) for part in parts[half:]]
    send = [(a.astype(F32) + b.astype(F32)).astype(BF16) for a, b in zip(parts[1:half], got[1:])]
    return [parts[0], got[0]], send


def scatter_last(own, send):
    return own + [flip_with(part, "seq", place) for part, place in zip(send, places_of(2 * len(send) + 2)[1:])]


def add_up(parts):
    return functools.reduce(jnp.add, [part.astype(F32) for part in parts])


def scatter_step(x, bit):
    axis = bits_of("dp").index(bit)
    low, high = lax.index_in_dim(x, 0, axis), lax.index_in_dim(x, 1, axis)
    upper = (lax.axis_index("dp") & bit) != 0
    keep, send = jnp.where(upper, high, low), jnp.where(upper, low, high)
    return keep, flip_with(send.astype(BF16), "dp", bit)


def swap_dp(x):
    return lax.all_to_all(x, "dp", split_axis=0, concat_axis=0, tiled=True)


def sum_parts(x):
    return jnp.sum(x.astype(F32), axis=0)


def gather_step(x, bit, *gate):
    axis = bits_of("dp").index(bit)
    other = flip_with(x, "dp", bit)
    other = after(other, *gate) if gate else other
    upper = (lax.axis_index("dp") & bit) != 0
    return jnp.concatenate([jnp.where(upper, other, x), jnp.where(upper, x, other)], axis=axis)


def gather_start(x):
    return x.reshape((1,) * len(bits_of("dp")) + x.shape)


def sum_step(x, bit):
    low = x.astype(BF16)
    return low.astype(F32) + flip_with(low, "seq", bit).astype(F32)


def sum_seq(x):
    for bit in bits_of("seq")[::-1]:
        x = sum_step(x, bit)
    return x


def in_order(blocks, me):
    n = len(blocks)
    bits = bits_of("seq")
    x = jnp.stack(blocks).reshape((2,) * len(bits) + blocks[0].shape)
    for at, bit in enumerate(bits[::-1]):
        upper = (me & bit) != 0
        x = jnp.where(upper, jnp.flip(x, at), x)
    x = x.transpose(tuple(range(len(bits)))[::-1] + tuple(range(len(bits), x.ndim)))
    return x.reshape((n,) + blocks[0].shape)


def on_device(
    byte_ids,
    lengths,
    deal_order,
    buckets,
    embedding,
    conv_w,
    score_w,
    gain_one,
    w_query,
    w_key,
    w_value,
    w_out,
    rel_bias,
    gain_two,
    w_gate,
    w_up,
    w_down,
    cotangent,
):
    n = lax.axis_size("seq")
    dp = lax.axis_size("dp")
    me = lax.axis_index("seq")
    rows_dev, extent = byte_ids.shape
    share, width = w_query.shape
    d_model = share * dp
    head_cols = width // n
    heads_dev = head_cols // DH
    ff_cols = w_gate.shape[1] // n
    down_rows = w_down.shape[0] // n
    tok = cotangent.shape[1]
    place = jnp.array(places_of(n), jnp.int32) ^ me

    vocab = embedding.shape[0]
    rel_rows = -(-rel_bias.size // share)
    pad_vocab = -(-(vocab + 7 + rel_rows) // 16) * 16
    front_pack = jnp.concatenate(
        [embedding, conv_w, score_w[None], gain_one[None], gain_two[None], jnp.zeros((pad_vocab - vocab - 7, share), BF16)], axis=0
    )

    def own_cols(weight):
        return lax.dynamic_slice_in_dim(weight, me * head_cols, head_cols, 1)

    qkv_pack = jnp.concatenate([own_cols(w_query), own_cols(w_key), own_cols(w_value), own_cols(w_out)], axis=1)
    front_all, qkv_w = gather_start(front_pack), gather_start(qkv_pack)
    up_bits = bits_of("dp")
    qkv_bits = up_bits[-1:] + up_bits[:-1]
    for at, bit in enumerate(up_bits):
        front_all = gather_step(front_all, bit)
        if at == 0:
            byte_ids, rel_in = (after(x, front_all) for x in (byte_ids, rel_bias))
        if at < len(up_bits) - 1:
            qkv_w = after(gather_step(qkv_w, qkv_bits[at]), front_all)
    front_all = front_all.reshape((dp,) + front_pack.shape)
    gain_first = front_all[:, vocab + 5].reshape(1, d_model).astype(F32)
    gain_second = front_all[:, vocab + 6].reshape(1, d_model).astype(F32)

    def own_ff(weight):
        return lax.dynamic_index_in_dim(weight.reshape(share, dp, n, down_rows), me, 2, keepdims=False).reshape(
            share, ff_cols
        )

    down_own = lax.dynamic_slice_in_dim(w_down, me * down_rows, down_rows, 0)
    rest_pack = jnp.concatenate([own_ff(w_gate), own_ff(w_up), pack_down(down_own[None])[0]], axis=1)
    offset = me * extent
    matches = deal_order[:, None] == jnp.arange(lengths.shape[0], dtype=jnp.int32)[None, :]
    row_len = jnp.sum(jnp.where(matches, lengths[None, :], 0), axis=1)
    rim_low, rim_high = rims_of(byte_ids, EDGE)
    ids = jnp.concatenate([rim_low, byte_ids, rim_high], axis=1)[:, None, :]
    at = jnp.full((1,), offset, jnp.int32)
    row_ids = range(rows_dev)
    lens = [row_len[r : r + 1] for r in row_ids]

    first_head = me * heads_dev
    bias_loc = lax.dynamic_slice_in_dim(rel_in, first_head, heads_dev, 1)
    offsets = jnp.concatenate([jnp.full((1,), -1, jnp.int32), buckets[::-1]])
    onehot = (offsets[None, :] == jnp.arange(rel_bias.shape[0], dtype=jnp.int32)[:, None]).astype(BF16)
    strips = bias_strips(jnp.einsum("nh,nx->hx", bias_loc, onehot, preferred_element_type=F32), n)

    cots = gather_two(cotangent)
    normed, h_zero, kept = [], [], []
    gate = (strips,)
    for r in row_ids:
        h, low, *rest = front_forward(at, lens[r], after(ids[r : r + 1], *gate), front_all, vocab, d_model)
        if r == 0:
            qkv_w = after(qkv_w, low)
        gate = (low,)
        h_zero.append(h[0])
        normed.append(low[0])
        kept.append(rest)
    low_one = [gather_two(low) if r == 0 else gather_direct(low) for r, low in enumerate(normed)]
    qkv_w = gather_step(qkv_w, qkv_bits[-1], *gate, low_one[0][1])
    qkv_w = qkv_w.reshape(d_model, 4 * head_cols)
    rest_all = lax.all_gather(after(rest_pack, qkv_w), "dp", axis=0, tiled=False)
    out_blocks = gather_first(qkv_w[:, 3 * head_cols :])
    qkv_w = qkv_w[:, : 3 * head_cols]
    gate = gate + tuple(cots)
    atts, qkvs, logs, mixed = [], [], [], []
    for r in row_ids:
        xs = [after(low_one[r][0], *gate)] + list(low_one[r][1:])
        att, qkv, log = attend(place, lens[r], xs, qkv_w, strips)
        gate = (qkv,)
        atts.append(att)
        qkvs.append(qkv)
        logs.append(log)
        mixed.append(swap_blocks([after(a, *mixed[r - 1]) for a in att] if r else att))
        if r == rows_dev - 1:
            out_blocks = gather_last([after(block, *gate) for block in out_blocks])
    w_out_all, h_one, lows = project(place, out_blocks, [[after(m[0], *gate)] + m[1:] for m in mixed], h_zero, gain_second)
    low_two = [gather_two(low) if r == 0 else gather_direct(low) for r, low in enumerate(lows)]
    sizes = (share, ff_cols, width, down_rows)
    d_norm_two, before = [], ()
    for r in row_ids:
        xs = [after(low_two[r][0], *gate)] + low_two[r][1:]
        ff_outs, d_norm, sums = feed(xs, cots, rest_all, before, r, sizes)
        before = (*ff_outs, *sums)
        gate = (d_norm[0],)
        if r:
            d_norm = [after(part, *d_norm_two[r - 1]) for part in d_norm]
        if r < rows_dev - 1:
            d_norm_two.append(swap_blocks(d_norm))
        else:
            two_own, two_send = scatter_first(d_norm)
            d_norm_two.append(scatter_last(two_own, two_send))
    ff_sum = lax.psum_scatter(sums[0], "dp", scatter_dimension=0, tiled=False)
    d_h_one, gains_two, earlier, d_norms, qkv_grad, d_revs = [], [], [], [], None, []
    for r in row_ids:
        last = r == rows_dev - 1
        adds = [after(d_norm_two[r][0], *gate)] + d_norm_two[r][1:]
        d_h, gain_grad, d_att, out_grad = project_back(
            place, adds, mixed[r], w_out_all, h_one[r], cotangent, r, gain_second, earlier, dp if last else 0
        )
        gate = (d_h,)
        earlier = earlier + [*mixed[r], out_grad]
        d_h_one.append(d_h)
        gains_two.append(gain_grad)
        douts = swap_blocks(d_att)
        if r == 0:
            ff_own, ff_send = scatter_first([after(ff_out, *gate) for ff_out in ff_outs])
            ff_whole = scatter_last(ff_own, ff_send)
            gate = gate + tuple(two_send) + tuple(ff_send)
        elif r == 1:
            gate = gate + tuple(ff_whole)
        d_norm, qkv_grad, d_rev = attend_back(
            place, lens[r], low_one[r], qkv_w, qkvs[r], atts[r], [after(douts[0], *gate)] + douts[1:], logs[r], strips,
            qkv_grad, dp if last else 0,
        )
        gate = (d_norm[0],)
        d_norms.append(d_norm)
        d_revs.append(d_rev)
    out_parts = swap_dp(out_grad)
    dp_bits = bits_of("dp")[::-1]
    qkv_sum = [qkv_grad.reshape((2,) * len(dp_bits) + qkv_grad.shape[1:])]
    d_rel_loc = jnp.einsum("nx,hx->nh", onehot.astype(F32), sum(d_revs), precision=lax.Precision.HIGHEST)
    d_rel = lax.dynamic_update_slice_in_dim(jnp.zeros(rel_bias.shape, F32), d_rel_loc, first_head, 1)
    d_rel = jnp.pad(d_rel.reshape(-1), (0, rel_rows * share - rel_bias.size)).reshape(rel_rows, share)

    d_first = [swap_blocks(d_norm) for d_norm in d_norms[:-1]]
    last_own, last_send = scatter_first([after(part, *d_first[-1]) for part in d_norms[-1]])
    d_first.append(scatter_last(last_own, last_send))
    seq_bits = bits_of("seq")[::-1]
    g_out = sum_parts(after(out_parts, *gate))
    front_grad = ()
    for r in row_ids:
        adds = [after(d_first[r][0], *gate)] + d_first[r][1:]
        d_h_zero, low_rim, high_rim, gain_grad = first_back(adds, h_zero[r], d_h_one[r], gain_first)
        size = lax.axis_size("seq")
        low_side = lax.ppermute(high_rim, "seq", [(i, i + 1) for i in range(size - 1)])
        high_side = lax.ppermute(low_rim, "seq", [(i + 1, i) for i in range(size - 1)])
        if dp_bits:
            qkv_sum = scatter_step(add_up([after(part, *gate) for part in qkv_sum]), dp_bits.pop(0))
        extra = (*last_send, g_out, ff_sum) if r == 0 else (g_out,)
        conv_out, masked, shares = kept[r]
        d_input, front_sum = front_backward(
            at, lens[r], ids[r : r + 1], front_all, after(d_h_zero, *extra), (low_side, high_side), conv_out, masked, shares,
            (gain_grad, gains_two[r]), d_rel, vocab, r, rows_dev, front_grad,
        )
        front_grad = (front_sum, d_input)
        gate = (front_sum,)
        if r == 0:
            ff_all = gather_first(ff_sum)
            ff_all = [ff_all[0]] + [after(block, *gate) for block in ff_all[1:]]
            gate = gate + tuple(ff_all[1:])
            ff_all = gather_last(ff_all)
            g_out = sum_step(after(g_out, *gate), seq_bits.pop(0))
    ff_all = [after(block, *gate) for block in ff_all]
    front_parts = swap_dp(front_sum)
    qkv_sum = add_up([after(part, *gate) for part in qkv_sum])
    while dp_bits:
        qkv_sum = add_up(scatter_step(qkv_sum, dp_bits.pop(0)))
    g_out = after(g_out, *gate)
    while seq_bits:
        g_out = sum_step(g_out, seq_bits.pop(0))
    tail = (g_out,)
    output = (jnp.stack([after(h, *tail) for h in h_one]) + add_up(ff_whole)).astype(BF16)
    ff_all = in_order([after(block, *tail) for block in ff_all], me)
    g_gu = ff_all[:, :, : 2 * ff_cols].reshape(n, share, 2, dp, down_rows)
    g_gu = g_gu.transpose(2, 1, 3, 0, 4).reshape(2, share, n * ff_cols).astype(F32)
    g_down = unpack_down(ff_all[:, :, 2 * ff_cols :]).reshape(n * down_rows, width).astype(F32)
    g_qkv = in_order(gather_two(qkv_sum.astype(BF16).reshape(share, 3, head_cols)), me)
    g_qkv = g_qkv.transpose(2, 1, 0, 3).reshape(3, share, width).astype(F32)
    front_sum = sum_parts(front_parts)
    front_bits = bits_of("seq")[::-1]
    for bit in front_bits[:-1]:
        front_sum = sum_step(front_sum, bit)
    front_low = front_sum.astype(BF16)
    g_emb, g_conv, g_vec, g_rel = settle(front_low.astype(F32), flip_with(front_low, "seq", front_bits[-1]), vocab, rel_rows)
    return (
        output,
        d_input,
        g_emb,
        g_conv,
        g_vec[0],
        g_vec[1],
        g_qkv[0],
        g_qkv[1],
        g_qkv[2],
        g_out,
        g_rel.reshape(-1)[: rel_bias.size].reshape(rel_bias.shape),
        g_vec[2],
        g_gu[0],
        g_gu[1],
        g_down,
    )


def solution(mesh):
    return jax.shard_map(
        on_device,
        mesh=mesh,
        in_specs=(
            P("dp", "seq"),
            P(),
            P("dp"),
            P(),
            P(None, "dp"),
            P(None, "dp"),
            P("dp"),
            P("dp"),
            P("dp", None),
            P("dp", None),
            P("dp", None),
            P("dp", None),
            P(),
            P("dp"),
            P("dp", None),
            P("dp", None),
            P("dp", None),
            P("dp", "seq", None),
        ),
        out_specs=(
            P("dp", "seq", None),
            P("dp", "seq", None),
            P(None, "dp"),
            P(None, "dp"),
            P("dp"),
            P("dp"),
            P("dp", None),
            P("dp", None),
            P("dp", None),
            P("dp", None),
            P(),
            P("dp"),
            P("dp", None),
            P("dp", None),
            P("dp", None),
        ),
        check_vma=False,
    )
```

```python
import functools
import jax, jax.numpy as jnp
from jax import lax
from jax.experimental import pallas as pl
from jax.experimental.pallas import tpu as pltpu
DH=64
NEG=-1e9
F32, BF16 = jnp.float32, jnp.bfloat16


def dot_nt(a, b):
    return lax.dot_general(a, b, (((1,), (1,)), ((), ())), preferred_element_type=F32)


def dot_nn(a, b):
    return lax.dot_general(a, b, (((1,), (0,)), ((), ())), preferred_element_type=F32)


def tile_at(place_ref, kb, qb, nblk):
    return jnp.clip(place_ref[kb] - place_ref[qb], -2, 2) + 2


def strip_kernel(nblk, rev_ref, strip_ref):
    heads, _, blk = strip_ref.shape
    for head in range(heads):
        for part in range(5):
            low = (nblk + 1 - part) * blk
            here = slice(part * blk, (part + 1) * blk)
            if part in (0, 4):
                strip_ref[head, here, :] = jnp.broadcast_to(rev_ref[head : head + 1, low + blk : low + blk + 1], (blk, blk))
                continue
            segment = jnp.broadcast_to(rev_ref[head : head + 1, low : low + 2 * blk], (blk, 2 * blk))
            strip_ref[head, here, :] = pltpu.roll(segment, 0, 1, stride=1, stride_axis=0)[:, blk:]


def bias_strips(rev, nblk):
    heads, width = rev.shape
    blk = width // (2 * nblk)
    return pl.pallas_call(
        functools.partial(strip_kernel, nblk),
        out_shape=jax.ShapeDtypeStruct((heads, 5 * blk, blk), F32),
        compiler_params=pltpu.CompilerParams(vmem_limit_bytes=32 << 20),
        name="strips",
    )(rev)


def key_side(key, ok_col):
    rows = key.shape[0]
    lane = lax.broadcasted_iota(jnp.int32, (rows, DH), 1)
    extra = jnp.where(lane == 0, ok_col, 0.0).astype(BF16)
    return jnp.concatenate([key, extra], axis=1)


def query_side(query):
    rows = query.shape[0]
    lane = lax.broadcasted_iota(jnp.int32, (rows, DH), 1)
    return jnp.concatenate([query, jnp.where(lane == 0, 1.0, 0.0).astype(BF16)], axis=1)


def mask_column(place_ref, limit, blk, nblk):
    cols = []
    for b in range(nblk):
        at = place_ref[b] * blk + lax.broadcasted_iota(jnp.int32, (blk, DH), 0)
        cols.append(jnp.where(2 * at < limit, 0.0, NEG))
    return jnp.concatenate(cols, axis=0)


def dot_tn(a, b):
    return lax.dot_general(a, b, (((0,), (0,)), ((), ())), preferred_element_type=F32)


def whole(arg):
    return pl.BlockSpec(arg.shape, lambda *_: (0,) * len(arg.shape), pipeline_mode=pl.Buffered(1))


def in_vmem(args):
    return [whole(arg) for arg in args]


def scalars():
    return pl.BlockSpec(memory_space=pltpu.SMEM)


def attend_kernel(heads, nblk, place_ref, len_ref, *refs):
    xs, (w_ref, strip_ref), refs = refs[:nblk], refs[nblk : nblk + 2], refs[nblk + 2 :]
    outs, (qkv_ref, log_ref, att_ref, kaug_ref, qaug_ref, vt_ref) = refs[:nblk], refs[nblk:]
    blk = xs[0].shape[0]
    for b in range(nblk):
        qkv_ref[b * blk : (b + 1) * blk, :] = dot_nn(xs[b][...], w_ref[:, : qkv_ref.shape[1]]).astype(BF16)
    ok_col = mask_column(place_ref, len_ref[0], blk, nblk)
    width = heads * DH
    for head in range(heads):
        at = head * DH
        qaug_ref[...] = query_side(qkv_ref[:, at : at + DH])
        kaug_ref[...] = key_side(qkv_ref[:, width + at : width + at + DH], ok_col)
        vt_ref[...] = qkv_ref[:, 2 * width + at : 2 * width + at + DH].T

        def one_block(qb, carry):
            q_at = pl.multiple_of(qb * blk, blk)
            query = qaug_ref[pl.ds(q_at, blk), :]
            parts = []
            for kb in range(nblk):
                m_at = pl.multiple_of(tile_at(place_ref, kb, qb, nblk) * blk, blk)
                parts.append(dot_nt(kaug_ref[kb * blk : (kb + 1) * blk, :], query) + strip_ref[head, pl.ds(m_at, blk), :])
            top = functools.reduce(jnp.maximum, [jnp.max(p, axis=0, keepdims=True) for p in parts])
            total = jnp.zeros((1, blk), F32)
            acc = jnp.zeros((DH, blk), F32)
            for kb in range(nblk):
                weight = jnp.exp(parts[kb] - top)
                total += jnp.sum(weight, axis=0, keepdims=True)
                acc += dot_nn(vt_ref[:, kb * blk : (kb + 1) * blk], weight.astype(BF16))
            att_ref[pl.ds(q_at, blk), at : at + DH] = (acc / total).T.astype(BF16)
            log_ref[head, pl.ds(qb, 1), :] = top + jnp.log(total)
            return carry

        lax.fori_loop(0, nblk, one_block, 0, unroll=2)
    for b in range(nblk):
        outs[b][...] = att_ref[b * blk : (b + 1) * blk, :]


def attend(place, row_len, xs, w_qkv, strips):
    nblk = len(xs)
    blk = xs[0].shape[0]
    heads = strips.shape[0]
    tokens = nblk * blk
    outs = [jax.ShapeDtypeStruct((blk, heads * DH), BF16)] * nblk + [
        jax.ShapeDtypeStruct((tokens, 3 * heads * DH), BF16),
        jax.ShapeDtypeStruct((heads, nblk, blk), F32),
    ]
    args = [*xs, w_qkv, strips]
    got = pl.pallas_call(
        functools.partial(attend_kernel, heads, nblk),
        grid=(1,),
        in_specs=[scalars(), scalars(), *in_vmem(args)],
        out_specs=in_vmem(outs),
        out_shape=outs,
        scratch_shapes=[
            pltpu.VMEM((tokens, heads * DH), BF16),
            pltpu.VMEM((tokens, 2 * DH), BF16),
            pltpu.VMEM((tokens, 2 * DH), BF16),
            pltpu.VMEM((DH, tokens), BF16),
        ],
        compiler_params=pltpu.CompilerParams(vmem_limit_bytes=48 << 20),
        cost_estimate=pl.CostEstimate(flops=48 * heads * tokens * tokens * DH, bytes_accessed=8 << 20, transcendentals=heads * tokens * tokens),
        name="attend",
    )(place, row_len, *args)
    return got[:nblk], got[nblk], got[nblk + 1]


def attend_back_kernel(heads, nblk, first, final, place_ref, len_ref, *refs):
    xs, (w_ref, qkv_ref), refs = refs[:nblk], refs[nblk : nblk + 2], refs[nblk + 2 :]
    os, dos, (log_ref, strip_ref), refs = refs[:nblk], refs[nblk : 2 * nblk], refs[2 * nblk : 2 * nblk + 2], refs[2 * nblk + 2 :]
    sum_in = None
    if not first:
        sum_in, refs = refs[0], refs[1:]
    dns, (sum_ref, drev_ref), refs = refs[:nblk], refs[nblk : nblk + 2], refs[nblk + 2 :]
    grads_ref, kaug_ref, qaug_ref, kt_ref, dk_ref, dv_ref, o_ref, do_ref, dqkv_ref = refs
    blk = xs[0].shape[0]
    for b in range(nblk):
        o_ref[b * blk : (b + 1) * blk, :] = os[b][...]
        do_ref[b * blk : (b + 1) * blk, :] = dos[b][...]
    ok_col = mask_column(place_ref, len_ref[0], blk, nblk)
    width = heads * DH
    for head in range(heads):
        grads_ref[head] = jnp.zeros(grads_ref.shape[1:], F32)
        at = head * DH
        qaug_ref[...] = query_side(qkv_ref[:, at : at + DH])
        key = qkv_ref[:, width + at : width + at + DH]
        kaug_ref[...] = key_side(key, ok_col)
        kt_ref[...] = key.T
        dk_ref[...] = jnp.zeros_like(dk_ref)
        dv_ref[...] = jnp.zeros_like(dv_ref)

        def one_block(qb, carry):
            q_at = pl.multiple_of(qb * blk, blk)
            query = qaug_ref[pl.ds(q_at, blk), :]
            dout = do_ref[pl.ds(q_at, blk), at : at + DH]
            prod = dout.astype(F32) * o_ref[pl.ds(q_at, blk), at : at + DH].astype(F32)
            inner = jnp.sum(prod.T, axis=0, keepdims=True)
            log_row = log_ref[head, pl.ds(qb, 1), :]
            dqt = jnp.zeros((DH, blk), F32)
            for kb in range(nblk):
                here = slice(kb * blk, (kb + 1) * blk)
                m_at = pl.multiple_of(tile_at(place_ref, kb, qb, nblk) * blk, blk)
                score = dot_nt(kaug_ref[here, :], query) + strip_ref[head, pl.ds(m_at, blk), :]
                prob = jnp.exp(score - log_row)
                d_prob = dot_nt(qkv_ref[here, 2 * width + at : 2 * width + at + DH], dout)
                d_score = prob * (d_prob - inner)
                low = d_score.astype(BF16)
                grads_ref[head, pl.ds(m_at, blk), :] += d_score
                dv_ref[here, :] += dot_nn(prob.astype(BF16), dout)
                dk_ref[here, :] += dot_nn(low, query[:, :DH])
                dqt += dot_nn(kt_ref[:, here], low)
            dqkv_ref[pl.ds(q_at, blk), at : at + DH] = dqt.T.astype(BF16)
            return carry

        [one_block(qb, 0) for qb in range(nblk)]
        dqkv_ref[:, width + at : width + at + DH] = dk_ref[...].astype(BF16)
        dqkv_ref[:, 2 * width + at : 2 * width + at + DH] = dv_ref[...].astype(BF16)

    total = None
    for b in range(nblk):
        here = dqkv_ref[b * blk : (b + 1) * blk, :]
        dns[b][...] = dot_nt(here, w_ref[:, : here.shape[1]]).astype(BF16)
        grad = dot_tn(xs[b][...], here)
        total = grad if total is None else total + grad
    if not first:
        total += sum_in[...]
    sum_ref[...] = total.astype(BF16).reshape(sum_ref.shape) if final else total

    flip = (
        lax.broadcasted_iota(jnp.int32, (blk, blk), 0) + lax.broadcasted_iota(jnp.int32, (blk, blk), 1) == blk - 1
    ).astype(F32).astype(BF16)
    drev_ref[...] = jnp.zeros_like(drev_ref)
    for head in range(heads):
        for part in range(5):
            low = (nblk + 1 - part) * blk
            grad = grads_ref[head, part * blk : (part + 1) * blk, :]
            if part in (0, 4):
                whole = jnp.sum(jnp.sum(grad, axis=0, keepdims=True), axis=1, keepdims=True)
                drev_ref[head : head + 1, low + blk : low + blk + 1] += whole
                continue
            high = grad.astype(BF16)
            rest = (grad - high.astype(F32)).astype(BF16)
            turned = dot_nn(flip, high) + dot_nn(flip, rest)
            wide = jnp.concatenate([jnp.zeros((blk, blk), F32), turned], axis=1)
            moved = pltpu.roll(wide, blk + 1, 1, stride=1, stride_axis=0)
            drev_ref[head : head + 1, low : low + 2 * blk] += jnp.sum(moved, axis=0, keepdims=True)


def attend_back(place, row_len, xs, w_qkv, qkv, outs, douts, logs, strips, sum_in, parts):
    nblk = len(xs)
    blk, d_model = xs[0].shape
    heads = strips.shape[0]
    tokens = nblk * blk
    cols = 3 * heads * DH
    args = [*xs, w_qkv, qkv, *outs, *douts, logs, strips] + ([] if sum_in is None else [sum_in])
    sum_shape = jax.ShapeDtypeStruct((parts, d_model // parts, cols), BF16) if parts else jax.ShapeDtypeStruct((d_model, cols), F32)
    shapes = [jax.ShapeDtypeStruct((blk, d_model), BF16)] * nblk + [sum_shape, jax.ShapeDtypeStruct((heads, 2 * tokens), F32)]
    got = pl.pallas_call(
        functools.partial(attend_back_kernel, heads, nblk, sum_in is None, bool(parts)),
        grid=(1,),
        in_specs=[scalars(), scalars(), *in_vmem(args)],
        out_specs=in_vmem(shapes),
        out_shape=shapes,
        scratch_shapes=[
            pltpu.VMEM((heads, 5 * blk, blk), F32),
            pltpu.VMEM((tokens, 2 * DH), BF16),
            pltpu.VMEM((tokens, 2 * DH), BF16),
            pltpu.VMEM((DH, tokens), BF16),
            pltpu.VMEM((tokens, DH), F32),
            pltpu.VMEM((tokens, DH), F32),
            pltpu.VMEM((tokens, heads * DH), BF16),
            pltpu.VMEM((tokens, heads * DH), BF16),
            pltpu.VMEM((tokens, cols), BF16),
        ],
        compiler_params=pltpu.CompilerParams(vmem_limit_bytes=56 << 20),
        cost_estimate=pl.CostEstimate(flops=120 * heads * tokens * tokens * DH, bytes_accessed=16 << 20, transcendentals=heads * tokens * tokens),
        name="attend_back",
    )(place, row_len, *args)
    return got[:nblk], got[nblk], got[nblk + 1]


EPS = 1e-06


def project_kernel(nblk, rows, place_ref, *refs):
    cols_refs, refs = refs[:nblk], refs[nblk:]
    atts, refs = refs[: rows * nblk], refs[rows * nblk :]
    hids, gain_ref, w_ref, outs = refs[:rows], refs[rows], refs[rows + 1], refs[rows + 2 :]
    cols = cols_refs[0].shape[1]
    for b in range(nblk):
        for g in range(nblk):

            @pl.when(place_ref[b] == g)
            def _():
                w_ref[:, g * cols : (g + 1) * cols] = cols_refs[b][...]

    for r in range(rows):
        hid = hids[r][...]
        for b in range(nblk):
            here = pl.ds(pl.multiple_of(place_ref[b] * cols, 16), cols)
            hid += dot_nn(atts[r * nblk + b][...], w_ref[here, :])
        outs[2 * r][...] = hid
        factor = lax.rsqrt(jnp.mean(hid * hid, axis=-1, keepdims=True) + EPS)
        outs[2 * r + 1][...] = (hid * factor * gain_ref[...]).astype(BF16)


def project(place, w_blocks, atts, hids, gain):
    rows, nblk = len(atts), len(w_blocks)
    width = w_blocks[0].shape[0]
    args = [*w_blocks, *[block for row in atts for block in row], *hids, gain]
    outs = [jax.ShapeDtypeStruct((width, hids[0].shape[1]), BF16)]
    for hid in hids:
        outs += [jax.ShapeDtypeStruct(hid.shape, F32), jax.ShapeDtypeStruct(hid.shape, BF16)]
    got = pl.pallas_call(
        functools.partial(project_kernel, nblk, rows),
        grid=(1,),
        in_specs=[scalars(), *in_vmem(args)],
        out_specs=in_vmem(outs),
        out_shape=outs,
        compiler_params=pltpu.CompilerParams(vmem_limit_bytes=60 << 20),
        cost_estimate=pl.CostEstimate(flops=4 * rows * hids[0].shape[0] * width * width, bytes_accessed=3 << 20, transcendentals=0),
        name="project",
    )(place, *args)
    return got[0], got[1::2], got[2::2]


def norm_back(hid, gain, d_norm):
    factor = lax.rsqrt(jnp.mean(hid * hid, axis=-1, keepdims=True) + EPS)
    scaled = hid * factor
    weighted = d_norm * gain
    inner = jnp.mean(scaled * weighted, axis=-1, keepdims=True)
    return factor * (weighted - scaled * inner), jnp.sum(d_norm * scaled, axis=0, keepdims=True)


def project_back_kernel(nblk, pieces, row, final, place_ref, *refs):
    adds, atts, refs = refs[:pieces], refs[pieces : pieces + nblk], refs[pieces + nblk :]
    (w_ref, hid_ref, cot_ref, gain_ref), refs = refs[:4], refs[4:]
    earlier, refs = refs[: row * (nblk + 1)], refs[row * (nblk + 1) :]
    dhid_ref, gain_out, datts, sum_ref, acc_ref = refs[0], refs[1], refs[2 : 2 + nblk], refs[2 + nblk], refs[3 + nblk]
    d_norm = adds[0][...].astype(F32)
    for add in adds[1:]:
        d_norm += add[...].astype(F32)
    back, gain_grad = norm_back(hid_ref[...], gain_ref[...], d_norm)
    gain_out[...] = gain_grad
    d_hid = cot_ref[row].astype(F32) + back
    dhid_ref[...] = d_hid
    branch = d_hid.astype(BF16)
    cols = atts[0].shape[1]
    for b in range(nblk):
        here = pl.ds(pl.multiple_of(place_ref[b] * cols, 16), cols)
        datts[b][...] = dot_nt(branch, w_ref[here, :]).astype(BF16)
        if final:
            grad = dot_tn(atts[b][...], branch)
            for r in range(row):
                grad += dot_tn(earlier[r * (nblk + 1) + b][...], earlier[r * (nblk + 1) + nblk][...])
            acc_ref[here, :] = grad
    sum_ref[...] = acc_ref[...].astype(BF16).reshape(sum_ref.shape) if final else branch


def project_back(place, adds, atts, w_out, hid, cot, row, gain, earlier, parts):
    nblk = len(atts)
    blk, cols = atts[0].shape
    width, d_model = w_out.shape
    args = [*adds, *atts, w_out, hid, cot, gain, *earlier]
    sum_shape = jax.ShapeDtypeStruct((parts, width // parts, d_model) if parts else (blk, d_model), BF16)
    outs = [jax.ShapeDtypeStruct(hid.shape, F32), jax.ShapeDtypeStruct((1, d_model), F32)]
    outs += [jax.ShapeDtypeStruct((blk, cols), BF16)] * nblk + [sum_shape]
    got = pl.pallas_call(
        functools.partial(project_back_kernel, nblk, len(adds), row, bool(parts)),
        grid=(1,),
        in_specs=[scalars(), *in_vmem(args)],
        out_specs=in_vmem(outs),
        out_shape=outs,
        scratch_shapes=[pltpu.VMEM((width, d_model), F32)],
        compiler_params=pltpu.CompilerParams(vmem_limit_bytes=60 << 20),
        cost_estimate=pl.CostEstimate(flops=8 * blk * width * d_model, bytes_accessed=6 << 20, transcendentals=0),
        name="project_back",
    )(place, *args)
    return got[0], got[1], got[2 : 2 + nblk], got[2 + nblk]


def first_back_kernel(pieces, *refs):
    adds, (hid_ref, dhid_ref, gain_ref, out_ref, low_ref, high_ref, gain_out) = refs[:pieces], refs[pieces:]
    d_norm = adds[0][...].astype(F32)
    for add in adds[1:]:
        d_norm += add[...].astype(F32)
    back, gain_grad = norm_back(hid_ref[...], gain_ref[...], d_norm)
    gain_out[...] = gain_grad
    d_hid = dhid_ref[...] + back
    out_ref[...] = d_hid
    low_ref[...] = d_hid[:8]
    high_ref[...] = d_hid[-8:]


def first_back(adds, hid, d_hid, gain):
    args = [*adds, hid, d_hid, gain]
    d_model = hid.shape[1]
    outs = [jax.ShapeDtypeStruct(s, F32) for s in (hid.shape, (8, d_model), (8, d_model), (1, d_model))]
    return pl.pallas_call(
        functools.partial(first_back_kernel, len(adds)),
        grid=(1,),
        in_specs=in_vmem(args),
        out_specs=in_vmem(outs),
        out_shape=outs,
        compiler_params=pltpu.CompilerParams(vmem_limit_bytes=32 << 20),
        cost_estimate=pl.CostEstimate(flops=20 * hid.shape[0] * d_model, bytes_accessed=4 << 20, transcendentals=0),
        name="first_back",
    )(*args)


EDGE = 8


def split_two(x):
    high = x.astype(BF16)
    return high, (x - high.astype(F32)).astype(BF16)


def dot_fine(dot, a, b):
    a_high, a_rest = split_two(a)
    b_high, b_rest = split_two(b)
    return dot(a_high, b_high) + (dot(a_high, b_rest) + dot(a_rest, b_high))


def dot_half(dot, a, b_low):
    a_high, a_rest = split_two(a)
    return dot(a_high, b_low) + dot(a_rest, b_low)


def same_block(first, frame, size):
    def group(axis, shape):
        place = lax.broadcasted_iota(jnp.int32, shape, axis) + first
        return jnp.floor((place.astype(F32) + 0.5) * (1.0 / size))

    return (group(0, (frame, 1)) == group(1, (1, frame))).astype(F32)


def unpack_front(pack_ref, wall_ref):
    parts, _, share = pack_ref.shape
    for d in range(parts):
        wall_ref[:, d * share : (d + 1) * share] = pack_ref[d]


def front_kernel(vocab, at_ref, len_ref, ids_ref, pack_ref, hid_ref, norm_ref, conv_ref, mask_ref, share_ref, wall_ref, tri_ref, quad_ref, pair_ref, x_ref):
    row = pl.program_id(0)
    frame = ids_ref.shape[2]
    tok = hid_ref.shape[1]
    first = at_ref[0] - EDGE

    @pl.when(row == 0)
    def _():
        unpack_front(pack_ref, wall_ref)
        for ref, size in ((pair_ref, 2), (tri_ref, 3), (quad_ref, 4)):
            ref[...] = same_block(first + 12 * EDGE, frame, size).astype(BF16)

    limit = len_ref[row]
    pad = wall_ref.shape[0]
    place_row = lax.broadcasted_iota(jnp.int32, (1, frame), 1) + first
    live_row = (place_row >= 0) & (place_row < limit)
    ids = jnp.where(live_row, ids_ref[0], -1)
    onehot = (lax.broadcasted_iota(jnp.int32, (pad, frame), 0) == ids).astype(F32).astype(BF16)
    masked = lax.dot_general(onehot, wall_ref[...], (((0,), (0,)), ((), ())), preferred_element_type=F32)
    mask_ref[0] = masked[EDGE : frame - EDGE].astype(BF16)
    x_ref[0:EDGE, :] = jnp.zeros((EDGE, masked.shape[1]), F32)
    x_ref[EDGE : EDGE + frame, :] = masked
    x_ref[EDGE + frame :, :] = jnp.zeros((EDGE, masked.shape[1]), F32)
    low = vocab // 16 * 16
    vectors = wall_ref[low : -(-(vocab + 7) // 16) * 16, :].astype(F32)
    base = vocab - low
    place_col = lax.broadcasted_iota(jnp.int32, (frame, 1), 0) + first
    live_col = ((place_col >= 0) & (place_col < limit)).astype(F32)
    conv = vectors[base : base + 1] * x_ref[EDGE - 2 : EDGE - 2 + frame, :]
    for j in range(1, 4):
        conv += vectors[base + j : base + j + 1] * x_ref[EDGE - 2 + j : EDGE - 2 + j + frame, :]
    conv = conv * live_col
    conv_ref[0] = conv
    c_high, c_rest = split_two(conv)
    score_w = jnp.broadcast_to(vectors[base + 4 : base + 5], (8, conv.shape[1])).astype(BF16)
    single = (dot_nt(score_w, c_high) + dot_nt(score_w, c_rest))[0:1]
    s_high = single.astype(BF16).astype(F32)
    s_mid = (single - s_high).astype(BF16).astype(F32)
    stack = jnp.concatenate([s_high, s_mid, single - s_high - s_mid, jnp.zeros((5, frame), F32)], axis=0).astype(BF16)
    scores = [single]
    for ref, size in ((pair_ref, 2), (tri_ref, 3), (quad_ref, 4)):
        scores.append(jnp.sum(dot_nn(stack, ref[...]), axis=0, keepdims=True) * (1.0 / size))
    top = functools.reduce(jnp.maximum, scores)
    raw = [jnp.exp(s - top) for s in scores]
    total = raw[0] + raw[1] + raw[2] + raw[3]
    shares = jnp.concatenate([r / total for r in raw] + [jnp.zeros((4, frame), F32)], axis=0)
    share_ref[0] = shares
    cols = shares.T
    one = (lax.broadcasted_iota(jnp.int32, (frame, frame), 0) == lax.broadcasted_iota(jnp.int32, (frame, frame), 1))
    mix = jnp.where(one, cols[:, 0:1], 0.0)
    for at, (ref, size) in enumerate(((pair_ref, 2), (tri_ref, 3), (quad_ref, 4))):
        mix += ref[...].astype(F32) * (cols[:, at + 1 : at + 2] * (1.0 / size))
    start = 2 * lax.broadcasted_iota(jnp.int32, (tok, frame), 0) + EDGE
    here = lax.broadcasted_iota(jnp.int32, (tok, frame), 1)
    pool = jnp.where((here == start) | (here == start + 1), 0.5, 0.0).astype(BF16)
    m_high, m_rest = split_two(mix)
    weights = dot_nn(pool, m_high) + dot_nn(pool, m_rest)
    w_high, w_rest = split_two(weights)
    hid = dot_nn(w_high, c_high) + (dot_nn(w_high, c_rest) + dot_nn(w_rest, c_high))
    hid_ref[0] = hid
    factor = lax.rsqrt(jnp.mean(hid * hid, axis=-1, keepdims=True) + EPS)
    norm_ref[0] = (hid * factor * vectors[base + 5 : base + 6]).astype(BF16)


def front_forward(at, row_len, ids, pack, vocab, d_model):
    rows, _, frame = ids.shape
    extent = frame - 2 * EDGE
    tok = extent // 2
    pad = pack.shape[1]
    by_row = lambda r, *_: (r, 0, 0)
    return pl.pallas_call(
        functools.partial(front_kernel, vocab),
        grid_spec=pltpu.PrefetchScalarGridSpec(
            num_scalar_prefetch=2,
            grid=(rows,),
            in_specs=[
                pl.BlockSpec((1, 1, frame), by_row),
                pl.BlockSpec(pack.shape, lambda r, *_: (0, 0, 0)),
            ],
            out_specs=[
                pl.BlockSpec((1, tok, d_model), by_row),
                pl.BlockSpec((1, tok, d_model), by_row),
                pl.BlockSpec((1, frame, d_model), by_row),
                pl.BlockSpec((1, extent, d_model), by_row),
                pl.BlockSpec((1, 8, frame), by_row),
            ],
            scratch_shapes=[
                pltpu.VMEM((pad, d_model), BF16),
                pltpu.VMEM((frame, frame), BF16),
                pltpu.VMEM((frame, frame), BF16),
                pltpu.VMEM((frame, frame), BF16),
                pltpu.VMEM((frame + 2 * EDGE, d_model), F32),
            ],
        ),
        out_shape=[
            jax.ShapeDtypeStruct((rows, tok, d_model), F32),
            jax.ShapeDtypeStruct((rows, tok, d_model), BF16),
            jax.ShapeDtypeStruct((rows, frame, d_model), F32),
            jax.ShapeDtypeStruct((rows, extent, d_model), BF16),
            jax.ShapeDtypeStruct((rows, 8, frame), F32),
        ],
        compiler_params=pltpu.CompilerParams(vmem_limit_bytes=48 << 20),
        cost_estimate=pl.CostEstimate(flops=rows * 8 * frame * frame * d_model, bytes_accessed=rows * frame * d_model * 9, transcendentals=0),
        name="front",
    )(at, row_len, ids, pack)


def front_back_kernel(vocab, first_row, last_row, at_ref, len_ref, ids_ref, pack_ref, dhid_ref, low_ref, high_ref, conv_ref, mask_ref, share_ref, gain_one_ref, gain_two_ref, *refs):
    if last_row:
        rel_ref, refs = refs[0], refs[1:]
    if not first_row:
        before_ref, refs = refs[0], refs[2:]
    din_ref, grad_ref, wall_ref, tri_ref, quad_ref, pair_ref, dconv_ref, sum_ref = refs
    frame = ids_ref.shape[2]
    tok = dhid_ref.shape[0]
    extent = frame - 2 * EDGE
    first = at_ref[0] - EDGE
    pad = wall_ref.shape[0]

    unpack_front(pack_ref, wall_ref)
    for ref, size in ((pair_ref, 2), (tri_ref, 3), (quad_ref, 4)):
        ref[...] = same_block(first + 12 * EDGE, frame, size).astype(BF16)
    sum_ref[...] = jnp.zeros_like(sum_ref) if first_row else before_ref[...]
    limit = len_ref[0]
    low = vocab // 16 * 16
    vectors = wall_ref[low : -(-(vocab + 7) // 16) * 16, :].astype(F32)
    base = vocab - low
    shares = [share_ref[0, b : b + 1, :] for b in range(4)]
    one = (lax.broadcasted_iota(jnp.int32, (frame, frame), 0) == lax.broadcasted_iota(jnp.int32, (frame, frame), 1)).astype(F32)
    masks = [one] + [ref[...].astype(F32) * (1.0 / size) for ref, size in ((pair_ref, 2), (tri_ref, 3), (quad_ref, 4))]
    mix = functools.reduce(jnp.add, [m * s for m, s in zip(masks, shares)])
    start = 2 * lax.broadcasted_iota(jnp.int32, (frame, tok), 1) + EDGE
    here = lax.broadcasted_iota(jnp.int32, (frame, tok), 0)
    pool = jnp.where((here == start) | (here == start + 1), 0.5, 0.0).astype(BF16)
    rim_at = lax.broadcasted_iota(jnp.int32, (frame, 16), 1)
    rim_start = 2 * rim_at + jnp.where(rim_at < 8, EDGE - 16, EDGE + extent - 16)
    rim_here = lax.broadcasted_iota(jnp.int32, (frame, 16), 0)
    rim_pool = jnp.where((rim_here == rim_start) | (rim_here == rim_start + 1), 0.5, 0.0).astype(BF16)
    rims = jnp.concatenate([low_ref[...], high_ref[...]], axis=0)
    m_high, m_rest = split_two(mix)
    conv = conv_ref[0]
    c_high, c_rest = split_two(conv)
    d_conv = jnp.zeros(conv.shape, F32)
    cross = jnp.zeros((frame, frame), F32)
    for d_hid, spread in ((dhid_ref[...], pool), (rims, rim_pool)):
        d_high, d_rest = split_two(d_hid)
        weights = dot_nn(m_high, spread) + dot_nn(m_rest, spread)
        w_high, w_rest = split_two(weights)
        d_conv += dot_nn(w_high, d_high) + (dot_nn(w_high, d_rest) + dot_nn(w_rest, d_high))
        pairs = dot_nt(c_high, d_high) + (dot_nt(c_high, d_rest) + dot_nt(c_rest, d_high))
        cross += dot_half(dot_nt, pairs, spread)
    d_shares = [jnp.sum(m * cross, axis=0, keepdims=True) for m in masks]
    inner = functools.reduce(jnp.add, [s * d for s, d in zip(shares, d_shares)])
    d_single = jnp.sum(
        functools.reduce(jnp.add, [m * (s * (d - inner)) for m, s, d in zip(masks, shares, d_shares)]), axis=1, keepdims=True
    )
    own_col = lax.broadcasted_iota(jnp.int32, (frame, 1), 0)
    place_col = own_col + first
    live_col = ((place_col >= 0) & (place_col < limit)).astype(F32)
    own = ((own_col >= EDGE) & (own_col < frame - EDGE)).astype(F32)
    dconv_ref[...] = (d_conv + d_single * vectors[base + 4 : base + 5]) * live_col
    grad_score = jnp.sum(conv * (d_single * own), axis=0, keepdims=True)
    masked = mask_ref[0].astype(F32)
    d_masked = jnp.zeros(masked.shape, F32)
    for j in range(4):
        moved = dconv_ref[EDGE + 2 - j : EDGE + 2 - j + extent, :]
        d_masked += vectors[base + j : base + j + 1] * moved
        sum_ref[vocab + j : vocab + j + 1, :] += jnp.sum(masked * moved, axis=0, keepdims=True)
    sum_ref[vocab + 4 : vocab + 5, :] += grad_score
    d_in = (d_masked * live_col[EDGE : frame - EDGE]).astype(BF16)
    din_ref[0] = d_in
    ids = ids_ref[0][:, EDGE : frame - EDGE]
    emb_rows = -(-vocab // 8) * 8
    onehot = (lax.broadcasted_iota(jnp.int32, (emb_rows, extent), 0) == ids).astype(F32).astype(BF16)
    sum_ref[0:emb_rows, :] += dot_nn(onehot, d_in)

    sum_ref[vocab + 5 : vocab + 6, :] += gain_one_ref[...]
    sum_ref[vocab + 6 : vocab + 7, :] += gain_two_ref[...]
    if last_row:
        parts, _, share = grad_ref.shape
        for d in range(parts):
            grad_ref[d] = sum_ref[:, d * share : (d + 1) * share].astype(BF16)
            grad_ref[d, vocab + 7 : vocab + 7 + rel_ref.shape[0], :] = rel_ref[...].astype(BF16)
    else:
        grad_ref[...] = sum_ref[...]


def front_backward(at, row_len, ids, pack, d_hid, rims, conv, masked, shares, gains, rel, vocab, row, rows, before):
    frame = ids.shape[2]
    extent = frame - 2 * EDGE
    d_model = d_hid.shape[1]
    pad = pack.shape[1]
    args = [ids, pack, d_hid, *rims, conv, masked, shares, *gains] + ([rel] if row == rows - 1 else [])
    specs = [scalars(), scalars(), *in_vmem(args)]
    aliases = {}
    if before:
        specs += [whole(before[0]), pl.BlockSpec(memory_space=pl.ANY)]
        aliases = {len(specs) - 1: 0}
    grads = jax.ShapeDtypeStruct(pack.shape, BF16) if row == rows - 1 else jax.ShapeDtypeStruct((pad, d_model), F32)
    return pl.pallas_call(
        functools.partial(front_back_kernel, vocab, row == 0, row == rows - 1),
        grid=(1,),
        in_specs=specs,
        out_specs=[pl.BlockSpec((1, extent, d_model), lambda *_: (row, 0, 0)), whole(grads)],
        out_shape=[jax.ShapeDtypeStruct((rows, extent, d_model), BF16), grads],
        scratch_shapes=[
            pltpu.VMEM((pad, d_model), BF16),
            pltpu.VMEM((frame, frame), BF16),
            pltpu.VMEM((frame, frame), BF16),
            pltpu.VMEM((frame, frame), BF16),
            pltpu.VMEM((frame, d_model), F32),
            pltpu.VMEM((pad, d_model), F32),
        ],
        input_output_aliases=aliases,
        compiler_params=pltpu.CompilerParams(vmem_limit_bytes=56 << 20),
        cost_estimate=pl.CostEstimate(flops=16 * frame * frame * d_model, bytes_accessed=frame * d_model * 12, transcendentals=0),
        name="front_back",
    )(at, row_len, *args, *before)


def settle_kernel(vocab, x_ref, got_ref, emb_ref, conv_ref, vec_ref, rel_ref):
    total = x_ref[...] + got_ref[...].astype(F32)
    emb_ref[...] = total[:vocab]
    conv_ref[...] = total[vocab : vocab + 4]
    vec_ref[...] = total[vocab + 4 : vocab + 7]
    rel_ref[...] = total[vocab + 7 : vocab + 7 + rel_ref.shape[0]]


def settle(x, got, vocab, rel_rows):
    share = x.shape[1]
    outs = [jax.ShapeDtypeStruct((rows, share), F32) for rows in (vocab, 4, 3, rel_rows)]
    return pl.pallas_call(
        functools.partial(settle_kernel, vocab),
        grid=(1,),
        in_specs=in_vmem([x, got]),
        out_specs=in_vmem(outs),
        out_shape=outs,
        name="settle",
    )(x, got)


GELU_C = 0.7978845608
GELU_A = 0.044715


def pack_down(x):
    rows, third = x.shape[1], x.shape[2] // 3
    left, mid, right = x[..., :third], x[..., third : 2 * third], x[..., 2 * third :]
    return jnp.concatenate(
        [jnp.concatenate([left, right[:, : rows // 2]], axis=1), jnp.concatenate([mid, right[:, rows // 2 :]], axis=1)], axis=2
    )


def unpack_down(x):
    rows, third = x.shape[1] * 2 // 3, x.shape[2] // 2
    right = jnp.concatenate([x[:, rows:, :third], x[:, rows:, third:]], axis=1)
    return jnp.concatenate([x[:, :rows, :third], x[:, :rows, third:], right], axis=2)


def feed_kernel(nblk, rows, row, sizes, *refs):
    share, ff_cols, width, down_rows = sizes
    x_refs, cot_refs, rest_ref = refs[:nblk], refs[nblk : 2 * nblk], refs[2 * nblk]
    refs = refs[2 * nblk + 1 :]
    sums_in, outs_in = None, ()
    if row > 0:
        outs_in, sums_in, refs = refs[:nblk], refs[nblk : nblk + 2], refs[nblk + 2 :]
    outs, dnorms, grads = refs[:nblk], refs[nblk : 2 * nblk], refs[2 * nblk :]
    if row == rows - 1:
        pack_ref, sum_a, sum_b = grads
    else:
        sum_a, sum_b = grads
    parts = rest_ref.shape[0]
    w_in = rest_ref[:, :share, : 2 * ff_cols].reshape(parts * share, 2 * ff_cols)
    w_down = unpack_down(rest_ref[:, :, 2 * ff_cols :]).reshape(parts * down_rows, width)
    for b in range(nblk):
        x, cot = x_refs[b][...], cot_refs[b][row]
        both = dot_nn(x, w_in)
        gate, up = both[:, :ff_cols], both[:, ff_cols:]
        square = gate * gate
        turned = jnp.tanh(GELU_C * gate * (1.0 + GELU_A * square))
        half = 0.5 * (1.0 + turned)
        gelu = gate * half
        slope = half + (0.5 * GELU_C) * gate * (1.0 - turned * turned) * (1.0 + (3.0 * GELU_A) * square)
        hidden = (gelu * up).astype(BF16)
        if row > 0:
            outs[b][:row] = outs_in[b][...]
        outs[b][row] = dot_nn(hidden, w_down).astype(BF16)
        d_hidden = dot_nt(cot, w_down)
        d_both = jnp.concatenate([(d_hidden * up * slope).astype(BF16), (d_hidden * gelu).astype(BF16)], axis=1)
        dnorms[b][...] = dot_nt(d_both, w_in).astype(BF16)
        grad_a, grad_b = dot_tn(x, d_both), dot_tn(hidden, cot)
        if b == 0 and sums_in is None:
            sum_a[...] = grad_a
            sum_b[...] = grad_b
        elif b == 0:
            sum_a[...] = sums_in[0][...] + grad_a
            sum_b[...] = sums_in[1][...] + grad_b
        else:
            sum_a[...] += grad_a
            sum_b[...] += grad_b
    if row == rows - 1:
        pack_ref[:, :, : 2 * ff_cols] = sum_a[...].astype(BF16).reshape(parts, share, 2 * ff_cols)
        pack_ref[:, :, 2 * ff_cols :] = pack_down(sum_b[...].astype(BF16).reshape(parts, down_rows, width))


def feed(xs, cots, rest, before, row, sizes):
    nblk = len(xs)
    tok, d_model = xs[0].shape
    share, ff_cols, width, down_rows = sizes
    parts, rows = rest.shape[0], cots[0].shape[0]
    sum_shapes = [(d_model, 2 * ff_cols), (parts * down_rows, width)]
    outs = [jax.ShapeDtypeStruct((row + 1, tok, width), BF16)] * nblk + [jax.ShapeDtypeStruct((tok, d_model), BF16)] * nblk
    scratch = []
    if row == rows - 1:
        outs.append(jax.ShapeDtypeStruct(rest.shape, BF16))
        scratch = [pltpu.VMEM(s, F32) for s in sum_shapes]
    else:
        outs += [jax.ShapeDtypeStruct(s, F32) for s in sum_shapes]
    args = [*xs, *cots, rest, *before]
    flops = 2 * nblk * tok * d_model * ff_cols * 9
    got = pl.pallas_call(
        functools.partial(feed_kernel, nblk, rows, row, sizes),
        grid=(1,),
        in_specs=in_vmem(args),
        out_specs=in_vmem(outs),
        out_shape=outs,
        scratch_shapes=scratch,
        compiler_params=pltpu.CompilerParams(vmem_limit_bytes=56 << 20),
        cost_estimate=pl.CostEstimate(flops=flops, bytes_accessed=12 << 20, transcendentals=nblk * tok * ff_cols),
        name="feed",
    )(*args)
    return got[:nblk], got[nblk : 2 * nblk], got[2 * nblk :]


P = jax.sharding.PartitionSpec


def rims_of(x, width):
    size, length = lax.axis_size("seq"), x.shape[1]
    up = [(i, i + 1) for i in range(size - 1)]
    down = [(j, i) for i, j in up]
    before = lax.ppermute(x[:, length - width :], "seq", up)
    after = lax.ppermute(x[:, :width], "seq", down)
    return before, after


def flip_with(x, axis, bit):
    return lax.ppermute(x, axis, [(i, i ^ bit) for i in range(lax.axis_size(axis))])


def bits_of(axis):
    bits, bit = [], 1
    while bit < lax.axis_size(axis):
        bits.append(bit)
        bit *= 2
    return bits[::-1]


def after(x, *others):
    return lax.optimization_barrier((x,) + others)[0]


def places_of(n):
    places = [0]
    bit = n // 2
    while bit:
        places = places + [p ^ bit for p in places]
        bit //= 2
    return places


def swap_blocks(parts):
    return [part if bit == 0 else flip_with(part, "seq", bit) for part, bit in zip(parts, places_of(len(parts)))]


def gather_direct(x):
    return swap_blocks([x] * lax.axis_size("seq"))


def gather_first(x):
    blocks = [x]
    for bit in bits_of("seq")[:-1]:
        blocks = blocks + [flip_with(block, "seq", bit) for block in blocks]
    return blocks


def gather_last(blocks):
    return blocks + [flip_with(block, "seq", 1) for block in blocks]


def gather_two(x):
    return gather_last(gather_first(x))


def scatter_first(parts):
    half = len(parts) // 2
    got = [flip_with(part, "seq", 1) for part in parts[half:]]
    send = [(a.astype(F32) + b.astype(F32)).astype(BF16) for a, b in zip(parts[1:half], got[1:])]
    return [parts[0], got[0]], send


def scatter_last(own, send):
    return own + [flip_with(part, "seq", place) for part, place in zip(send, places_of(2 * len(send) + 2)[1:])]


def add_up(parts):
    return functools.reduce(jnp.add, [part.astype(F32) for part in parts])


def scatter_step(x, bit):
    axis = bits_of("dp").index(bit)
    low, high = lax.index_in_dim(x, 0, axis), lax.index_in_dim(x, 1, axis)
    upper = (lax.axis_index("dp") & bit) != 0
    keep, send = jnp.where(upper, high, low), jnp.where(upper, low, high)
    return keep, flip_with(send.astype(BF16), "dp", bit)


def swap_dp(x):
    return lax.all_to_all(x, "dp", split_axis=0, concat_axis=0, tiled=True)


def sum_parts(x):
    return jnp.sum(x.astype(F32), axis=0)


def gather_step(x, bit, *gate):
    axis = bits_of("dp").index(bit)
    other = flip_with(x, "dp", bit)
    other = after(other, *gate) if gate else other
    upper = (lax.axis_index("dp") & bit) != 0
    return jnp.concatenate([jnp.where(upper, other, x), jnp.where(upper, x, other)], axis=axis)


def gather_start(x):
    return x.reshape((1,) * len(bits_of("dp")) + x.shape)


def sum_step(x, bit):
    low = x.astype(BF16)
    return low.astype(F32) + flip_with(low, "seq", bit).astype(F32)


def sum_seq(x):
    for bit in bits_of("seq")[::-1]:
        x = sum_step(x, bit)
    return x


def in_order(blocks, me):
    n = len(blocks)
    bits = bits_of("seq")
    x = jnp.stack(blocks).reshape((2,) * len(bits) + blocks[0].shape)
    for at, bit in enumerate(bits[::-1]):
        upper = (me & bit) != 0
        x = jnp.where(upper, jnp.flip(x, at), x)
    x = x.transpose(tuple(range(len(bits)))[::-1] + tuple(range(len(bits), x.ndim)))
    return x.reshape((n,) + blocks[0].shape)


def on_device(
    byte_ids,
    lengths,
    deal_order,
    buckets,
    embedding,
    conv_w,
    score_w,
    gain_one,
    w_query,
    w_key,
    w_value,
    w_out,
    rel_bias,
    gain_two,
    w_gate,
    w_up,
    w_down,
    cotangent,
):
    n = lax.axis_size("seq")
    dp = lax.axis_size("dp")
    me = lax.axis_index("seq")
    rows_dev, extent = byte_ids.shape
    share, width = w_query.shape
    d_model = share * dp
    head_cols = width // n
    heads_dev = head_cols // DH
    ff_cols = w_gate.shape[1] // n
    down_rows = w_down.shape[0] // n
    tok = cotangent.shape[1]
    place = jnp.array(places_of(n), jnp.int32) ^ me

    vocab = embedding.shape[0]
    rel_rows = -(-rel_bias.size // share)
    pad_vocab = -(-(vocab + 7 + rel_rows) // 16) * 16
    front_pack = jnp.concatenate(
        [embedding, conv_w, score_w[None], gain_one[None], gain_two[None], jnp.zeros((pad_vocab - vocab - 7, share), BF16)], axis=0
    )

    def own_cols(weight):
        return lax.dynamic_slice_in_dim(weight, me * head_cols, head_cols, 1)

    qkv_pack = jnp.concatenate([own_cols(w_query), own_cols(w_key), own_cols(w_value), own_cols(w_out)], axis=1)
    front_all, qkv_w = gather_start(front_pack), gather_start(qkv_pack)
    up_bits = bits_of("dp")
    qkv_bits = up_bits[-1:] + up_bits[:-1]
    for at, bit in enumerate(up_bits):
        front_all = gather_step(front_all, bit)
        if at == 0:
            byte_ids, rel_in = (after(x, front_all) for x in (byte_ids, rel_bias))
        if at < len(up_bits) - 1:
            qkv_w = after(gather_step(qkv_w, qkv_bits[at]), front_all)
    front_all = front_all.reshape((dp,) + front_pack.shape)
    gain_first = front_all[:, vocab + 5].reshape(1, d_model).astype(F32)
    gain_second = front_all[:, vocab + 6].reshape(1, d_model).astype(F32)

    def own_ff(weight):
        return lax.dynamic_index_in_dim(weight.reshape(share, dp, n, down_rows), me, 2, keepdims=False).reshape(
            share, ff_cols
        )

    down_own = lax.dynamic_slice_in_dim(w_down, me * down_rows, down_rows, 0)
    rest_pack = jnp.concatenate([own_ff(w_gate), own_ff(w_up), pack_down(down_own[None])[0]], axis=1)
    offset = me * extent
    matches = deal_order[:, None] == jnp.arange(lengths.shape[0], dtype=jnp.int32)[None, :]
    row_len = jnp.sum(jnp.where(matches, lengths[None, :], 0), axis=1)
    rim_low, rim_high = rims_of(byte_ids, EDGE)
    ids = jnp.concatenate([rim_low, byte_ids, rim_high], axis=1)[:, None, :]
    at = jnp.full((1,), offset, jnp.int32)
    row_ids = range(rows_dev)
    lens = [row_len[r : r + 1] for r in row_ids]

    first_head = me * heads_dev
    bias_loc = lax.dynamic_slice_in_dim(rel_in, first_head, heads_dev, 1)
    offsets = jnp.concatenate([jnp.full((1,), -1, jnp.int32), buckets[::-1]])
    onehot = (offsets[None, :] == jnp.arange(rel_bias.shape[0], dtype=jnp.int32)[:, None]).astype(BF16)
    strips = bias_strips(jnp.einsum("nh,nx->hx", bias_loc, onehot, preferred_element_type=F32), n)

    cots = gather_two(cotangent)
    normed, h_zero, kept = [], [], []
    gate = (strips,)
    for r in row_ids:
        h, low, *rest = front_forward(at, lens[r], after(ids[r : r + 1], *gate), front_all, vocab, d_model)
        if r == 0:
            qkv_w = after(qkv_w, low)
        gate = (low,)
        h_zero.append(h[0])
        normed.append(low[0])
        kept.append(rest)
    low_one = [gather_two(low) if r == 0 else gather_direct(low) for r, low in enumerate(normed)]
    qkv_w = gather_step(qkv_w, qkv_bits[-1], *gate, low_one[0][1])
    qkv_w = qkv_w.reshape(d_model, 4 * head_cols)
    rest_all = lax.all_gather(after(rest_pack, qkv_w), "dp", axis=0, tiled=False)
    out_blocks = gather_first(qkv_w[:, 3 * head_cols :])
    gate = gate + tuple(cots)
    atts, qkvs, logs, mixed = [], [], [], []
    for r in row_ids:
        xs = [after(low_one[r][0], *gate)] + list(low_one[r][1:])
        att, qkv, log = attend(place, lens[r], xs, qkv_w, strips)
        gate = (qkv,)
        atts.append(att)
        qkvs.append(qkv)
        logs.append(log)
        mixed.append(swap_blocks([after(a, *mixed[r - 1]) for a in att] if r else att))
        if r == rows_dev - 1:
            out_blocks = gather_last([after(block, *gate, *mixed[0]) for block in out_blocks])
    w_out_all, h_one, lows = project(place, out_blocks, [[after(m[0], *gate)] + m[1:] for m in mixed], h_zero, gain_second)
    low_two = [gather_two(low) if r == 0 else gather_direct(low) for r, low in enumerate(lows)]
    sizes = (share, ff_cols, width, down_rows)
    d_norm_two, before = [], ()
    for r in row_ids:
        xs = [after(low_two[r][0], *gate)] + low_two[r][1:]
        ff_outs, d_norm, sums = feed(xs, cots, rest_all, before, r, sizes)
        before = (*ff_outs, *sums)
        gate = (d_norm[0],)
        if r:
            d_norm = [after(part, *d_norm_two[r - 1]) for part in d_norm]
        if r < rows_dev - 1:
            d_norm_two.append(swap_blocks(d_norm))
        else:
            two_own, two_send = scatter_first(d_norm)
            d_norm_two.append(scatter_last(two_own, two_send))
    ff_sum = lax.psum_scatter(sums[0], "dp", scatter_dimension=0, tiled=False)
    d_h_one, gains_two, earlier, d_norms, qkv_grad, d_revs = [], [], [], [], None, []
    for r in row_ids:
        last = r == rows_dev - 1
        adds = [after(d_norm_two[r][0], *gate)] + d_norm_two[r][1:]
        d_h, gain_grad, d_att, out_grad = project_back(
            place, adds, mixed[r], w_out_all, h_one[r], cotangent, r, gain_second, earlier, dp if last else 0
        )
        gate = (d_h,)
        earlier = earlier + [*mixed[r], out_grad]
        d_h_one.append(d_h)
        gains_two.append(gain_grad)
        douts = swap_blocks(d_att)
        if r == 0:
            ff_own, ff_send = scatter_first([after(ff_out, *gate) for ff_out in ff_outs])
            ff_whole = scatter_last(ff_own, ff_send)
            gate = gate + tuple(two_send) + tuple(ff_send)
        elif r == 1:
            gate = gate + tuple(ff_whole)
        d_norm, qkv_grad, d_rev = attend_back(
            place, lens[r], low_one[r], qkv_w, qkvs[r], atts[r], [after(douts[0], *gate)] + douts[1:], logs[r], strips,
            qkv_grad, dp if last else 0,
        )
        gate = (d_norm[0],)
        d_norms.append(d_norm)
        d_revs.append(d_rev)
    out_parts = swap_dp(out_grad)
    dp_bits = bits_of("dp")[::-1]
    qkv_sum = [qkv_grad.reshape((2,) * len(dp_bits) + qkv_grad.shape[1:])]
    d_rel_loc = jnp.einsum("nx,hx->nh", onehot.astype(F32), sum(d_revs), precision=lax.Precision.HIGHEST)
    d_rel = lax.dynamic_update_slice_in_dim(jnp.zeros(rel_bias.shape, F32), d_rel_loc, first_head, 1)
    d_rel = jnp.pad(d_rel.reshape(-1), (0, rel_rows * share - rel_bias.size)).reshape(rel_rows, share)

    d_first = [swap_blocks(d_norm) for d_norm in d_norms[:-1]]
    last_own, last_send = scatter_first([after(part, *d_first[-1]) for part in d_norms[-1]])
    d_first.append(scatter_last(last_own, last_send))
    seq_bits = bits_of("seq")[::-1]
    g_out = sum_parts(after(out_parts, *gate))
    front_grad = ()
    for r in row_ids:
        adds = [after(d_first[r][0], *gate)] + d_first[r][1:]
        d_h_zero, low_rim, high_rim, gain_grad = first_back(adds, h_zero[r], d_h_one[r], gain_first)
        size = lax.axis_size("seq")
        low_side = lax.ppermute(high_rim, "seq", [(i, i + 1) for i in range(size - 1)])
        high_side = lax.ppermute(low_rim, "seq", [(i + 1, i) for i in range(size - 1)])
        if dp_bits:
            qkv_sum = scatter_step(add_up([after(part, *gate) for part in qkv_sum]), dp_bits.pop(0))
        extra = (*last_send, g_out, ff_sum) if r == 0 else (g_out,)
        conv_out, masked, shares = kept[r]
        d_input, front_sum = front_backward(
            at, lens[r], ids[r : r + 1], front_all, after(d_h_zero, *extra), (low_side, high_side), conv_out, masked, shares,
            (gain_grad, gains_two[r]), d_rel, vocab, r, rows_dev, front_grad,
        )
        front_grad = (front_sum, d_input)
        gate = (front_sum,)
        if r == 0:
            ff_all = gather_first(ff_sum)
            ff_all = [ff_all[0]] + [after(block, *gate) for block in ff_all[1:]]
            gate = gate + tuple(ff_all[1:])
            ff_all = gather_last(ff_all)
            g_out = sum_step(after(g_out, *gate), seq_bits.pop(0))
    ff_all = [after(block, *gate) for block in ff_all]
    front_parts = swap_dp(front_sum)
    qkv_sum = add_up([after(part, *gate) for part in qkv_sum])
    while dp_bits:
        qkv_sum = add_up(scatter_step(qkv_sum, dp_bits.pop(0)))
    g_out = after(g_out, *gate)
    while seq_bits:
        g_out = sum_step(g_out, seq_bits.pop(0))
    tail = (g_out,)
    output = (jnp.stack([after(h, *tail) for h in h_one]) + add_up(ff_whole)).astype(BF16)
    ff_all = in_order([after(block, *tail) for block in ff_all], me)
    g_gu = ff_all[:, :, : 2 * ff_cols].reshape(n, share, 2, dp, down_rows)
    g_gu = g_gu.transpose(2, 1, 3, 0, 4).reshape(2, share, n * ff_cols).astype(F32)
    g_down = unpack_down(ff_all[:, :, 2 * ff_cols :]).reshape(n * down_rows, width).astype(F32)
    g_qkv = in_order(gather_two(qkv_sum.astype(BF16).reshape(share, 3, head_cols)), me)
    g_qkv = g_qkv.transpose(2, 1, 0, 3).reshape(3, share, width).astype(F32)
    front_sum = sum_parts(front_parts)
    front_bits = bits_of("seq")[::-1]
    for bit in front_bits[:-1]:
        front_sum = sum_step(front_sum, bit)
    front_low = front_sum.astype(BF16)
    g_emb, g_conv, g_vec, g_rel = settle(front_low.astype(F32), flip_with(front_low, "seq", front_bits[-1]), vocab, rel_rows)
    return (
        output,
        d_input,
        g_emb,
        g_conv,
        g_vec[0],
        g_vec[1],
        g_qkv[0],
        g_qkv[1],
        g_qkv[2],
        g_out,
        g_rel.reshape(-1)[: rel_bias.size].reshape(rel_bias.shape),
        g_vec[2],
        g_gu[0],
        g_gu[1],
        g_down,
    )


def solution(mesh):
    return jax.shard_map(
        on_device,
        mesh=mesh,
        in_specs=(
            P("dp", "seq"),
            P(),
            P("dp"),
            P(),
            P(None, "dp"),
            P(None, "dp"),
            P("dp"),
            P("dp"),
            P("dp", None),
            P("dp", None),
            P("dp", None),
            P("dp", None),
            P(),
            P("dp"),
            P("dp", None),
            P("dp", None),
            P("dp", None),
            P("dp", "seq", None),
        ),
        out_specs=(
            P("dp", "seq", None),
            P("dp", "seq", None),
            P(None, "dp"),
            P(None, "dp"),
            P("dp"),
            P("dp"),
            P("dp", None),
            P("dp", None),
            P("dp", None),
            P("dp", None),
            P(),
            P("dp"),
            P("dp", None),
            P("dp", None),
            P("dp", None),
        ),
        check_vma=False,
    )
```
